32 devices in a mesh: batch: 16 (over z, y, x), mp: 2 (over core).
Axes of the slice: x: 2, y: 2, z: 4, core: 2. Of those that a mesh axis runs over, the one named last changes fastest.
Arguments:
- features: bfloat16 [131072, 512], P('batch'), may hold values from -67 to 67, as said below
- validity: int32 [131072], P('batch'), may hold values from 0 to 1, as said below
- labels: int32 [131072, 2], P('batch'), may hold values from 0 to 1
- expert_in: float32 [6, 512, 256], P(None, None, 'mp'), may hold values from -0.25 to 0.25
- expert_in_bias: float32 [6, 256], P(None, 'mp'), may hold values from -2 to 2
- norm_gain: float32 [6, 256], P(None, 'mp'), may hold values from 0.25 to 1.75
- norm_bias: float32 [6, 256], P(None, 'mp'), may hold values from -2 to 2
- expert_out: float32 [6, 256, 256], P(None, 'mp'), may hold values from -0.375 to 0.375
- expert_out_bias: float32 [6, 256], replicated, may hold values from -2 to 2
- gate_weight: float32 [2, 512, 4], replicated, may hold values from -0.25 to 0.25
- gate_bias: float32 [2, 4], replicated, may hold values from -0.1 to 0.1
- tower_first: float32 [2, 256, 128], replicated, may hold values from -0.375 to 0.375
- tower_first_bias: float32 [2, 128], replicated, may hold values from -2 to 2
- tower_second: float32 [2, 128, 64], replicated, may hold values from -0.5 to 0.5
- tower_second_bias: float32 [2, 64], replicated, may hold values from -2 to 2
- tower_last: float32 [2, 64], replicated, may hold values from -0.75 to 0.75
- tower_last_bias: float32 [2], replicated, may hold values from -2 to 2
Outputs:
- predictions: float32 [131072, 2], P('batch')
- features_grad: float32 [131072, 512], P('batch', 'mp')
- grad_expert_in: float32 [6, 512, 256], P(None, None, 'mp')
- grad_expert_in_bias: float32 [6, 256], P(None, 'mp')
- grad_norm_gain: float32 [6, 256], P(None, 'mp')
- grad_norm_bias: float32 [6, 256], P(None, 'mp')
- grad_expert_out: float32 [6, 256, 256], P(None, 'mp')
- grad_expert_out_bias: float32 [6, 256], replicated
- grad_gate_weight: float32 [2, 512, 4], replicated
- grad_gate_bias: float32 [2, 4], replicated
- grad_tower_first: float32 [2, 256, 128], replicated
- grad_tower_first_bias: float32 [2, 128], replicated
- grad_tower_second: float32 [2, 128, 64], replicated
- grad_tower_second_bias: float32 [2, 64], replicated
- grad_tower_last: float32 [2, 64], replicated
- grad_tower_last_bias: float32 [2], replicated
The draws below stay inside these ranges and needn't reach their ends.
Inputs may be any that keep to these rules, and one draw needn't show every extreme that they name: The features have a per-feature offset and scale. `validity`: each index of batch holds between 2048 and 8192 valid events; low indices tend to hold fewer than high ones, but neighbouring indices may be in either order.
All inputs are finite; a program needn't handle non-finite values.
Results may differ from the reference program's by a relative error of at most 0.0075.
Values may be sent and summed in bfloat16 or wider, within the bound.
A program may use at most 320 MiB of HBM per device.

```python
import math
import jax
import jax.numpy as jnp
from jax import lax

D = 512
HID = 256
TW1 = 128
TW2 = 64
EXPERTS = 6
TASKS = 2
ROWS = 8192
EVENTS = 131072


def draw_features(key, part):
    key = jax.random.fold_in(key, 7)
    first, second, third = jax.random.split(key, 3)
    offset = jax.random.uniform(first, (D,), jnp.float32, -2.0, 2.0)
    scales = jnp.exp(jax.random.uniform(second, (D,), jnp.float32, 0.0, math.log(8.0)))
    noise = jnp.clip(jax.random.normal(third, (EVENTS, D), jnp.float32), -4.0, 4.0)
    return (offset + scales * noise).astype(jnp.bfloat16)


def draw_validity(key, part):
    key = jax.random.fold_in(key, 11)
    first, second = jax.random.split(key)
    blocks = EVENTS // ROWS
    row_ids = jnp.arange(EVENTS, dtype=jnp.int32)
    block_ids = row_ids // ROWS
    level = ROWS // 3 + 2 * ROWS // 3 * block_ids // max(blocks - 1, 1)
    jitter = jax.random.randint(first, (blocks,), 0, ROWS // 8 + 1)
    level = jnp.clip(level + jitter[block_ids] - ROWS // 16, ROWS // 4 + 1, ROWS)
    ticket = jax.random.randint(second, (EVENTS,), 0, ROWS)
    return (ticket < level).astype(jnp.int32)


def touch_ends(values, stream_key, smallest, largest):
    shape = values.shape
    spot = [jax.random.randint(jax.random.fold_in(stream_key, axis), (), 0, shape[axis]) for axis in range(len(shape))]
    values = values.at[tuple(spot)].set(smallest)
    longest = shape.index(max(shape))
    spot[longest] = (spot[longest] + 1) % shape[longest]
    return values.at[tuple(spot)].set(largest)


def block_scale(own_key, shape, cuts, low, largest):
    level = 1.0
    for position, blocks in cuts:
        steps = jax.random.uniform(jax.random.fold_in(jax.random.fold_in(own_key, 6), position), (blocks,), jnp.float32, low / len(cuts), largest / len(cuts))
        level = level * jnp.repeat(jnp.exp(steps), shape[position] // blocks).reshape((-1,) + (1,) * (len(shape) - 1 - position))
    return level


def normal_values(own_key, shape, deviation, reach, shards=(), held_as=jnp.bfloat16):
    values = deviation * jax.random.normal(own_key, shape, jnp.float32)
    if shards:
        values = values * block_scale(own_key, shape, shards, -0.22, 0.18)
    return jnp.clip(values, -reach, reach).astype(held_as)


def setup_inputs(seed: int = 0) -> dict:
    arg_keys = jax.random.split(jax.random.key(seed), 18)
    return {
        "features": draw_features(jax.random.fold_in(arg_keys[17], 71), 0),
        "validity": draw_validity(jax.random.fold_in(arg_keys[17], 71), 0),
        "labels": touch_ends(jax.random.randint(arg_keys[2], (EVENTS, TASKS), 0, 2), jax.random.fold_in(arg_keys[2], 1), 0, 1).astype(jnp.int32),
        "expert_in": normal_values(arg_keys[3], (EXPERTS, D, HID), D ** -0.5, 0.25, ((2, 2),), jnp.float32),
        "expert_in_bias": normal_values(arg_keys[4], (EXPERTS, HID), 0.3, 2.0, ((1, 2),), jnp.float32),
        "norm_gain": jnp.clip(1.0 + 0.15 * jax.random.normal(arg_keys[5], (EXPERTS, HID), jnp.float32), 0.25, 1.75),
        "norm_bias": normal_values(arg_keys[6], (EXPERTS, HID), 0.3, 2.0, ((1, 2),), jnp.float32),
        "expert_out": normal_values(arg_keys[7], (EXPERTS, HID, HID), HID ** -0.5, 0.375, ((1, 2),), jnp.float32),
        "expert_out_bias": normal_values(arg_keys[8], (EXPERTS, HID), 0.3, 2.0, (), jnp.float32),
        "gate_weight": normal_values(arg_keys[9], (TASKS, D, 4), D ** -0.5, 0.25, (), jnp.float32),
        "gate_bias": jnp.clip(jax.random.uniform(arg_keys[10], (TASKS, 4), jnp.float32, -0.1, 0.1), -0.1, 0.1),
        "tower_first": normal_values(arg_keys[11], (TASKS, HID, TW1), HID ** -0.5, 0.375, (), jnp.float32),
        "tower_first_bias": normal_values(arg_keys[12], (TASKS, TW1), 0.3, 2.0, (), jnp.float32),
        "tower_second": normal_values(arg_keys[13], (TASKS, TW1, TW2), TW1 ** -0.5, 0.5, (), jnp.float32),
        "tower_second_bias": normal_values(arg_keys[14], (TASKS, TW2), 0.3, 2.0, (), jnp.float32),
        "tower_last": normal_values(arg_keys[15], (TASKS, TW2), TW2 ** -0.5, 0.75, (), jnp.float32),
        "tower_last_bias": normal_values(arg_keys[16], (TASKS,), 0.5, 2.0, (), jnp.float32),
    }


@jax.custom_vjp
def low(v):
    return lax.optimization_barrier(v.astype(jnp.bfloat16)).astype(jnp.float32)

@jax.custom_vjp
def low_back(v):
    return v

def low_keep(v):
    return (low(v), None)

def low_pass(kept, grad):
    return (grad,)

def back_keep(v):
    return (v, None)

def back_low(kept, grad):
    return (low(grad),)
low.defvjp(low_keep, low_pass)
low_back.defvjp(back_keep, back_low)
EPS = 1e-05
HIGHEST = lax.Precision.HIGHEST
TASK_EXPERTS = ((0, 1, 4, 5), (2, 3, 4, 5))

def silu(value):
    return value * jax.nn.sigmoid(value)

def block_loss(params, normed_rows, weight_matrix, label_f):
    expert_in, expert_in_bias, norm_gain, norm_bias, expert_out, expert_out_bias, gate_weight, gate_bias, tower_first, tower_first_bias, tower_second, tower_second_bias, tower_last, tower_last_bias = params
    pre_act = jnp.einsum('rd,edh->erh', normed_rows, expert_in, precision=HIGHEST) + expert_in_bias[:, None, :]
    pre_act = low_back(pre_act)
    centre = pre_act - lax.optimization_barrier(jnp.mean(pre_act, axis=-1, keepdims=True))
    spread = lax.optimization_barrier(jnp.mean(centre * centre, axis=-1, keepdims=True))
    zhat = centre * lax.rsqrt(spread + EPS)
    hidden = low(silu(zhat * norm_gain[:, None, :] + norm_bias[:, None, :]))
    outputs = jnp.einsum('erh,eho->ero', hidden, expert_out, precision=HIGHEST) + expert_out_bias[:, None, :]
    outputs = low_back(low(outputs))
    logits = jnp.einsum('rd,tdk->trk', normed_rows, gate_weight, precision=HIGHEST) + gate_bias[:, None, :]
    gate_prob = jax.nn.softmax(logits, axis=-1)
    loss_total = jnp.zeros((), jnp.float32)
    columns = []
    for task_id in range(TASKS):
        mixed = jnp.zeros_like(outputs[0])
        for slot_id in range(4):
            mixed = mixed + gate_prob[task_id, :, slot_id, None] * outputs[TASK_EXPERTS[task_id][slot_id]]
        first = silu(jnp.dot(mixed, tower_first[task_id], precision=HIGHEST) + tower_first_bias[task_id])
        second = silu(jnp.dot(first, tower_second[task_id], precision=HIGHEST) + tower_second_bias[task_id])
        logit = jnp.dot(second, tower_last[task_id], precision=HIGHEST) + tower_last_bias[task_id]
        target = label_f[:, task_id]
        loss_total = loss_total + jnp.sum(weight_matrix * (jax.nn.softplus(logit) - target * logit))
        columns.append(jax.nn.sigmoid(logit))
    return (loss_total, jnp.stack(columns, axis=1))

def forward(features_f, params, weight_matrix, label_f):
    count = jnp.sum(weight_matrix)
    mean_x = lax.optimization_barrier(jnp.sum(weight_matrix[:, None] * features_f, axis=0)) / count
    mean_removed = features_f - mean_x
    variance = lax.optimization_barrier(jnp.sum(weight_matrix[:, None] * mean_removed * mean_removed, axis=0)) / count
    normed_rows = low(mean_removed * lax.rsqrt(variance + EPS))
    rounded = tuple((low(item) if place in (0, 4, 6) else item for place, item in enumerate(params)))
    blocks = EVENTS // ROWS

    def one_block(items):
        return block_loss(rounded, items[0], items[1], items[2])
    losses, preds = lax.map(jax.checkpoint(one_block), (normed_rows.reshape(blocks, ROWS, D), weight_matrix.reshape(blocks, ROWS), label_f.reshape(blocks, ROWS, TASKS)))
    return (jnp.sum(losses), preds.reshape(EVENTS, TASKS))

def reference(features, validity, labels, expert_in, expert_in_bias, norm_gain, norm_bias, expert_out, expert_out_bias, gate_weight, gate_bias, tower_first, tower_first_bias, tower_second, tower_second_bias, tower_last, tower_last_bias):
    features_f = features.astype(jnp.float32)
    weight_matrix = validity.astype(jnp.float32)
    label_f = labels.astype(jnp.float32)
    params = (expert_in, expert_in_bias, norm_gain, norm_bias, expert_out, expert_out_bias, gate_weight, gate_bias, tower_first, tower_first_bias, tower_second, tower_second_bias, tower_last, tower_last_bias)

    def loss_only(feat_in, param_in):
        return forward(feat_in, param_in, weight_matrix, label_f)
    loss_value, back_fn, preds = jax.vjp(loss_only, features_f, params, has_aux=True)
    feat_grad, param_grad = back_fn(jnp.ones((), loss_value.dtype))
    count = jnp.sum(weight_matrix)
    scaled = tuple((item / count for item in param_grad))
    return (preds, feat_grad) + scaled
```

```python
import functools

import jax
import jax.numpy as jnp
from jax import lax
from jax.experimental import pallas as pl
from jax.experimental.pallas import tpu as pltpu
from jax.sharding import PartitionSpec as P

MESH = pl.DeviceIdType.MESH
F32 = jnp.float32
BF16 = jnp.bfloat16
EPS = 1e-05
TASK_EXPERTS = ((0, 1, 4, 5), (2, 3, 4, 5))
E = 6
H = 256
D = 512
TF = 256
TB = 512
SB = 256
CH = 32
VR = 72
CW = 384
NC = E + 1


def levels_of(count):
    levels, stride = [], 1
    while stride < count:
        radix = 4 if (count // stride) % 4 == 0 else count // stride
        levels.append((stride, radix))
        stride *= radix
    return levels


def plan_of(count):
    plan, rows = [], H
    for stride, radix in levels_of(count):
        split = rows % radix == 0 and (rows // radix) % 16 == 0
        plan.append((stride, radix, rows, rows // radix if split else rows))
        rows = plan[-1][3]
    return plan


def nn(a, b):
    return lax.dot_general(a, b, (((1,), (0,)), ((), ())), preferred_element_type=F32)


def nt(a, b):
    return lax.dot_general(a, b, (((1,), (1,)), ((), ())), preferred_element_type=F32)


def column(row):
    return jnp.broadcast_to(row, (128, 128)).T


def wide(table, width):
    return jnp.concatenate([table] * (width // 128), axis=1)


def fold8(value):
    total = value[0:8]
    for start in range(8, value.shape[0], 8):
        total = total + value[start : start + 8]
    return total


def fold_lanes(value):
    total = value[:, 0:128]
    for start in range(128, value.shape[1], 128):
        total = total + value[:, start : start + 128]
    return total


def lane_sums(partial):
    ones = jnp.ones((8, 128), F32)
    sums = lax.dot_general(
        ones, partial, (((1,), (1,)), ((), ())),
        preferred_element_type=F32, precision=lax.Precision.HIGHEST,
    )
    return sums[0:1]


def merge_stats(items):
    count = items[0][2:3]
    total = items[0][0:1]
    for item in items[1:]:
        count = count + item[2:3]
        total = total + item[0:1]
    mean = total / jnp.maximum(count, 1.0)
    square = jnp.zeros_like(total)
    for item in items:
        shift = item[0:1] / jnp.maximum(item[2:3], 1.0) - mean
        square = square + item[1:2] + item[2:3] * shift * shift
    return total, square, count


def main_kernel(
    plan, rows_core,
    x_hbm, v_ref, y_ref, win_ref, wout_ref, bin_ref, gain_ref, nb_ref, bout_ref, gate_ref, gb_ref,
    w1_ref, b1_ref, w2_ref, b2_ref, wl_ref, bl_ref,
    d_hbm, pred_hbm, gout_hbm, vout_ref, stat_ref,
    xbuf, zbuf, hbuf, dobuf, rbuf, dlogbuf, predbuf,
    wf, wb, gback, wot, wo, bct, g2t, b2t, gt, bot,
    w1t, w1n, w2f, w2b, b1t, b2tt, wlt, gbt,
    abuf, obuf, mixb, u1b, dmix,
    acc_in, acc_out, acc_gate, acc_first, acc_second,
    acc_u, acc_dlog, acc_lb, acc_last, acc_b2, acc_b1, s2row, vec,
    bias_snd, bias_rcv,
    st_mp, st_lv, v_mp, v_lv, hkeep, mprecv, lvrecv,
    sem_x, sem_w, sem_st, sem_v, sem_s, sem_r, sem_l, sem_d,
):
    R = rows_core
    n_levels = len(plan)
    b = lax.axis_index("batch")
    mp = lax.axis_index("mp")
    other = 1 - mp
    digits = [lax.rem(lax.div(b, stride), radix) for stride, radix, _, _ in plan]

    def peer(level, step):
        stride, radix = plan[level][:2]
        to = lax.rem(digits[level] + step, radix)
        return (b + (to - digits[level]) * stride, mp)

    def send(src, dst, ssem, rsem, to):
        copy = pltpu.make_async_remote_copy(
            src_ref=src, dst_ref=dst, send_sem=ssem, recv_sem=rsem,
            device_id=to, device_id_type=MESH,
        )
        copy.start()
        return copy

    n_x = 8
    xr = R // n_x
    x_copies = []
    for k in range(n_x):
        copy = pltpu.make_async_copy(
            x_hbm.at[pl.ds(pl.multiple_of(mp * R + k * xr, 16), xr), :],
            xbuf.at[pl.ds(k * xr, xr), :],
            sem_x.at[k],
        )
        copy.start()
        x_copies.append(copy)

    barrier = pltpu.get_barrier_semaphore()
    greets = [(b, other)]
    for level in range(n_levels):
        greets += [peer(level, step) for step in range(1, plan[level][1])]
    for to in greets:
        pl.semaphore_signal(barrier, inc=1, device_id=to, device_id_type=MESH)
    pl.semaphore_wait(barrier, len(greets))

    win_snd = dobuf.at[0:D, 0 : E * 128]
    win_rcv = dobuf.at[0:D, 1024 : 1024 + E * 128]
    wout_snd = dobuf.at[D : D + 128, 0 : E * H]
    wout_rcv = dobuf.at[D : D + 128, 2048 : 2048 + E * H]
    for e in range(E):
        win_snd[:, e * 128 : (e + 1) * 128] = win_ref[e].astype(BF16)
        wout_snd[:, e * H : (e + 1) * H] = wout_ref[e].astype(BF16)
    bias_snd[0:E] = bin_ref[...]
    bias_snd[8 : 8 + E] = gain_ref[...]
    bias_snd[16 : 16 + E] = nb_ref[...]
    w_copies = [
        send(win_snd, win_rcv, sem_w.at[0], sem_w.at[1], (b, other)),
        send(wout_snd, wout_rcv, sem_w.at[2], sem_w.at[3], (b, other)),
        send(bias_snd, bias_rcv, sem_w.at[4], sem_w.at[5], (b, other)),
    ]

    v_row = v_ref[:, pl.ds(pl.multiple_of(mp * R, 128), R)].astype(F32)
    count = jnp.sum(v_row, axis=1, keepdims=True)
    total = jnp.zeros((16, D), F32)
    for k in range(n_x):
        x_copies[k].wait()
        v16 = jnp.broadcast_to(v_row[:, k * xr : (k + 1) * xr], (16, xr)).astype(BF16)
        total = total + nn(v16, xbuf[pl.ds(k * xr, xr), :])
    mean = total[0:1] / jnp.maximum(count, 1.0)

    def square_step(k, total):
        r0 = pl.multiple_of(k * 256, 256)
        off = xbuf[pl.ds(r0, 256), :].astype(F32) - mean
        v16 = v_ref[:, pl.ds(pl.multiple_of(mp * R + k * 256, 128), 256)]
        v16 = jnp.broadcast_to(v16.astype(F32), (16, 256)).astype(BF16)
        return total + nn(v16, (off * off).astype(BF16))

    square = lax.fori_loop(0, R // 256, square_step, jnp.zeros((16, D), F32))
    st_mp[mp] = jnp.concatenate(
        [total[0:1], square[0:1], jnp.broadcast_to(count, (1, D)), jnp.zeros((5, D), F32)], axis=0
    )
    st_copy = send(st_mp.at[mp], st_mp.at[mp], sem_st.at[0], sem_st.at[1], (b, other))

    for t in range(2):
        w1n[t] = w1_ref[t].astype(BF16)
        w1t[t] = w1_ref[t].T.astype(BF16)
        b1t[t * 128 : (t + 1) * 128] = column(b1_ref[t : t + 1, :])
        for k in range(2):
            for e in range(3 * t, 3 * t + 3):
                bot[e * H + k * 128 : e * H + (k + 1) * 128] = column(
                    bout_ref[e : e + 1, k * 128 : (k + 1) * 128]
                )
    zero64 = jnp.zeros((64, 128), F32)
    zero128 = jnp.zeros((128, 64), F32)
    w2f[0:64] = jnp.concatenate([w2_ref[0], zero64], axis=1).astype(BF16)
    w2f[64:128] = jnp.concatenate([zero64, w2_ref[1]], axis=1).astype(BF16)
    w2b[0:128] = jnp.concatenate([w2_ref[0].T, zero128], axis=1).astype(BF16)
    w2b[128:256] = jnp.concatenate([zero128, w2_ref[1].T], axis=1).astype(BF16)
    b2tt[...] = column(jnp.concatenate([b2_ref[0:1, :], b2_ref[1:2, :]], axis=1))
    wlt[...] = column(jnp.concatenate([wl_ref[0:1, :], wl_ref[1:2, :]], axis=1))
    gbt[...] = jnp.concatenate(
        [jnp.full((1, 128), gb_ref[t, k], F32) for t in range(2) for k in range(4)], axis=0
    )
    gate = jnp.concatenate([gate_ref[0], gate_ref[1]], axis=0)
    gate_low = gate.astype(BF16).astype(F32)
    gback[...] = jnp.concatenate([gate_low, gate_low, jnp.zeros((112, D), F32)], axis=0).T.astype(BF16)
    acc_gate[...] = jnp.zeros_like(acc_gate)
    acc_first[...] = jnp.zeros_like(acc_first)
    acc_second[...] = jnp.zeros_like(acc_second)
    acc_dlog[...] = jnp.zeros_like(acc_dlog)
    acc_lb[...] = jnp.zeros_like(acc_lb)
    acc_last[...] = jnp.zeros_like(acc_last)
    acc_b1[...] = jnp.zeros_like(acc_b1)
    acc_b2[...] = jnp.zeros_like(acc_b2)

    def place(half, win, wout, bias):
        for e in range(E):
            at = pl.multiple_of(e * H + half * 128, 128)
            w = win[:, e * 128 : (e + 1) * 128]
            wb[:, pl.ds(at, 128)] = w
            wf[pl.ds(at, 128), :] = w.T
            o = wout[:, e * H : (e + 1) * H]
            wo[pl.ds(at, 128), :] = (o.astype(F32) * 0.5).astype(BF16)
            wot[pl.ds(e * H, H), pl.ds(pl.multiple_of(half * 128, 128), 128)] = o.T
            bct[pl.ds(at, 128), :] = column(bias[e : e + 1, :])
            gain = column(bias[8 + e : 9 + e, :])
            gt[pl.ds(at, 128), :] = gain
            g2t[pl.ds(at, 128), :] = gain * 0.5
            b2t[pl.ds(at, 128), :] = column(bias[16 + e : 17 + e, :]) * 0.5

    place(mp, win_snd, wout_snd, bias_snd)
    st_copy.wait()
    total, square, count = merge_stats([st_mp[0], st_mp[1]])
    st_copies = []
    for level in range(n_levels):
        own = digits[level]
        st_lv[level, own] = jnp.concatenate([total, square, count, jnp.zeros((5, D), F32)], axis=0)
        copies = []
        for step in range(1, plan[level][1]):
            base = 2 + (level * 3 + step - 1) * 2
            copies.append(
                send(
                    st_lv.at[level, own], st_lv.at[level, own],
                    sem_st.at[base], sem_st.at[base + 1], peer(level, step),
                )
            )
        if level == 0:
            for copy in w_copies:
                copy.wait()
            place(other, win_rcv, wout_rcv, bias_rcv)
            means = []
            for e in range(E):
                w = wf[e * H : (e + 1) * H, :].astype(F32)
                means.append(jnp.sum(w, axis=0, keepdims=True) * (1.0 / H))
                shift = jnp.sum(bct[e * H : (e + 1) * H, :], axis=0, keepdims=True) * (1.0 / H)
                bct[e * H : (e + 1) * H, :] = bct[e * H : (e + 1) * H, :] - shift
            pad = [jnp.zeros((2, D), F32)]
            means = jnp.concatenate(means + pad, axis=0)
            means_high = means.astype(BF16).astype(F32)
            wf[E * H : E * H + 32, :] = jnp.concatenate(
                [gate_low, means_high, means - means_high, jnp.zeros((8, D), F32)], axis=0
            ).astype(BF16)
        for copy in copies:
            copy.wait()
        total, square, count = merge_stats([st_lv[level, k] for k in range(plan[level][1])])
    mu = total / count
    inv = lax.rsqrt(square / count + EPS)
    stat_ref[...] = jnp.concatenate([mu, inv, count, jnp.zeros((5, D), F32)], axis=0)

    def forward(i):
        r0 = pl.multiple_of(i * TF, TF)
        x_tile = xbuf[pl.ds(r0, TF), :].astype(F32)
        xn = ((x_tile - stat_ref[0:1, :]) * stat_ref[1:2, :]).astype(BF16)
        xbuf[pl.ds(r0, TF), :] = xn
        ext = nt(wf[E * H : E * H + 32, :], xn)
        for e in range(E):
            abuf[e * H : (e + 1) * H, :] = nt(wf[e * H : (e + 1) * H, :], xn)
        for e in range(E):
            mean = ext[8 + e : 9 + e] + ext[16 + e : 17 + e]
            squares = jnp.zeros((8, TF), F32)
            for at in range(e * H, (e + 1) * H, CH):
                c = (abuf[at : at + CH, :] - mean) + wide(bct[at : at + CH, :], TF)
                abuf[at : at + CH, :] = c
                squares = squares + fold8(c * c)
            r = lax.rsqrt(jnp.sum(squares, axis=0, keepdims=True) * (1.0 / H) + EPS)
            rbuf[e : e + 1, pl.ds(r0, TF)] = r
            for at in range(e * H, (e + 1) * H, CH):
                zhat = abuf[at : at + CH, :] * r
                zbuf[at : at + CH, pl.ds(r0, TF)] = zhat.astype(BF16)
                half = zhat * wide(g2t[at : at + CH, :], TF) + wide(b2t[at : at + CH, :], TF)
                hbuf[at : at + CH, pl.ds(r0, TF)] = (half * (1.0 + jnp.tanh(half))).astype(BF16)
            o = nn(wot[e * H : (e + 1) * H, :], hbuf[e * H : (e + 1) * H, pl.ds(r0, TF)])
            obuf[e * H : (e + 1) * H, :] = o + wide(bot[e * H : (e + 1) * H, :], TF)
        return ext

    def heads(i, ext):
        r0 = pl.multiple_of(i * TF, TF)
        v0 = pl.multiple_of(mp * R + i * TF, 128)
        logits = ext[0:8] + wide(gbt[...], TF)
        probs = []
        for t in range(2):
            part = logits[4 * t : 4 * t + 4]
            part = jnp.exp(part - jnp.max(part, axis=0, keepdims=True))
            part = part / jnp.sum(part, axis=0, keepdims=True)
            probs.append([part[k : k + 1] for k in range(4)])
        for at in range(0, H, CH):
            for t in range(2):
                mixed = None
                for k in range(4):
                    e = TASK_EXPERTS[t][k]
                    term = probs[t][k] * obuf[e * H + at : e * H + at + CH, :]
                    mixed = term if mixed is None else mixed + term
                mixb[t * H + at : t * H + at + CH, :] = mixed.astype(BF16)
        slopes = []
        for t in range(2):
            pre = nn(w1t[t], mixb[t * H : (t + 1) * H, :])
            half = (pre + wide(b1t[t * 128 : (t + 1) * 128, :], TF)) * 0.5
            p = 1.0 + jnp.tanh(half)
            u1b[t * 128 : (t + 1) * 128, :] = (half * p).astype(BF16)
            slopes.append(0.5 * p * (1.0 + half * (2.0 - p)))
        half = (nn(w2f[...], u1b[...]) + wide(b2tt[...], TF)) * 0.5
        p = 1.0 + jnp.tanh(half)
        u2 = half * p
        slope2 = 0.5 * p * (1.0 + half * (2.0 - p))
        wl = wide(wlt[...], TF)
        weighted = u2 * wl
        d_logits = []
        valid = v_ref[:, pl.ds(v0, TF)].astype(F32)
        for t in range(2):
            logit = jnp.sum(weighted[t * 64 : (t + 1) * 64], axis=0, keepdims=True) + bl_ref[t]
            pred = 0.5 + 0.5 * jnp.tanh(0.5 * logit)
            predbuf[t : t + 1, pl.ds(r0, TF)] = pred
            label = y_ref[t : t + 1, pl.ds(v0, TF)].astype(F32)
            d_logits.append(valid * (pred - label))
        d_logit = jnp.concatenate(
            [jnp.broadcast_to(d_logits[t], (64, TF)) for t in range(2)], axis=0
        )
        acc_last[...] += fold_lanes(u2 * d_logit)
        acc_lb[0:2] += fold_lanes(jnp.concatenate(d_logits, axis=0))
        d2 = d_logit * wl * slope2
        acc_b2[...] += fold_lanes(d2)
        d2_low = d2.astype(BF16)
        acc_second[...] += nt(d2_low, u1b[...])
        d_u1 = nn(w2b[...], d2_low)
        for t in range(2):
            d1 = d_u1[t * 128 : (t + 1) * 128] * slopes[t]
            acc_b1[t * 128 : (t + 1) * 128] += fold_lanes(d1)
            d1_low = d1.astype(BF16)
            acc_first[t] += nt(mixb[t * H : (t + 1) * H, :], d1_low)
            dmix[t * H : (t + 1) * H, :] = nn(w1n[t], d1_low)
        dots = [[jnp.zeros((8, TF), F32) for _ in range(4)] for _ in range(2)]
        for at in range(0, H, CH):
            dm = [dmix[t * H + at : t * H + at + CH, :] for t in range(2)]
            grads = [None] * E
            for t in range(2):
                for k in range(4):
                    e = TASK_EXPERTS[t][k]
                    term = probs[t][k] * dm[t]
                    grads[e] = term if grads[e] is None else grads[e] + term
                    o = obuf[e * H + at : e * H + at + CH, :]
                    dots[t][k] = dots[t][k] + fold8(dm[t] * o)
            for e in range(E):
                dobuf[e * H + at : e * H + at + CH, pl.ds(r0, TF)] = grads[e].astype(BF16)
        rows = []
        for t in range(2):
            sums = [jnp.sum(dots[t][k], axis=0, keepdims=True) for k in range(4)]
            centre = sum(probs[t][k] * sums[k] for k in range(4))
            rows += [probs[t][k] * (sums[k] - centre) for k in range(4)]
        d_gate = jnp.concatenate(rows, axis=0)
        acc_dlog[...] += fold_lanes(d_gate)
        high = d_gate.astype(BF16).astype(F32)
        d_gate = jnp.concatenate([high, d_gate - high], axis=0).astype(BF16)
        dlogbuf[:, pl.ds(r0, TF)] = d_gate
        acc_gate[...] += nn(d_gate, xbuf[pl.ds(r0, TF), :])

    def forward_step(i, carry):
        heads(i, forward(i))
        return carry

    lax.fori_loop(0, R // TF, forward_step, 0)

    pending = []
    pred_at = pl.ds(pl.multiple_of(mp * R, 128), R)
    pred_local = pltpu.make_async_copy(predbuf, pred_hbm.at[:, pred_at], sem_l.at[0])
    pred_local.start()
    pending.append(pred_local)
    pending.append(send(predbuf, pred_hbm.at[:, pred_at], sem_w.at[6], sem_w.at[7], (b, other)))

    flight = {}
    n_sems = 1 + 2 * sum(radix - 1 for _, radix, _, _ in plan)

    def source(c, rows, place_at):
        base = 2048 if c == E else 0
        e = 0 if c == E else c
        return hbuf.at[pl.ds(e * H, rows), pl.ds(base + place_at * CW, CW)]

    def level_sems(level):
        return 1 + 2 * sum(radix - 1 for _, radix, _, _ in plan[:level])

    def start_pair(c):
        src = source(c, H, 0)
        flight[c] = [send(src, mprecv.at[c], sem_s.at[c, 0], sem_r.at[c, 0], (b, other))]

    def start_level(c, level, value):
        stride, radix, rows, after = plan[level]
        out = source(c, rows, 1 + level)
        out[...] = value.astype(BF16)
        copies = []
        for step in range(1, radix):
            k = level_sems(level) + step - 1
            part = out
            if after != rows:
                to = lax.rem(digits[level] + step, radix)
                part = out.at[pl.ds(pl.multiple_of(to * after, 16), after), :]
            dst = lvrecv[level].at[c, step]
            copies.append(send(part, dst, sem_s.at[c, k], sem_r.at[c, k], peer(level, step)))
        flight[c] = copies
        if after != rows:
            mine = out[pl.ds(pl.multiple_of(digits[level] * after, 16), after), :]
        else:
            mine = out[...]
        lvrecv[level][c, 0] = mine

    def finish_level(c, level):
        stride, radix, rows, after = plan[level]
        for copy in flight[c]:
            copy.wait()
        if after != rows:
            parts = [lvrecv[level][c, step].astype(F32) for step in range(radix)]
            return functools.reduce(lambda p, q: p + q, parts)
        total = None
        for k in range(radix):
            step = lax.rem(k - digits[level] + radix, radix)
            part = lvrecv[level][c, step].astype(F32)
            total = part if total is None else total + part
        return total

    def region(c, level):
        at = 0
        for k in range(level + 1):
            if plan[k][2] != plan[k][3]:
                at = at + digits[k] * plan[k][3]
        rows = plan[level][3] if level >= 0 else H
        if isinstance(at, int):
            return gout_hbm.at[c, pl.ds(at, rows), :]
        return gout_hbm.at[c, pl.ds(pl.multiple_of(at, 16), rows), :]

    split = [level for level in range(n_levels) if plan[level][2] != plan[level][3]]

    def start_result(c, value):
        rows = plan[-1][3]
        final = source(c, rows, 1 + n_levels)
        final[...] = value.astype(BF16)
        local = pltpu.make_async_copy(final, region(c, n_levels - 1), sem_l.at[1 + c])
        local.start()
        flight[c] = [local]
        if split:
            start_gather(c, split[-1], final)

    def start_gather(c, level, src):
        dst = region(c, level)
        for step in range(1, plan[level][1]):
            k = level_sems(level) + plan[level][1] - 1 + step - 1
            flight[c].append(send(src, dst, sem_s.at[c, k], sem_r.at[c, k], peer(level, step)))

    def chunk_steps(c):
        steps = []

        def from_pair():
            for copy in flight[c]:
                copy.wait()
            if c < E:
                value = hkeep[c % 2] + mprecv[c].astype(F32)
            else:
                value = source(c, H, 0)[...].astype(F32) + mprecv[c].astype(F32)
            start_level(c, 0, value)

        steps.append(from_pair)
        for level in range(n_levels):

            def next_level(level=level):
                value = finish_level(c, level)
                if level + 1 < n_levels:
                    start_level(c, level + 1, value)
                else:
                    start_result(c, value)

            steps.append(next_level)
        for place_in in range(len(split) - 1, 0, -1):

            def gather(place_in=place_in):
                for copy in flight[c]:
                    copy.wait()
                flight[c] = []
                start_gather(c, split[place_in - 1], region(c, split[place_in] - 1))

            steps.append(gather)

        def finish():
            for copy in flight[c]:
                copy.wait()
            flight[c] = []

        steps.append(finish)
        return steps

    queue = []

    def turn():
        for steps in list(queue):
            steps.pop(0)()
            if not steps:
                queue.remove(steps)

    def pack_towers():
        src = source(E, H, 0)
        src[:, 0:128] = acc_first[0].astype(BF16)
        src[:, 128:256] = acc_first[1].astype(BF16)
        gates = acc_gate[0:8] + acc_gate[8:16]
        rest = [acc_second[0:64, 0:128], acc_second[64:128, 128:256]]
        rest += [gates[:, k * 128 : (k + 1) * 128] for k in range(4)]
        rest.append(jnp.zeros((H - 160, 128), F32))
        src[:, 256:384] = jnp.concatenate(rest, axis=0).astype(BF16)

    def pack_expert(e):
        def half(h):
            at = pl.ds(pl.multiple_of(h * 128, 128), 128)
            a, o = acc_in[at, :], acc_out[at, :]
            top = jnp.concatenate([a[:, 0:256], o[:, 0:128]], axis=1)
            low = jnp.concatenate([a[:, 256:512], o[:, 128:256]], axis=1)
            return top, low

        top, low = half(mp)
        hkeep[e % 2, 0:128] = top
        hkeep[e % 2, 128:256] = low
        src = source(e, H, 0)
        top, low = half(other)
        src[0:128, :] = top.astype(BF16)
        src[128:256, :] = low.astype(BF16)

    ones16 = jnp.ones((16, SB), BF16)
    s2row[...] = jnp.sum(
        (gate_low * (acc_gate[0:8] + acc_gate[8:16])), axis=0, keepdims=True
    )

    def backward_part(e, r0):
        at0 = e * H
        lanes = pl.ds(r0, SB)
        do = dobuf[at0 : at0 + H, lanes]
        dmix[0:H, :] = nn(wo[at0 : at0 + H, :], do)
        acc_out[...] += nt(hbuf[at0 : at0 + H, lanes], do)
        vec[3] += nt(ones16, do)[0:8]
        r = rbuf[e : e + 1, lanes]
        m1 = jnp.zeros((8, SB), F32)
        m2 = jnp.zeros((8, SB), F32)
        for u in range(0, H, CH):
            at = at0 + u
            zhat = zbuf[at : at + CH, lanes].astype(F32)
            half = zhat * wide(g2t[at : at + CH, :], SB) + wide(b2t[at : at + CH, :], SB)
            p = 1.0 + jnp.tanh(half)
            dz = dmix[u : u + CH, :] * (p * (1.0 + half * (2.0 - p)))
            q = dz * zhat
            acc_u[0, u : u + CH, :] += fold_lanes(dz)
            acc_u[1, u : u + CH, :] += fold_lanes(q)
            g = wide(gt[at : at + CH, :], SB)
            dzg = dz * g
            dmix[u : u + CH, :] = dzg
            m1 = m1 + fold8(dzg)
            m2 = m2 + fold8(q * g)
        m1 = jnp.sum(m1, axis=0, keepdims=True) * (1.0 / H)
        m2 = jnp.sum(m2, axis=0, keepdims=True) * (1.0 / H)
        for u in range(0, H, CH):
            at = at0 + u
            zhat = zbuf[at : at + CH, lanes].astype(F32)
            da = r * (dmix[u : u + CH, :] - m1 - zhat * m2)
            acc_u[2, u : u + CH, :] += fold_lanes(da)
            zbuf[at : at + CH, lanes] = da.astype(BF16)
        acc_in[...] += nn(zbuf[at0 : at0 + H, lanes], xbuf[pl.ds(r0, SB), :])

    for e in range(E):
        acc_in[...] = jnp.zeros_like(acc_in)
        acc_out[...] = jnp.zeros_like(acc_out)
        acc_u[...] = jnp.zeros_like(acc_u)
        vec[3] = jnp.zeros((8, H), F32)

        def backward_step(i, carry, e=e):
            for part in range(TB // SB):
                backward_part(e, pl.multiple_of(i * TB + part * SB, SB))
            return carry

        n_b = R // TB
        lax.fori_loop(0, n_b // 2, backward_step, 0)
        turn()
        lax.fori_loop(n_b // 2, n_b, backward_step, 0)
        turn()
        if e == 0:
            pack_towers()
            start_pair(E)
            queue.append(chunk_steps(E))
        pack_expert(e)
        start_pair(e)
        queue.append(chunk_steps(e))
        for k, row in ((0, 2), (1, 1), (2, 0)):
            sums = lane_sums(acc_u[row])
            v_mp[mp, k * 12 + 2 * e : k * 12 + 2 * e + 1, :] = sums[:, 0:128]
            v_mp[mp, k * 12 + 2 * e + 1 : k * 12 + 2 * e + 2, :] = sums[:, 128:256]
        bo = vec[3][0:1]
        v_mp[mp, 36 + 2 * e : 37 + 2 * e, :] = bo[:, 0:128]
        v_mp[mp, 37 + 2 * e : 38 + 2 * e, :] = bo[:, 128:256]
        cross = jnp.zeros((8, D), F32)
        for u in range(0, H, CH):
            w = wf[e * H + u : e * H + u + CH, :].astype(F32)
            cross = cross + fold8(w * acc_in[u : u + CH, :])
        s2row[...] += jnp.sum(cross, axis=0, keepdims=True)

    for k in range(4):
        v_mp[mp, 48 + k : 49 + k, :] = s2row[:, k * 128 : (k + 1) * 128]
    v_mp[mp, 52:60, :] = acc_dlog[...]
    v_mp[mp, 60:61, :] = lane_sums(acc_last[...])
    v_mp[mp, 61:63, :] = acc_lb[0:2]
    b1_sums = lane_sums(acc_b1[...])
    v_mp[mp, 63:64, :] = b1_sums[:, 0:128]
    v_mp[mp, 64:65, :] = b1_sums[:, 128:256]
    v_mp[mp, 65:66, :] = lane_sums(acc_b2[...])
    v_mp[mp, 66:VR, :] = jnp.zeros((VR - 66, 128), F32)
    flight["v"] = [send(v_mp.at[mp], v_mp.at[mp], sem_v.at[0], sem_v.at[1], (b, other))]

    def small_level(level, total):
        own = digits[level]
        v_lv[level, own] = total
        flight["v"] = []
        for step in range(1, plan[level][1]):
            base = 2 + (level * 3 + step - 1) * 2
            flight["v"].append(
                send(
                    v_lv.at[level, own], v_lv.at[level, own],
                    sem_v.at[base], sem_v.at[base + 1], peer(level, step),
                )
            )

    def small_steps():
        steps = []

        def first():
            for copy in flight["v"]:
                copy.wait()
            small_level(0, v_mp[0] + v_mp[1])

        steps.append(first)
        for level in range(n_levels):

            def step(level=level):
                for copy in flight["v"]:
                    copy.wait()
                total = v_lv[level, 0]
                for k in range(1, plan[level][1]):
                    total = total + v_lv[level, k]
                if level + 1 < n_levels:
                    small_level(level + 1, total)
                    return
                vout_ref[...] = total
                row = jnp.concatenate([total[k : k + 1] for k in range(2 * E)], axis=1)
                row_high = row.astype(BF16).astype(F32)
                rows = jnp.concatenate(
                    [row_high, row - row_high, jnp.zeros((14, E * H), F32)], axis=0
                ).astype(BF16)
                s1 = nn(rows, wf[0 : E * H, :])
                gate_sum = jnp.sum(total[52:60], axis=1, keepdims=True)
                gate_part = jnp.sum(gate_low * gate_sum, axis=0, keepdims=True)
                stat_ref[3:4, :] = s1[0:1] + s1[1:2] + gate_part
                stat_ref[4:5, :] = jnp.concatenate([total[48 + k : 49 + k] for k in range(4)], axis=1)

            steps.append(step)
        return steps

    queue.append(small_steps())

    def input_gradient(i, carry):
        r0 = pl.multiple_of(i * TB, TB)
        lanes = pl.ds(r0, TB)
        da = zbuf[:, lanes]
        dl = dlogbuf[:, lanes]
        for k, half in ((0, mp), (1, other)):
            at = pl.ds(pl.multiple_of(half * 256, 256), 256)
            grad = nn(wb[at, :], da) + nn(gback[at, 0:16], dl)
            dobuf[k * H : (k + 1) * H, lanes] = grad.astype(BF16)
        return carry

    n_c = R // TB
    for part in range(4):
        lax.fori_loop(part * n_c // 4, (part + 1) * n_c // 4, input_gradient, 0)
        turn()
        w = R // 4
        at = pl.ds(part * w, w)
        to = pl.ds(pl.multiple_of(mp * R + part * w, 128), w)
        local = pltpu.make_async_copy(dobuf.at[0:H, at], d_hbm.at[:, to], sem_l.at[8 + part])
        local.start()
        pending.append(local)
        pending.append(
            send(dobuf.at[H : 2 * H, at], d_hbm.at[:, to], sem_d.at[part], sem_d.at[4 + part], (b, other))
        )
    while queue:
        turn()
    for copy in pending:
        copy.wait()


def final_kernel(
    rows_tile, dt_ref, x_ref, v_ref, pred_ref, gout_ref, vout_ref, stat_ref,
    o_pred, o_feat, o_in, o_inb, o_gain, o_nb, o_out, o_outb, o_gate, o_gateb,
    o_w1, o_b1, o_w2, o_b2, o_wl, o_bl,
):
    mp = lax.axis_index("mp")
    half = pl.ds(pl.multiple_of(mp * 256, 256), 256)
    count = stat_ref[2:3, half]
    inv = stat_ref[1:2, half]
    mu = stat_ref[0:1, half]
    s1 = stat_ref[3:4, half] / count
    s2 = stat_ref[4:5, half] / count
    for at in range(0, rows_tile, 128):
        valid = jnp.broadcast_to(v_ref[:, at : at + 128].astype(F32), (128, 128)).T
        for k in range(2):
            cols = slice(k * 128, (k + 1) * 128)
            grad = dt_ref[cols, at : at + 128].astype(F32).T
            xhat = (x_ref[at : at + 128, cols].astype(F32) - mu[:, cols]) * inv[:, cols]
            o_feat[at : at + 128, cols] = inv[:, cols] * (
                grad - valid * (s1[:, cols] + xhat * s2[:, cols])
            )

    @pl.when(pl.program_id(0) == 0)
    def _():
        scale = 1.0 / stat_ref[2:3, 0:128]
        o_pred[...] = pred_ref[...]
        for e in range(E):
            g = gout_ref[e].astype(F32) * scale[:, 0:1]
            for k in range(2):
                o_in[e, k * 256 : k * 256 + 128, :] = g[k * 128 : (k + 1) * 128, 0:128].T
                o_in[e, k * 256 + 128 : k * 256 + 256, :] = g[k * 128 : (k + 1) * 128, 128:256].T
                o_out[e, :, k * 128 : (k + 1) * 128] = g[k * 128 : (k + 1) * 128, 256:384]
            for ref, base in ((o_inb, 0), (o_gain, 12), (o_nb, 24)):
                ref[e : e + 1, :] = vout_ref[pl.ds(base + 2 * e + mp, 1), :] * scale
            for k in range(2):
                o_outb[e : e + 1, k * 128 : (k + 1) * 128] = (
                    vout_ref[36 + 2 * e + k : 37 + 2 * e + k, :] * scale
                )
        g = gout_ref[E].astype(F32) * scale[:, 0:1]
        o_w1[0] = g[:, 0:128]
        o_w1[1] = g[:, 128:256]
        o_w2[0] = g[0:64, 256:384]
        o_w2[1] = g[64:128, 256:384]
        for k in range(4):
            part = g[128 + 8 * k : 136 + 8 * k, 256:384]
            o_gate[0, :, k * 128 : (k + 1) * 128] = part[0:4]
            o_gate[1, :, k * 128 : (k + 1) * 128] = part[4:8]
        gate_bias = jnp.sum(vout_ref[52:60, :], axis=1, keepdims=True) * scale
        table = jnp.concatenate([gate_bias, jnp.zeros((120, 128), F32)], axis=0).T
        o_gateb[0:1, :] = table[0:1, 0:4]
        o_gateb[1:2, :] = table[0:1, 4:8]
        last = vout_ref[60:61, :] * scale
        o_wl[0:1, :] = last[:, 0:64]
        o_wl[1:2, :] = last[:, 64:128]
        o_bl[...] = jnp.sum(vout_ref[61:63, :], axis=1, keepdims=True) * scale
        o_b1[...] = vout_ref[63:65, :] * scale
        b2 = vout_ref[65:66, :] * scale
        o_b2[0:1, :] = b2[:, 0:64]
        o_b2[1:2, :] = b2[:, 64:128]


def on_device(
    features, validity, labels, expert_in, expert_in_bias, norm_gain, norm_bias, expert_out,
    expert_out_bias, gate_weight, gate_bias, tower_first, tower_first_bias, tower_second,
    tower_second_bias, tower_last, tower_last_bias,
):
    rows = features.shape[0]
    R = rows // 2
    n_batch = lax.axis_size("batch")
    plan = plan_of(n_batch)
    n_levels = len(plan)
    n_peers = sum(radix - 1 for _, radix, _, _ in plan)
    n_sems = 1 + 2 * n_peers
    v_row = validity.reshape(1, rows)
    y_rows = labels.T
    vm = pl.BlockSpec(memory_space=pltpu.VMEM)
    sm = pl.BlockSpec(memory_space=pltpu.SMEM)
    hb = pl.BlockSpec(memory_space=pl.ANY)
    dma = pltpu.SemaphoreType.DMA

    def scr(*shape, dtype=F32):
        return pltpu.VMEM(shape, dtype)

    scratch = [
        scr(R, D, dtype=BF16), scr(E * H, R, dtype=BF16), scr(E * H, R, dtype=BF16),
        scr(E * H, R, dtype=BF16), scr(8, R), scr(16, R, dtype=BF16), scr(2, R),
        scr(E * H + 32, D, dtype=BF16), scr(D, E * H, dtype=BF16), scr(D, 128, dtype=BF16),
        scr(E * H, H, dtype=BF16), scr(E * H, H, dtype=BF16),
        scr(E * H, 128), scr(E * H, 128), scr(E * H, 128), scr(E * H, 128), scr(E * H, 128),
        scr(2, 128, H, dtype=BF16), scr(2, H, 128, dtype=BF16), scr(128, H, dtype=BF16),
        scr(H, 128, dtype=BF16), scr(H, 128), scr(128, 128), scr(128, 128), scr(8, 128),
        scr(E * H, TF), scr(E * H, TF), scr(2 * H, TF, dtype=BF16), scr(H, TF, dtype=BF16), scr(2 * H, TF),
        scr(H, D), scr(H, H), scr(16, D), scr(2, H, 128), scr(128, H),
        scr(3, H, 128), scr(8, 128), scr(8, 128), scr(128, 128), scr(128, 128), scr(H, 128),
        scr(1, D), scr(4, 8, H),
        scr(24, 128), scr(24, 128),
        scr(2, 8, D), scr(n_levels, 4, 8, D), scr(2, VR, 128), scr(n_levels, 4, VR, 128),
        scr(2, H, CW), scr(NC, H, CW, dtype=BF16),
        [scr(NC, radix, after, CW, dtype=BF16) for _, radix, _, after in plan],
        dma((8,)), dma((8,)), dma((2 + 6 * n_levels,)), dma((2 + 6 * n_levels,)),
        dma((NC, n_sems)), dma((NC, n_sems)), dma((12,)), dma((8,)),
    ]
    flops = 2 * R * (6 * D * E * H // 2 + 3 * E * H * H)
    d_half, preds, gsum, vsum, stats = pl.pallas_call(
        functools.partial(main_kernel, plan, R),
        out_shape=(
            jax.ShapeDtypeStruct((256, rows), BF16),
            jax.ShapeDtypeStruct((2, rows), F32),
            jax.ShapeDtypeStruct((NC, H, CW), BF16),
            jax.ShapeDtypeStruct((VR, 128), F32),
            jax.ShapeDtypeStruct((8, D), F32),
        ),
        in_specs=[hb] + [vm] * 9 + [sm] + [vm] * 5 + [sm],
        out_specs=(hb, hb, hb, vm, vm),
        scratch_shapes=scratch,
        compiler_params=pltpu.CompilerParams(
            collective_id=0, has_side_effects=True, vmem_limit_bytes=64 * 2**20 - 65536
        ),
        cost_estimate=pl.CostEstimate(flops=flops, bytes_accessed=20 * 2**20, transcendentals=0),
        name="layer",
    )(
        features, v_row, y_rows, expert_in, expert_out, expert_in_bias, norm_gain, norm_bias,
        expert_out_bias, jnp.swapaxes(gate_weight, 1, 2), gate_bias, tower_first, tower_first_bias,
        jnp.swapaxes(tower_second, 1, 2), tower_second_bias, tower_last, tower_last_bias,
    )

    tile = 512
    whole = lambda *shape: pl.BlockSpec(shape, lambda i: (0,) * len(shape))
    half_index = lambda i: (i, lax.axis_index("mp"))
    out_shapes = [
        (2, rows), (rows, 256), (E, D, 128), (E, 128), (E, 128), (E, 128), (E, 128, H), (E, H),
        (2, 4, D), (2, 4), (2, H, 128), (2, 128), (2, 64, 128), (2, 64), (2, 64), (2, 128),
    ]
    out_specs = [whole(*shape) for shape in out_shapes]
    out_specs[1] = pl.BlockSpec((tile, 256), lambda i: (i, 0))
    outs = pl.pallas_call(
        functools.partial(final_kernel, tile),
        grid=(rows // tile,),
        out_shape=[jax.ShapeDtypeStruct(shape, F32) for shape in out_shapes],
        in_specs=[
            pl.BlockSpec((256, tile), lambda i: (0, i)),
            pl.BlockSpec((tile, 256), half_index),
            pl.BlockSpec((1, tile), lambda i: (0, i)),
            whole(2, rows), whole(NC, H, CW), whole(VR, 128), whole(8, D),
        ],
        out_specs=out_specs,
        compiler_params=pltpu.CompilerParams(vmem_limit_bytes=48 * 2**20),
        cost_estimate=pl.CostEstimate(
            flops=rows * 256 * 8, bytes_accessed=rows * 256 * 8, transcendentals=0
        ),
        name="finish",
    )(d_half, features, v_row, preds, gsum, vsum, stats)
    outs = list(outs)
    outs[0] = outs[0].T
    outs[8] = jnp.swapaxes(outs[8], 1, 2)
    outs[12] = jnp.swapaxes(outs[12], 1, 2)
    outs[15] = outs[15][:, 0]
    return tuple(outs)


def solution(mesh):
    in_specs = (
        P("batch", None), P("batch"), P("batch", None), P(None, None, "mp"), P(None, "mp"),
        P(None, "mp"), P(None, "mp"), P(None, "mp", None), P(), P(), P(), P(), P(), P(), P(), P(), P(),
    )
    out_specs = (
        P("batch", None), P("batch", "mp"), P(None, None, "mp"), P(None, "mp"), P(None, "mp"),
        P(None, "mp"), P(None, "mp", None), P(), P(), P(), P(), P(), P(), P(), P(), P(),
    )
    return jax.shard_map(
        on_device, mesh=mesh, in_specs=in_specs, out_specs=out_specs, check_vma=False
    )
```

```python
import functools

import jax
import jax.numpy as jnp
from jax import lax
from jax.experimental import pallas as pl
from jax.experimental.pallas import tpu as pltpu
from jax.sharding import PartitionSpec as P

MESH = pl.DeviceIdType.MESH
F32 = jnp.float32
BF16 = jnp.bfloat16
EPS = 1e-05
TASK_EXPERTS = ((0, 1, 4, 5), (2, 3, 4, 5))
E = 6
H = 256
D = 512
TF = 256
TB = 512
SB = 256
CH = 32
VR = 72
HE = H + 16
WIDTHS = (256,) * E + (384,) * 3
NC = len(WIDTHS)
TOWERS = E


def levels_of(count):
    levels, stride = [], 1
    while stride < count:
        radix = 4 if (count // stride) % 4 == 0 else count // stride
        levels.append((stride, radix))
        stride *= radix
    return levels


def plan_of(count):
    plan, rows = [], H
    for stride, radix in levels_of(count):
        split = rows % radix == 0 and (rows // radix) % 16 == 0
        plan.append((stride, radix, rows, rows // radix if split else rows))
        rows = plan[-1][3]
    return plan


def nn(a, b):
    return lax.dot_general(a, b, (((1,), (0,)), ((), ())), preferred_element_type=F32)


def nt(a, b):
    return lax.dot_general(a, b, (((1,), (1,)), ((), ())), preferred_element_type=F32)


def column(row):
    return jnp.broadcast_to(row, (128, 128)).T


def wide(table, width):
    return jnp.concatenate([table] * (width // 128), axis=1)


def fold8(value):
    total = value[0:8]
    for start in range(8, value.shape[0], 8):
        total = total + value[start : start + 8]
    return total


def fold_lanes(value):
    total = value[:, 0:128]
    for start in range(128, value.shape[1], 128):
        total = total + value[:, start : start + 128]
    return total


def lane_sums(partial):
    ones = jnp.ones((8, 128), F32)
    sums = lax.dot_general(
        ones, partial, (((1,), (1,)), ((), ())),
        preferred_element_type=F32, precision=lax.Precision.HIGHEST,
    )
    return sums[0:1]


def merge_stats(items):
    count = items[0][2:3]
    total = items[0][0:1]
    for item in items[1:]:
        count = count + item[2:3]
        total = total + item[0:1]
    mean = total / jnp.maximum(count, 1.0)
    square = jnp.zeros_like(total)
    for item in items:
        shift = item[0:1] / jnp.maximum(item[2:3], 1.0) - mean
        square = square + item[1:2] + item[2:3] * shift * shift
    return total, square, count


def main_kernel(
    plan, rows_core,
    x_hbm, v_ref, y_ref, win_hbm, wout_hbm, bin_ref, gain_ref, nb_ref, bout_ref, gate_ref, gb_ref,
    w1_ref, b1_ref, w2_ref, b2_ref, wl_ref, bl_ref,
    d_hbm, pred_hbm, gout_hbm, vout_ref, stat_ref, wb_hbm,
    xbuf, zbuf, sbuf, dobuf, rbuf, dlogbuf, predbuf,
    wf, gback, wot, pk, g2t, b2t,
    w1t, w1n, w2f, w2b, b1t, b2tt, wlt, gbt,
    abufs, hbufs, logit_bufs, mixb, u1b, dmix,
    acc_out, acc_gate, acc_first, acc_second,
    acc_dlog, acc_lb, acc_last, acc_b2, acc_b1, s2row,
    bias_snd, bias_rcv,
    st_mp, st_lv, v_mp, v_lv, sends, sends_low, mprecv, lvrecv,
    sem_x, sem_w, sem_st, sem_v, sem_s, sem_r, sem_l, sem_d, sem_f,
):
    R = rows_core
    abuf = abufs[0]
    acc_in = (abuf.at[0:H, :], abuf.at[H : 2 * H, :])
    hkeep = (abuf.at[2 * H : 3 * H, :], abuf.at[3 * H : 4 * H, :])
    acc_u = (
        abuf.at[4 * H : 5 * H, 0:128], abuf.at[4 * H : 5 * H, 128:256], abuf.at[5 * H : 6 * H, 0:128]
    )
    n_levels = len(plan)
    b = lax.axis_index("batch")
    mp = lax.axis_index("mp")
    other = 1 - mp
    digits = [lax.rem(lax.div(b, stride), radix) for stride, radix, _, _ in plan]

    def peer(level, step):
        stride, radix = plan[level][:2]
        to = lax.rem(digits[level] + step, radix)
        return (b + (to - digits[level]) * stride, mp)

    def send(src, dst, ssem, rsem, to):
        copy = pltpu.make_async_remote_copy(
            src_ref=src, dst_ref=dst, send_sem=ssem, recv_sem=rsem,
            device_id=to, device_id_type=MESH,
        )
        copy.start()
        return copy

    n_x = 8
    xr = R // n_x
    x_copies = []
    for k in range(n_x):
        copy = pltpu.make_async_copy(
            x_hbm.at[pl.ds(pl.multiple_of(mp * R + k * xr, 16), xr), :],
            xbuf.at[pl.ds(k * xr, xr), :],
            sem_x.at[k],
        )
        copy.start()
        x_copies.append(copy)

    f_copies = []
    for e in range(E):
        for k in range(2):
            f_copies.append(
                pltpu.make_async_copy(
                    win_hbm.at[e, k * H : (k + 1) * H, :],
                    abuf.at[e * H : (e + 1) * H, k * 128 : (k + 1) * 128],
                    sem_f.at[2 * e + k],
                )
            )
        f_copies.append(
            pltpu.make_async_copy(
                wout_hbm.at[e], acc_out.at[e * 128 : (e + 1) * 128, :], sem_f.at[2 * E + e]
            )
        )
    for copy in f_copies:
        copy.start()

    barrier = pltpu.get_barrier_semaphore()
    greets = [(b, other)]
    for level in range(n_levels):
        greets += [peer(level, step) for step in range(1, plan[level][1])]
    for to in greets:
        pl.semaphore_signal(barrier, inc=1, device_id=to, device_id_type=MESH)
    pl.semaphore_wait(barrier, len(greets))

    win_snd = dobuf.at[0:D, 0 : E * 128]
    win_rcv = dobuf.at[0:D, 1024 : 1024 + E * 128]
    wout_snd = dobuf.at[D : D + 128, 0 : E * H]
    wout_rcv = dobuf.at[D : D + 128, 2048 : 2048 + E * H]
    for copy in f_copies:
        copy.wait()
    for e in range(E):
        for k in range(2):
            win_snd[k * H : (k + 1) * H, e * 128 : (e + 1) * 128] = abuf[
                e * H : (e + 1) * H, k * 128 : (k + 1) * 128
            ].astype(BF16)
        wout_snd[:, e * H : (e + 1) * H] = acc_out[e * 128 : (e + 1) * 128, :].astype(BF16)
    bias_snd[0:E] = bin_ref[...]
    bias_snd[8 : 8 + E] = gain_ref[...]
    bias_snd[16 : 16 + E] = nb_ref[...]
    w_copies = [
        send(win_snd, win_rcv, sem_w.at[0], sem_w.at[1], (b, other)),
        send(wout_snd, wout_rcv, sem_w.at[2], sem_w.at[3], (b, other)),
        send(bias_snd, bias_rcv, sem_w.at[4], sem_w.at[5], (b, other)),
    ]

    v_row = v_ref[:, pl.ds(pl.multiple_of(mp * R, 128), R)].astype(F32)
    count = jnp.sum(v_row, axis=1, keepdims=True)
    total = jnp.zeros((16, D), F32)
    for k in range(n_x):
        x_copies[k].wait()
        v16 = jnp.broadcast_to(v_row[:, k * xr : (k + 1) * xr], (16, xr)).astype(BF16)
        total = total + nn(v16, xbuf[pl.ds(k * xr, xr), :])
    mean = total[0:1] / jnp.maximum(count, 1.0)

    def square_step(k, total):
        r0 = pl.multiple_of(k * 256, 256)
        off = xbuf[pl.ds(r0, 256), :].astype(F32) - mean
        v16 = v_ref[:, pl.ds(pl.multiple_of(mp * R + k * 256, 128), 256)]
        v16 = jnp.broadcast_to(v16.astype(F32), (16, 256)).astype(BF16)
        return total + nn(v16, (off * off).astype(BF16))

    square = lax.fori_loop(0, R // 256, square_step, jnp.zeros((16, D), F32))
    st_mp[mp] = jnp.concatenate(
        [total[0:1], square[0:1], jnp.broadcast_to(count, (1, D)), jnp.zeros((5, D), F32)], axis=0
    )
    st_copy = send(st_mp.at[mp], st_mp.at[mp], sem_st.at[0], sem_st.at[1], (b, other))

    for t in range(2):
        w1n[t] = w1_ref[t].astype(BF16)
        w1t[t] = (w1_ref[t].T * 0.5).astype(BF16)
        b1t[t * 128 : (t + 1) * 128] = column(b1_ref[t : t + 1, :]) * 0.5
    zero64 = jnp.zeros((64, 128), F32)
    zero128 = jnp.zeros((128, 64), F32)
    w2f[0:64] = (jnp.concatenate([w2_ref[0], zero64], axis=1) * 0.5).astype(BF16)
    w2f[64:128] = (jnp.concatenate([zero64, w2_ref[1]], axis=1) * 0.5).astype(BF16)
    w2b[0:128] = (jnp.concatenate([w2_ref[0].T, zero128], axis=1) * 0.5).astype(BF16)
    w2b[128:256] = (jnp.concatenate([zero128, w2_ref[1].T], axis=1) * 0.5).astype(BF16)
    b2tt[...] = column(jnp.concatenate([b2_ref[0:1, :], b2_ref[1:2, :]], axis=1)) * 0.5
    wlt[...] = column(jnp.concatenate([wl_ref[0:1, :], wl_ref[1:2, :]], axis=1))
    gbt[...] = jnp.concatenate(
        [jnp.full((1, 128), gb_ref[t, k], F32) for t in range(2) for k in range(4)], axis=0
    )
    gate = jnp.concatenate([gate_ref[0], gate_ref[1]], axis=0)
    gate_low = gate.astype(BF16).astype(F32)
    gback[...] = jnp.concatenate([gate_low, gate_low, jnp.zeros((112, D), F32)], axis=0).T.astype(BF16)
    acc_gate[...] = jnp.zeros_like(acc_gate)
    acc_out[...] = jnp.zeros_like(acc_out)
    for hbuf in hbufs:
        for e in range(E):
            hbuf[e * HE + H : (e + 1) * HE, :] = jnp.ones((16, TF), BF16)
    acc_first[...] = jnp.zeros_like(acc_first)
    acc_second[...] = jnp.zeros_like(acc_second)
    acc_dlog[...] = jnp.zeros_like(acc_dlog)
    acc_lb[...] = jnp.zeros_like(acc_lb)
    acc_last[...] = jnp.zeros_like(acc_last)
    acc_b1[...] = jnp.zeros_like(acc_b1)
    acc_b2[...] = jnp.zeros_like(acc_b2)

    lane = lax.broadcasted_iota(jnp.int32, (128, 128), 1)

    def place(half, win, wout, bias):
        for e in range(E):
            at = pl.multiple_of(e * H + half * 128, 128)
            w = win[:, e * 128 : (e + 1) * 128]
            wf[pl.ds(at, 128), :] = w.T
            o = wout[:, e * H : (e + 1) * H]
            wot[pl.ds(e * H, H), pl.ds(pl.multiple_of(half * 128, 128), 128)] = o.T
            gain = column(bias[8 + e : 9 + e, :])
            pk[pl.ds(at, 128), :] = jnp.where(lane == 0, column(bias[e : e + 1, :]), gain)
            g2t[pl.ds(at, 128), :] = gain * 0.5
            b2t[pl.ds(at, 128), :] = column(bias[16 + e : 17 + e, :]) * 0.5

    place(mp, win_snd, wout_snd, bias_snd)
    st_copy.wait()
    total, square, count = merge_stats([st_mp[0], st_mp[1]])
    st_copies = []
    for level in range(n_levels):
        own = digits[level]
        st_lv[level, own] = jnp.concatenate([total, square, count, jnp.zeros((5, D), F32)], axis=0)
        copies = []
        for step in range(1, plan[level][1]):
            base = 2 + (level * 3 + step - 1) * 2
            copies.append(
                send(
                    st_lv.at[level, own], st_lv.at[level, own],
                    sem_st.at[base], sem_st.at[base + 1], peer(level, step),
                )
            )
        if level == 0:
            for copy in w_copies:
                copy.wait()
            place(other, win_rcv, wout_rcv, bias_rcv)
            keep = [
                pltpu.make_async_copy(win_snd, wb_hbm.at[mp], sem_f.at[0]),
                pltpu.make_async_copy(win_rcv, wb_hbm.at[other], sem_f.at[1]),
            ]
            for copy in keep:
                copy.start()
            means = []
            for e in range(E):
                w = wf[e * H : (e + 1) * H, :].astype(F32)
                means.append(jnp.sum(w, axis=0, keepdims=True) * (1.0 / H))
                shift = jnp.sum(pk[e * H : (e + 1) * H, 0:1], axis=0, keepdims=True) * (1.0 / H)
                for k in range(2):
                    at = slice(e * H + k * 128, e * H + (k + 1) * 128)
                    table = pk[at, :]
                    table = jnp.where(lane == 0, table - shift, table)
                    second = column(bout_ref[e : e + 1, k * 128 : (k + 1) * 128])
                    pk[at, :] = jnp.where(lane == 1, second, table)
            pad = [jnp.zeros((2, D), F32)]
            means = jnp.concatenate(means + pad, axis=0)
            means_high = means.astype(BF16).astype(F32)
            wf[E * H : E * H + 32, :] = jnp.concatenate(
                [gate_low, means_high, means - means_high, jnp.zeros((8, D), F32)], axis=0
            ).astype(BF16)
        for copy in copies:
            copy.wait()
        total, square, count = merge_stats([st_lv[level, k] for k in range(plan[level][1])])
    mu = total / count
    inv = lax.rsqrt(square / count + EPS)
    stat_ref[...] = jnp.concatenate([mu, inv, count, jnp.zeros((5, D), F32)], axis=0)

    def forward(i, side):
        abuf, hbuf = abufs[side], hbufs[side]
        r0 = pl.multiple_of(i * TF, TF)
        x_tile = xbuf[pl.ds(r0, TF), :].astype(F32)
        xn = ((x_tile - stat_ref[0:1, :]) * stat_ref[1:2, :]).astype(BF16)
        xbuf[pl.ds(r0, TF), :] = xn
        ext = nt(wf[E * H : E * H + 32, :], xn)
        logit_bufs[side][...] = ext[0:8] + wide(gbt[...], TF)
        means = ext[8:16] + ext[16:24]

        def product(e):
            abuf[e * H : (e + 1) * H, :] = nt(wf[e * H : (e + 1) * H, :], xn)

        def norm(e):
            squares = jnp.zeros((8, TF), F32)
            for at in range(e * H, (e + 1) * H, CH):
                c = (abuf[at : at + CH, :] - means[e : e + 1]) + pk[at : at + CH, 0:1]
                abuf[at : at + CH, :] = c
                squares = squares + fold8(c * c)
            r = lax.rsqrt(jnp.sum(squares, axis=0, keepdims=True) * (1.0 / H) + EPS)
            rbuf[e : e + 1, pl.ds(r0, TF)] = r
            for u in range(0, H, CH):
                at = e * H + u
                zhat = abuf[at : at + CH, :] * r
                zbuf[at : at + CH, pl.ds(r0, TF)] = zhat.astype(BF16)
                half = zhat * wide(g2t[at : at + CH, :], TF) + wide(b2t[at : at + CH, :], TF)
                p = 1.0 + jnp.tanh(half)
                h = half * p
                hbuf[e * HE + u : e * HE + u + CH, :] = h.astype(BF16)
                slope = (p + h * (2.0 - p)) * pk[at : at + CH, 2:3]
                sbuf[at : at + CH, pl.ds(r0, TF)] = slope.astype(BF16)

        def output(e):
            o = nn(wot[e * H : (e + 1) * H, :], hbuf[e * HE : e * HE + H, :])
            abuf[e * H : (e + 1) * H, :] = o + pk[e * H : (e + 1) * H, 1:2]

        product(0)
        product(1)
        yield
        for e in range(E):
            norm(e)
            if e + 2 < E:
                product(e + 2)
            output(e)
            yield

    def heads(i, side):
        abuf, hbuf = abufs[side], hbufs[side]
        r0 = pl.multiple_of(i * TF, TF)
        v0 = pl.multiple_of(mp * R + i * TF, 128)
        logits = logit_bufs[side][...]
        probs = []
        for t in range(2):
            part = logits[4 * t : 4 * t + 4]
            part = jnp.exp(part - jnp.max(part, axis=0, keepdims=True))
            part = part / jnp.sum(part, axis=0, keepdims=True)
            probs.append([part[k : k + 1] for k in range(4)])
        for at in range(0, H, CH):
            for t in range(2):
                mixed = None
                for k in range(4):
                    e = TASK_EXPERTS[t][k]
                    term = probs[t][k] * abuf[e * H + at : e * H + at + CH, :]
                    mixed = term if mixed is None else mixed + term
                mixb[t * H + at : t * H + at + CH, :] = mixed.astype(BF16)
        pres = [nn(w1t[t], mixb[t * H : (t + 1) * H, :]) for t in range(2)]
        yield
        slopes = []
        for t in range(2):
            half = pres[t] + wide(b1t[t * 128 : (t + 1) * 128, :], TF)
            p = 1.0 + jnp.tanh(half)
            u1 = half * p
            u1b[t * 128 : (t + 1) * 128, :] = u1.astype(BF16)
            slopes.append(p + u1 * (2.0 - p))
        pre = nn(w2f[...], u1b[...])
        yield
        half = pre + wide(b2tt[...], TF)
        p = 1.0 + jnp.tanh(half)
        u2 = half * p
        slope2 = p + u2 * (2.0 - p)
        wl = wide(wlt[...], TF)
        weighted = u2 * wl
        d_logits = []
        valid = v_ref[:, pl.ds(v0, TF)].astype(F32)
        for t in range(2):
            logit = jnp.sum(weighted[t * 64 : (t + 1) * 64], axis=0, keepdims=True) + bl_ref[t]
            pred = 0.5 + 0.5 * jnp.tanh(0.5 * logit)
            predbuf[t : t + 1, pl.ds(r0, TF)] = pred
            label = y_ref[t : t + 1, pl.ds(v0, TF)].astype(F32)
            d_logits.append(valid * (pred - label))
        d_logit = jnp.concatenate(
            [jnp.broadcast_to(d_logits[t], (64, TF)) for t in range(2)], axis=0
        )
        acc_last[...] += fold_lanes(u2 * d_logit)
        acc_lb[0:2] += fold_lanes(jnp.concatenate(d_logits, axis=0))
        d2 = (d_logit * 0.5) * (wl * slope2)
        acc_b2[...] += fold_lanes(d2)
        d2_low = d2.astype(BF16)
        d_u1 = nn(w2b[...], d2_low)
        acc_second[...] += nt(d2_low, u1b[...])
        yield
        for t in range(2):
            d1 = d_u1[t * 128 : (t + 1) * 128] * slopes[t]
            acc_b1[t * 128 : (t + 1) * 128] += fold_lanes(d1)
            d1_low = d1.astype(BF16)
            dmix[t * H : (t + 1) * H, :] = nn(w1n[t], d1_low)
            acc_first[t] += nt(mixb[t * H : (t + 1) * H, :], d1_low)
        yield
        dots = [[jnp.zeros((8, TF), F32) for _ in range(4)] for _ in range(2)]
        for at in range(0, H, CH):
            dm = [dmix[t * H + at : t * H + at + CH, :] for t in range(2)]
            grads = [None] * E
            for t in range(2):
                for k in range(4):
                    e = TASK_EXPERTS[t][k]
                    term = probs[t][k] * dm[t]
                    grads[e] = term if grads[e] is None else grads[e] + term
                    o = abuf[e * H + at : e * H + at + CH, :]
                    dots[t][k] = dots[t][k] + fold8(dm[t] * o)
            for e in range(E):
                dobuf[e * H + at : e * H + at + CH, pl.ds(r0, TF)] = grads[e].astype(BF16)
        rows = []
        for t in range(2):
            sums = [jnp.sum(dots[t][k], axis=0, keepdims=True) for k in range(4)]
            centre = sum(probs[t][k] * sums[k] for k in range(4))
            rows += [probs[t][k] * (sums[k] - centre) for k in range(4)]
        d_gate = jnp.concatenate(rows, axis=0)
        acc_dlog[...] += fold_lanes(d_gate)
        high = d_gate.astype(BF16).astype(F32)
        d_gate = jnp.concatenate([high, d_gate - high], axis=0).astype(BF16)
        dlogbuf[:, pl.ds(r0, TF)] = d_gate
        acc_gate[...] += nn(d_gate, xbuf[pl.ds(r0, TF), :])
        yield
        for e in range(E):
            at = pl.ds(e * HE, HE)
            acc_out[at, :] += nt(hbuf[at, :], dobuf[e * H : (e + 1) * H, pl.ds(r0, TF)])
        yield

    def together(*parts):
        parts = list(parts)
        while parts:
            for part in list(parts):
                if next(part, "end") == "end":
                    parts.remove(part)

    for copy in keep:
        copy.wait()
    n_f = R // TF
    together(forward(0, 0))

    def forward_pair(j, carry):
        together(forward(2 * j + 1, 1), heads(2 * j, 0))
        together(forward(2 * j + 2, 0), heads(2 * j + 1, 1))
        return carry

    lax.fori_loop(0, n_f // 2 - 1, forward_pair, 0)
    together(forward(n_f - 1, 1), heads(n_f - 2, 0))
    together(heads(n_f - 1, 1))

    pending = []
    pred_at = pl.ds(pl.multiple_of(mp * R, 128), R)
    pred_local = pltpu.make_async_copy(predbuf, pred_hbm.at[:, pred_at], sem_l.at[0])
    pred_local.start()
    pending.append(pred_local)
    pending.append(send(predbuf, pred_hbm.at[:, pred_at], sem_w.at[6], sem_w.at[7], (b, other)))

    flight = {}
    n_sems = 1 + 2 * sum(radix - 1 for _, radix, _, _ in plan)

    def source(c, rows, place_at):
        w = WIDTHS[c]
        at = sum(p[2] for p in plan[1:place_at])
        if c < E:
            return sbuf.at[pl.ds(c * H + at, rows), pl.ds(min(place_at, 1) * w, w)]
        if place_at:
            return sends_low.at[c - E, pl.ds(at, rows), :]
        return sends.at[c - E, pl.ds(0, rows), :]

    def level_sems(level):
        return 1 + 2 * sum(radix - 1 for _, radix, _, _ in plan[:level])

    def start_pair(c):
        src = source(c, H, 0)
        flight[c] = [send(src, mprecv[c], sem_s.at[c, 0], sem_r.at[c, 0], (b, other))]

    def start_level(c, level, value):
        stride, radix, rows, after = plan[level]
        out = source(c, rows, level)
        out[...] = value.astype(BF16)
        copies = []
        for step in range(1, radix):
            k = level_sems(level) + step - 1
            part = out
            if after != rows:
                to = lax.rem(digits[level] + step, radix)
                part = out.at[pl.ds(pl.multiple_of(to * after, 16), after), :]
            dst = lvrecv[c][level].at[step]
            copies.append(send(part, dst, sem_s.at[c, k], sem_r.at[c, k], peer(level, step)))
        flight[c] = copies
        if after != rows:
            mine = out[pl.ds(pl.multiple_of(digits[level] * after, 16), after), :]
        else:
            mine = out[...]
        lvrecv[c][level][0] = mine

    def finish_level(c, level):
        stride, radix, rows, after = plan[level]
        for copy in flight[c]:
            copy.wait()
        if after != rows:
            parts = [lvrecv[c][level][step].astype(F32) for step in range(radix)]
            return functools.reduce(lambda p, q: p + q, parts)
        total = None
        for k in range(radix):
            step = lax.rem(k - digits[level] + radix, radix)
            part = lvrecv[c][level][step].astype(F32)
            total = part if total is None else total + part
        return total

    def region(c, level):
        at = 0
        for k in range(level + 1):
            if plan[k][2] != plan[k][3]:
                at = at + digits[k] * plan[k][3]
        rows = plan[level][3] if level >= 0 else H
        if isinstance(at, int):
            return gout_hbm.at[c, pl.ds(at, rows), pl.ds(0, WIDTHS[c])]
        return gout_hbm.at[c, pl.ds(pl.multiple_of(at, 16), rows), pl.ds(0, WIDTHS[c])]

    split = [level for level in range(n_levels) if plan[level][2] != plan[level][3]]

    def start_result(c, value):
        rows = plan[-1][3]
        final = source(c, rows, n_levels)
        final[...] = value.astype(BF16)
        local = pltpu.make_async_copy(final, region(c, n_levels - 1), sem_l.at[1 + c])
        local.start()
        flight[c] = [local]
        if split:
            start_gather(c, split[-1], final)

    def start_gather(c, level, src):
        dst = region(c, level)
        for step in range(1, plan[level][1]):
            k = level_sems(level) + plan[level][1] - 1 + step - 1
            flight[c].append(send(src, dst, sem_s.at[c, k], sem_r.at[c, k], peer(level, step)))

    def chunk_steps(c):
        steps = []

        def from_pair():
            for copy in flight[c]:
                copy.wait()
            if c < E:
                value = hkeep[c % 2][...]
            elif c == TOWERS:
                value = source(c, H, 0)[...].astype(F32)
            else:
                value = half_out(c - TOWERS - 1, mp)
            start_level(c, 0, value + mprecv[c][...].astype(F32))

        steps.append(from_pair)
        for level in range(n_levels):

            def next_level(level=level):
                value = finish_level(c, level)
                if level + 1 < n_levels:
                    start_level(c, level + 1, value)
                else:
                    start_result(c, value)

            steps.append(next_level)
        for place_in in range(len(split) - 1, 0, -1):

            def gather(place_in=place_in):
                for copy in flight[c]:
                    copy.wait()
                flight[c] = []
                start_gather(c, split[place_in - 1], region(c, split[place_in] - 1))

            steps.append(gather)

        def finish():
            for copy in flight[c]:
                copy.wait()
            flight[c] = []

        steps.append(finish)
        return steps

    queue = []
    clock = [0]

    def start_steps(steps, spacing):
        queue.append([clock[0] + spacing, spacing, steps])

    def turn():
        clock[0] += 1
        for item in list(queue):
            if clock[0] >= item[0]:
                item[2].pop(0)()
                item[0] = clock[0] + item[1]
                if not item[2]:
                    queue.remove(item)

    def half_out(group, h):
        parts = []
        for e in range(3 * group, 3 * group + 3):
            a = acc_out[pl.ds(pl.multiple_of(e * HE + h * 128, 16), 128), :]
            parts.append(jnp.concatenate([a[:, 0:128], a[:, 128:256]], axis=0))
        return jnp.concatenate(parts, axis=1)

    def half_in(h):
        at = pl.ds(pl.multiple_of(h * 128, 128), 128)
        return jnp.concatenate([acc_in[0][at, :], acc_in[1][at, :]], axis=0)

    def pack_towers():
        src = source(TOWERS, H, 0)
        src[:, 0:128] = acc_first[0].astype(BF16)
        src[:, 128:256] = acc_first[1].astype(BF16)
        gates = acc_gate[0:8] + acc_gate[8:16]
        rest = [acc_second[0:64, 0:128], acc_second[64:128, 128:256]]
        rest += [gates[:, k * 128 : (k + 1) * 128] for k in range(4)]
        rest.append(jnp.zeros((H - 160, 128), F32))
        src[:, 256:384] = jnp.concatenate(rest, axis=0).astype(BF16)

    def launch(c, spacing=3):
        start_pair(c)
        start_steps(chunk_steps(c), spacing)

    pack_towers()
    launch(TOWERS)

    def launch_out(group):
        source(TOWERS + 1 + group, H, 0)[...] = half_out(group, other).astype(BF16)
        launch(TOWERS + 1 + group)

    s2row[...] = jnp.sum(
        (gate_low * (acc_gate[0:8] + acc_gate[8:16])), axis=0, keepdims=True
    )

    def backward_start(e, i):
        rows = slice(e * H, (e + 1) * H)
        for part in range(TB // SB):
            lanes = pl.ds(pl.multiple_of(i * TB + part * SB, SB), SB)
            dmix[part * H : (part + 1) * H, :] = nn(wot[rows, :], dobuf[rows, lanes])

    def backward_part(e, r0, part):
        at0 = e * H
        lanes = pl.ds(r0, SB)
        work = dmix.at[part * H : (part + 1) * H]
        r = rbuf[e : e + 1, lanes]
        m1 = jnp.zeros((8, SB), F32)
        m2 = jnp.zeros((8, SB), F32)
        for u in range(0, H, CH):
            at = at0 + u
            zhat = zbuf[at : at + CH, lanes].astype(F32)
            dzg = work[u : u + CH, :] * sbuf[at : at + CH, lanes].astype(F32)
            q = dzg * zhat
            acc_u[0][u : u + CH, :] += fold_lanes(dzg)
            acc_u[1][u : u + CH, :] += fold_lanes(q)
            work[u : u + CH, :] = dzg
            m1 = m1 + fold8(dzg)
            m2 = m2 + fold8(q)
        m1 = jnp.sum(m1, axis=0, keepdims=True) * (1.0 / H)
        m2 = jnp.sum(m2, axis=0, keepdims=True) * (1.0 / H)
        for u in range(0, H, CH):
            at = at0 + u
            zhat = zbuf[at : at + CH, lanes].astype(F32)
            da = r * (work[u : u + CH, :] - m1 - zhat * m2)
            acc_u[2][u : u + CH, :] += fold_lanes(da)
            zbuf[at : at + CH, lanes] = da.astype(BF16)

    n_b = R // TB

    def weight_part(e, i):
        r0 = pl.multiple_of(i * TB, TB)
        rows = slice(e * H, (e + 1) * H)
        grad = nn(zbuf[rows, pl.ds(r0, TB)], xbuf[pl.ds(r0, TB), :])
        acc_in[0][...] += grad[:, 0:256]
        acc_in[1][...] += grad[:, 256:512]

    def backward_tile(e, i):
        for part in range(TB // SB):
            backward_part(e, pl.multiple_of(i * TB + part * SB, SB), part)

    def clear_units():
        for part in acc_u:
            part[...] = jnp.zeros((H, 128), F32)

    def clear_weights():
        for part in acc_in:
            part[...] = jnp.zeros((H, 256), F32)

    def finish_units(e):
        rows = slice(e * H, (e + 1) * H)
        for k in range(3):
            part = acc_u[2 - k][...]
            sums = lane_sums(part / pk[rows, 2:3] if k else part)
            v_mp[mp, k * 12 + 2 * e : k * 12 + 2 * e + 1, :] = sums[:, 0:128]
            v_mp[mp, k * 12 + 2 * e + 1 : k * 12 + 2 * e + 2, :] = sums[:, 128:256]
        bo = acc_out[e * HE + H : e * HE + H + 1, :]
        v_mp[mp, 36 + 2 * e : 37 + 2 * e, :] = bo[:, 0:128]
        v_mp[mp, 37 + 2 * e : 38 + 2 * e, :] = bo[:, 128:256]
        clear_units()

    def finish_expert(e):
        hkeep[e % 2][...] = half_in(mp)
        source(e, H, 0)[...] = half_in(other).astype(BF16)
        launch(e, 2 if e >= E - 2 else 3)
        cross = jnp.zeros((8, D), F32)
        for u in range(0, H, CH):
            w = wf[e * H + u : e * H + u + CH, :].astype(F32)
            grad = jnp.concatenate([acc_in[0][u : u + CH, :], acc_in[1][u : u + CH, :]], axis=1)
            cross = cross + fold8(w * grad)
        s2row[...] += jnp.sum(cross, axis=0, keepdims=True)
        clear_weights()

    clear_weights()
    clear_units()
    for e in range(E):
        rows = slice(e * H, (e + 1) * H)
        wot[rows, :] = (wot[rows, :].T.astype(F32) * 0.5).astype(BF16)
    for e in range(E):

        def backward_step(i, carry, e=e):
            backward_start(e, i)
            weight_part(e, i - 1)
            backward_tile(e, i)
            return carry

        backward_start(e, 0)
        if e:
            weight_part(e - 1, n_b - 1)
        backward_tile(e, 0)
        if e:
            finish_expert(e - 1)
        if e == 2:
            back = []
            for k in range(2 * E):
                half, to = k % 2, 2048 + k * 128
                copy = pltpu.make_async_copy(
                    wb_hbm.at[half, :, (k // 2) * 128 : (k // 2 + 1) * 128],
                    sbuf.at[0:D, to : to + 128],
                    sem_f.at[k],
                )
                copy.start()
                back.append(copy)
        turn()
        if e == 0:
            launch_out(0)
        for k in range(3):
            first, last = 1 + k * (n_b - 1) // 3, 1 + (k + 1) * (n_b - 1) // 3
            lax.fori_loop(first, last, backward_step, 0)
            turn()
            if e == 0 and k == 1:
                launch_out(1)
        finish_units(e)
    weight_part(E - 1, n_b - 1)
    finish_expert(E - 1)
    for copy in back:
        copy.wait()
    wb = sbuf.at[0:D, 2048 : 2048 + E * H]

    for k in range(4):
        v_mp[mp, 48 + k : 49 + k, :] = s2row[:, k * 128 : (k + 1) * 128]
    v_mp[mp, 52:60, :] = acc_dlog[...]
    v_mp[mp, 60:61, :] = lane_sums(acc_last[...])
    v_mp[mp, 61:63, :] = acc_lb[0:2]
    b1_sums = lane_sums(acc_b1[...])
    v_mp[mp, 63:64, :] = b1_sums[:, 0:128]
    v_mp[mp, 64:65, :] = b1_sums[:, 128:256]
    v_mp[mp, 65:66, :] = lane_sums(acc_b2[...])
    v_mp[mp, 66:VR, :] = jnp.zeros((VR - 66, 128), F32)
    flight["v"] = [send(v_mp.at[mp], v_mp.at[mp], sem_v.at[0], sem_v.at[1], (b, other))]

    def small_level(level, total):
        own = digits[level]
        v_lv[level, own] = total
        flight["v"] = []
        for step in range(1, plan[level][1]):
            base = 2 + (level * 3 + step - 1) * 2
            flight["v"].append(
                send(
                    v_lv.at[level, own], v_lv.at[level, own],
                    sem_v.at[base], sem_v.at[base + 1], peer(level, step),
                )
            )

    def small_steps():
        steps = []

        def first():
            for copy in flight["v"]:
                copy.wait()
            small_level(0, v_mp[0] + v_mp[1])

        steps.append(first)
        for level in range(n_levels):

            def step(level=level):
                for copy in flight["v"]:
                    copy.wait()
                total = v_lv[level, 0]
                for k in range(1, plan[level][1]):
                    total = total + v_lv[level, k]
                if level + 1 < n_levels:
                    small_level(level + 1, total)
                    return
                vout_ref[...] = total
                row = jnp.concatenate([total[k : k + 1] for k in range(2 * E)], axis=1)
                row_high = row.astype(BF16).astype(F32)
                rows = jnp.concatenate(
                    [row_high, row - row_high, jnp.zeros((14, E * H), F32)], axis=0
                ).astype(BF16)
                s1 = nn(rows, wf[0 : E * H, :])
                gate_sum = jnp.sum(total[52:60], axis=1, keepdims=True)
                gate_part = jnp.sum(gate_low * gate_sum, axis=0, keepdims=True)
                stat_ref[3:4, :] = s1[0:1] + s1[1:2] + gate_part
                stat_ref[4:5, :] = jnp.concatenate([total[48 + k : 49 + k] for k in range(4)], axis=1)

            steps.append(step)
        return steps

    start_steps(small_steps(), 2)
    turn()

    def input_gradient(i):
        lanes = pl.ds(i * TB, TB)
        da = zbuf[:, lanes]
        dl = dlogbuf[:, lanes]
        for k, half in ((0, mp), (1, other)):
            at = pl.ds(pl.multiple_of(half * 256, 256), 256)
            grad = nn(wb[at, :], da) + nn(gback[at, 0:16], dl)
            dobuf[k * H : (k + 1) * H, lanes] = grad.astype(BF16)

    n_c = R // TB
    for part in range(4):
        for k in range(part * n_c // 4, (part + 1) * n_c // 4):
            input_gradient(k)
            turn()
        w = R // 4
        at = pl.ds(part * w, w)
        to = pl.ds(pl.multiple_of(mp * R + part * w, 128), w)
        local = pltpu.make_async_copy(dobuf.at[0:H, at], d_hbm.at[:, to], sem_l.at[1 + NC + part])
        local.start()
        pending.append(local)
        pending.append(
            send(dobuf.at[H : 2 * H, at], d_hbm.at[:, to], sem_d.at[part], sem_d.at[4 + part], (b, other))
        )
    while queue:
        turn()
    for copy in pending:
        copy.wait()


def final_kernel(
    tile, dt_hbm, x_hbm, v_ref, pred_ref, gout_ref, vout_ref, stat_ref,
    o_pred, feat_hbm, o_in, o_inb, o_gain, o_nb, o_out, o_outb, o_gate, o_gateb,
    o_w1, o_b1, o_w2, o_b2, o_wl, o_bl,
    dtb, xb, fb, sem_d, sem_x, sem_o,
):
    mp = lax.axis_index("mp")
    rows = xb.shape[0]
    half = pl.ds(pl.multiple_of(mp * 256, 256), 256)
    loads = []
    for k in range(rows // tile):
        at = pl.ds(k * tile, tile)
        copies = (
            pltpu.make_async_copy(dt_hbm.at[:, at], dtb.at[:, at], sem_d.at[k]),
            pltpu.make_async_copy(x_hbm.at[at, half], xb.at[at, :], sem_x.at[k]),
        )
        for copy in copies:
            copy.start()
        loads.append(copies)

    scale = 1.0 / stat_ref[2:3, 0:128]
    one = scale[:, 0:1]
    o_pred[...] = pred_ref[...]
    for e in range(E):
        for k in range(4):
            g = gout_ref[e, (k // 2) * 128 : (k // 2 + 1) * 128, (k % 2) * 128 : (k % 2 + 1) * 128]
            o_in[e, k * 128 : (k + 1) * 128, :] = (g.astype(F32) * one).T
        for k in range(2):
            g = gout_ref[TOWERS + 1 + e // 3, k * 128 : (k + 1) * 128, (e % 3) * 128 : (e % 3 + 1) * 128]
            o_out[e, :, k * 128 : (k + 1) * 128] = g.astype(F32) * one
        for ref, base in ((o_inb, 0), (o_gain, 12), (o_nb, 24)):
            ref[e : e + 1, :] = vout_ref[pl.ds(base + 2 * e + mp, 1), :] * scale
        for k in range(2):
            o_outb[e : e + 1, k * 128 : (k + 1) * 128] = (
                vout_ref[36 + 2 * e + k : 37 + 2 * e + k, :] * scale
            )
    o_w1[0] = gout_ref[TOWERS, :, 0:128].astype(F32) * one
    o_w1[1] = gout_ref[TOWERS, :, 128:256].astype(F32) * one
    g = gout_ref[TOWERS, 0:160, 256:384].astype(F32) * one
    o_w2[0] = g[0:64]
    o_w2[1] = g[64:128]
    for k in range(4):
        part = g[128 + 8 * k : 136 + 8 * k]
        o_gate[0, :, k * 128 : (k + 1) * 128] = part[0:4]
        o_gate[1, :, k * 128 : (k + 1) * 128] = part[4:8]
    gate_bias = jnp.sum(vout_ref[52:60, :], axis=1, keepdims=True) * scale
    table = jnp.concatenate([gate_bias, jnp.zeros((120, 128), F32)], axis=0).T
    o_gateb[0:1, :] = table[0:1, 0:4]
    o_gateb[1:2, :] = table[0:1, 4:8]
    last = vout_ref[60:61, :] * scale
    o_wl[0:1, :] = last[:, 0:64]
    o_wl[1:2, :] = last[:, 64:128]
    for t in range(2):
        o_bl[t] = jnp.sum(vout_ref[61 + t : 62 + t, :] * scale)
    o_b1[...] = vout_ref[63:65, :] * scale
    b2 = vout_ref[65:66, :] * scale
    o_b2[0:1, :] = b2[:, 0:64]
    o_b2[1:2, :] = b2[:, 64:128]

    count = stat_ref[2:3, half]
    inv = stat_ref[1:2, half]
    slope = inv * inv * (stat_ref[4:5, half] / count)
    shift = inv * (stat_ref[3:4, half] / count) - stat_ref[0:1, half] * slope
    eye = jnp.where(
        lax.broadcasted_iota(jnp.int32, (256, 256), 0) == lax.broadcasted_iota(jnp.int32, (256, 256), 1), 1.0, 0.0
    ).astype(BF16)
    stores = []
    for k in range(rows // tile):
        for copy in loads[k]:
            copy.wait()

        def block(i, carry, k=k):
            at = pl.ds(pl.multiple_of(k * tile + i * 256, 256), 256)
            grad = nt(eye, dtb[:, at])
            valid = nt(eye, jnp.broadcast_to(v_ref[:, at].astype(F32), (128, 256)).astype(BF16))
            for c in range(2):
                cols = slice(c * 128, (c + 1) * 128)
                term = valid * (shift[:, cols] + xb[at, cols].astype(F32) * slope[:, cols])
                fb[at, cols] = inv[:, cols] * grad[:, cols] - term
            return carry

        lax.fori_loop(0, tile // 256, block, 0, unroll=True)
        at = pl.ds(k * tile, tile)
        copy = pltpu.make_async_copy(fb.at[at, :], feat_hbm.at[at, :], sem_o.at[k])
        copy.start()
        stores.append(copy)
    for copy in stores:
        copy.wait()


def on_device(
    features, validity, labels, expert_in, expert_in_bias, norm_gain, norm_bias, expert_out,
    expert_out_bias, gate_weight, gate_bias, tower_first, tower_first_bias, tower_second,
    tower_second_bias, tower_last, tower_last_bias,
):
    rows = features.shape[0]
    R = rows // 2
    n_batch = lax.axis_size("batch")
    plan = plan_of(n_batch)
    n_levels = len(plan)
    n_peers = sum(radix - 1 for _, radix, _, _ in plan)
    n_sems = 1 + 2 * n_peers
    v_row = validity.reshape(1, rows)
    y_rows = labels.T
    vm = pl.BlockSpec(memory_space=pltpu.VMEM)
    sm = pl.BlockSpec(memory_space=pltpu.SMEM)
    hb = pl.BlockSpec(memory_space=pl.ANY)
    dma = pltpu.SemaphoreType.DMA

    def scr(*shape, dtype=F32):
        return pltpu.VMEM(shape, dtype)

    low_rows = sum(p[2] for p in plan[1:]) + plan[-1][3]
    scratch = [
        scr(R, D, dtype=BF16), scr(E * H, R, dtype=BF16), scr(E * H, R, dtype=BF16),
        scr(E * H, R, dtype=BF16), scr(8, R), scr(16, R, dtype=BF16), scr(2, R),
        scr(E * H + 32, D, dtype=BF16), scr(D, 128, dtype=BF16),
        scr(E * H, H, dtype=BF16), scr(E * H, 128), scr(E * H, 128), scr(E * H, 128),
        scr(2, 128, H, dtype=BF16), scr(2, H, 128, dtype=BF16), scr(128, H, dtype=BF16),
        scr(H, 128, dtype=BF16), scr(H, 128), scr(128, 128), scr(128, 128), scr(8, 128),
        [scr(E * H, TF)] * 2, [scr(E * HE, TF, dtype=BF16)] * 2, [scr(8, TF)] * 2,
        scr(2 * H, TF, dtype=BF16), scr(H, TF, dtype=BF16), scr(2 * H, TF),
        scr(E * HE, H), scr(16, D), scr(2, H, 128), scr(128, H),
        scr(8, 128), scr(8, 128), scr(128, 128), scr(128, 128), scr(H, 128), scr(1, D),
        scr(24, 128), scr(24, 128),
        scr(2, 8, D), scr(n_levels, 4, 8, D), scr(2, VR, 128), scr(n_levels, 4, VR, 128),
        scr(3, H, 384, dtype=BF16), scr(3, low_rows, 384, dtype=BF16),
        [scr(H, w, dtype=BF16) for w in WIDTHS],
        [[scr(radix, after, w, dtype=BF16) for _, radix, _, after in plan] for w in WIDTHS],
        dma((8,)), dma((8,)), dma((2 + 6 * n_levels,)), dma((2 + 6 * n_levels,)),
        dma((NC, n_sems)), dma((NC, n_sems)), dma((5 + NC,)), dma((8,)), dma((3 * E,)),
    ]
    flops = 2 * R * (6 * D * E * H // 2 + 3 * E * H * H)
    d_half, preds, gsum, vsum, stats, _ = pl.pallas_call(
        functools.partial(main_kernel, plan, R),
        out_shape=(
            jax.ShapeDtypeStruct((256, rows), BF16),
            jax.ShapeDtypeStruct((2, rows), F32),
            jax.ShapeDtypeStruct((NC, H, 384), BF16),
            jax.ShapeDtypeStruct((VR, 128), F32),
            jax.ShapeDtypeStruct((8, D), F32),
            jax.ShapeDtypeStruct((2, D, E * 128), BF16),
        ),
        in_specs=[hb] + [vm] * 2 + [hb] * 2 + [vm] * 5 + [sm] + [vm] * 5 + [sm],
        out_specs=(hb, hb, hb, vm, vm, hb),
        scratch_shapes=scratch,
        compiler_params=pltpu.CompilerParams(
            collective_id=0, has_side_effects=True, vmem_limit_bytes=64 * 2**20 - 65536
        ),
        cost_estimate=pl.CostEstimate(flops=flops, bytes_accessed=20 * 2**20, transcendentals=0),
        name="layer",
    )(
        features, v_row, y_rows, expert_in, expert_out, expert_in_bias, norm_gain, norm_bias,
        expert_out_bias, jnp.swapaxes(gate_weight, 1, 2), gate_bias, tower_first, tower_first_bias,
        jnp.swapaxes(tower_second, 1, 2), tower_second_bias, tower_last, tower_last_bias,
    )

    tile = 1024
    n_tiles = rows // tile
    out_shapes = [
        (2, rows), (rows, 256), (E, D, 128), (E, 128), (E, 128), (E, 128), (E, 128, H), (E, H),
        (2, 4, D), (2, 4), (2, H, 128), (2, 128), (2, 64, 128), (2, 64), (2, 64), (2,),
    ]
    outs = pl.pallas_call(
        functools.partial(final_kernel, tile),
        out_shape=[jax.ShapeDtypeStruct(shape, F32) for shape in out_shapes],
        in_specs=[hb, hb] + [vm] * 5,
        out_specs=[vm, hb] + [vm] * 13 + [sm],
        scratch_shapes=[
            scr(256, rows, dtype=BF16), scr(rows, 256, dtype=BF16), scr(rows, 256),
            dma((n_tiles,)), dma((n_tiles,)), dma((n_tiles,)),
        ],
        compiler_params=pltpu.CompilerParams(vmem_limit_bytes=64 * 2**20 - 65536),
        cost_estimate=pl.CostEstimate(
            flops=rows * 256 * 8, bytes_accessed=rows * 256 * 8, transcendentals=0
        ),
        name="finish",
    )(d_half, features, v_row, preds, gsum, vsum, stats)
    outs = list(outs)
    outs[0] = outs[0].T
    outs[8] = jnp.swapaxes(outs[8], 1, 2)
    outs[12] = jnp.swapaxes(outs[12], 1, 2)
    return tuple(outs)


def solution(mesh):
    in_specs = (
        P("batch", None), P("batch"), P("batch", None), P(None, None, "mp"), P(None, "mp"),
        P(None, "mp"), P(None, "mp"), P(None, "mp", None), P(), P(), P(), P(), P(), P(), P(), P(), P(),
    )
    out_specs = (
        P("batch", None), P("batch", "mp"), P(None, None, "mp"), P(None, "mp"), P(None, "mp"),
        P(None, "mp"), P(None, "mp", None), P(), P(), P(), P(), P(), P(), P(), P(), P(),
    )
    return jax.shard_map(
        on_device, mesh=mesh, in_specs=in_specs, out_specs=out_specs, check_vma=False
    )
```

```python
import functools

import jax
import jax.numpy as jnp
from jax import lax
from jax.experimental import pallas as pl
from jax.experimental.pallas import tpu as pltpu
from jax.sharding import PartitionSpec as P

MESH = pl.DeviceIdType.MESH
F32 = jnp.float32
BF16 = jnp.bfloat16
EPS = 1e-05
TASK_EXPERTS = ((0, 1, 4, 5), (2, 3, 4, 5))
E = 6
H = 256
D = 512
TF = 256
TB = 512
SB = 256
CH = 32
VR = 72
HE = H + 16
WIDTHS = (256,) * E + (384,) * 3
NC = len(WIDTHS)
TOWERS = E


def levels_of(count):
    levels, stride = [], 1
    while stride < count:
        radix = 4 if (count // stride) % 4 == 0 else count // stride
        levels.append((stride, radix))
        stride *= radix
    return levels


def plan_of(count):
    plan, rows = [], H
    for stride, radix in levels_of(count):
        split = rows % radix == 0 and (rows // radix) % 16 == 0
        plan.append((stride, radix, rows, rows // radix if split else rows))
        rows = plan[-1][3]
    return plan


def nn(a, b):
    return lax.dot_general(a, b, (((1,), (0,)), ((), ())), preferred_element_type=F32)


def nt(a, b):
    return lax.dot_general(a, b, (((1,), (1,)), ((), ())), preferred_element_type=F32)


def column(row):
    return jnp.broadcast_to(row, (128, 128)).T


def wide(table, width):
    return jnp.concatenate([table] * (width // 128), axis=1)


def fold8(value):
    total = value[0:8]
    for start in range(8, value.shape[0], 8):
        total = total + value[start : start + 8]
    return total


def fold_lanes(value):
    total = value[:, 0:128]
    for start in range(128, value.shape[1], 128):
        total = total + value[:, start : start + 128]
    return total


def lane_sums(partial):
    rows = [
        jnp.sum(partial[at : at + 128].T, axis=0, keepdims=True)
        for at in range(0, partial.shape[0], 128)
    ]
    return jnp.concatenate(rows, axis=1)


def merge_stats(items):
    count = items[0][2:3]
    total = items[0][0:1]
    for item in items[1:]:
        count = count + item[2:3]
        total = total + item[0:1]
    mean = total / jnp.maximum(count, 1.0)
    square = jnp.zeros_like(total)
    for item in items:
        shift = item[0:1] / jnp.maximum(item[2:3], 1.0) - mean
        square = square + item[1:2] + item[2:3] * shift * shift
    return total, square, count


def main_kernel(
    plan, rows_core,
    x_hbm, v_ref, y_ref, win_hbm, wout_hbm, bin_ref, gain_ref, nb_ref, bout_ref, gate_ref, gb_ref,
    w1_ref, b1_ref, w2_ref, b2_ref, wl_ref, bl_ref,
    d_hbm, pred_hbm, gout_hbm, vout_ref, stat_ref, wb_hbm,
    xbuf, zbuf, sbuf, dobuf, rbuf, dlogbuf, predbuf,
    wf, gback, wot, pk, g2t, b2t,
    w1t, w1n, w2f, w2b, b1t, b2tt, wlt, gbt,
    abufs, hbufs, logit_bufs, mixb, u1b, dmix,
    acc_out, acc_gate, acc_first, acc_second,
    acc_dlog, acc_lb, acc_last, acc_b2, acc_b1, s2row,
    bias_snd, bias_rcv,
    st_near, st_lv, v_mp, v_lv, sends, sends_low, mprecv, lvrecv,
    sem_x, sem_w, sem_st, sem_v, sem_s, sem_r, sem_l, sem_d, sem_f,
):
    R = rows_core
    abuf = abufs[0]
    acc_in = (abuf.at[0:H, :], abuf.at[H : 2 * H, :])
    hkeep = (abuf.at[2 * H : 3 * H, :], abuf.at[3 * H : 4 * H, :])
    acc_u = (
        abuf.at[4 * H : 5 * H, 0:128], abuf.at[4 * H : 5 * H, 128:256], abuf.at[5 * H : 6 * H, 0:128]
    )
    n_levels = len(plan)
    b = lax.axis_index("batch")
    mp = lax.axis_index("mp")
    other = 1 - mp
    digits = [lax.rem(lax.div(b, stride), radix) for stride, radix, _, _ in plan]

    def peer(level, step):
        stride, radix = plan[level][:2]
        to = lax.rem(digits[level] + step, radix)
        return (b + (to - digits[level]) * stride, mp)

    def send(src, dst, ssem, rsem, to):
        copy = pltpu.make_async_remote_copy(
            src_ref=src, dst_ref=dst, send_sem=ssem, recv_sem=rsem,
            device_id=to, device_id_type=MESH,
        )
        copy.start()
        return copy

    n_x = 8
    xr = R // n_x
    x_copies = []
    for k in range(n_x):
        copy = pltpu.make_async_copy(
            x_hbm.at[pl.ds(pl.multiple_of(mp * R + k * xr, 16), xr), :],
            xbuf.at[pl.ds(k * xr, xr), :],
            sem_x.at[k],
        )
        copy.start()
        x_copies.append(copy)

    f_copies = []
    for e in range(E):
        for k in range(2):
            f_copies.append(
                pltpu.make_async_copy(
                    win_hbm.at[e, k * H : (k + 1) * H, :],
                    abuf.at[e * H : (e + 1) * H, k * 128 : (k + 1) * 128],
                    sem_f.at[2 * e + k],
                )
            )
        f_copies.append(
            pltpu.make_async_copy(
                wout_hbm.at[e], acc_out.at[e * 128 : (e + 1) * 128, :], sem_f.at[2 * E + e]
            )
        )
    for copy in f_copies:
        copy.start()

    barrier = pltpu.get_barrier_semaphore()
    near = [(step, m) for step in range(plan[0][1]) for m in range(2) if step or m]

    def near_peer(step, m):
        return (peer(0, step)[0], other if m else mp)

    greets = [near_peer(step, m) for step, m in near]
    for level in range(1, n_levels):
        greets += [peer(level, step) for step in range(1, plan[level][1])]
    for to in greets:
        pl.semaphore_signal(barrier, inc=1, device_id=to, device_id_type=MESH)

    v_row = v_ref[:, pl.ds(pl.multiple_of(mp * R, 128), R)].astype(F32)
    count = jnp.sum(v_row, axis=1, keepdims=True)
    total = jnp.zeros((16, D), F32)
    for k in range(n_x):
        x_copies[k].wait()
        v16 = jnp.broadcast_to(v_row[:, k * xr : (k + 1) * xr], (16, xr)).astype(BF16)
        total = total + nn(v16, xbuf[pl.ds(k * xr, xr), :])
    mean = total[0:1] / jnp.maximum(count, 1.0)

    def square_step(k, total):
        for part in range(2):
            r0 = pl.multiple_of(k * 512 + part * 256, 256)
            off = xbuf[pl.ds(r0, 256), :].astype(F32) - mean
            v16 = v_ref[:, pl.ds(pl.multiple_of(mp * R + r0, 128), 256)]
            v16 = jnp.broadcast_to(v16.astype(F32), (16, 256)).astype(BF16)
            total = total + nn(v16, (off * off).astype(BF16))
        return total

    square = lax.fori_loop(0, R // 512, square_step, jnp.zeros((16, D), F32))
    pl.semaphore_wait(barrier, len(greets))
    me = digits[0] * 2 + mp
    st_near[me] = jnp.concatenate(
        [total[0:1], square[0:1], jnp.broadcast_to(count, (1, D)), jnp.zeros((5, D), F32)], axis=0
    )
    st_copies = [
        send(st_near.at[me], st_near.at[me], sem_st.at[2 * k], sem_st.at[2 * k + 1], near_peer(*near[k]))
        for k in range(len(near))
    ]

    win_snd = dobuf.at[0:D, 0 : E * 128]
    win_rcv = dobuf.at[0:D, 1024 : 1024 + E * 128]
    wout_snd = dobuf.at[D : D + 128, 0 : E * H]
    wout_rcv = dobuf.at[D : D + 128, 2048 : 2048 + E * H]
    for copy in f_copies:
        copy.wait()
    for e in range(E):
        for k in range(2):
            win_snd[k * H : (k + 1) * H, e * 128 : (e + 1) * 128] = abuf[
                e * H : (e + 1) * H, k * 128 : (k + 1) * 128
            ].astype(BF16)
        wout_snd[:, e * H : (e + 1) * H] = acc_out[e * 128 : (e + 1) * 128, :].astype(BF16)
    bias_snd[0:E] = bin_ref[...]
    bias_snd[8 : 8 + E] = gain_ref[...]
    bias_snd[16 : 16 + E] = nb_ref[...]
    w_copies = [
        send(win_snd, win_rcv, sem_w.at[0], sem_w.at[1], (b, other)),
        send(wout_snd, wout_rcv, sem_w.at[2], sem_w.at[3], (b, other)),
        send(bias_snd, bias_rcv, sem_w.at[4], sem_w.at[5], (b, other)),
    ]

    for t in range(2):
        w1n[t] = w1_ref[t].astype(BF16)
        w1t[t] = (w1_ref[t].T * 0.5).astype(BF16)
        b1t[t * 128 : (t + 1) * 128] = column(b1_ref[t : t + 1, :]) * 0.5
    zero64 = jnp.zeros((64, 128), F32)
    zero128 = jnp.zeros((128, 64), F32)
    w2f[0:64] = (jnp.concatenate([w2_ref[0], zero64], axis=1) * 0.5).astype(BF16)
    w2f[64:128] = (jnp.concatenate([zero64, w2_ref[1]], axis=1) * 0.5).astype(BF16)
    w2b[0:128] = (jnp.concatenate([w2_ref[0].T, zero128], axis=1) * 0.5).astype(BF16)
    w2b[128:256] = (jnp.concatenate([zero128, w2_ref[1].T], axis=1) * 0.5).astype(BF16)
    b2tt[...] = column(jnp.concatenate([b2_ref[0:1, :], b2_ref[1:2, :]], axis=1)) * 0.5
    wlt[...] = column(jnp.concatenate([wl_ref[0:1, :], wl_ref[1:2, :]], axis=1))
    gbt[...] = jnp.concatenate(
        [jnp.full((1, 128), gb_ref[t, k], F32) for t in range(2) for k in range(4)], axis=0
    )
    gate = jnp.concatenate([gate_ref[0], gate_ref[1]], axis=0)
    gate_low = gate.astype(BF16).astype(F32)
    gback[...] = jnp.concatenate([gate_low, gate_low, jnp.zeros((112, D), F32)], axis=0).T.astype(BF16)
    acc_gate[...] = jnp.zeros_like(acc_gate)
    acc_out[...] = jnp.zeros_like(acc_out)
    for hbuf in hbufs:
        for e in range(E):
            hbuf[e * HE + H : (e + 1) * HE, :] = jnp.ones((16, TF), BF16)
    acc_first[...] = jnp.zeros_like(acc_first)
    acc_second[...] = jnp.zeros_like(acc_second)
    acc_dlog[...] = jnp.zeros_like(acc_dlog)
    acc_lb[...] = jnp.zeros_like(acc_lb)
    acc_last[...] = jnp.zeros_like(acc_last)
    acc_b1[...] = jnp.zeros_like(acc_b1)
    acc_b2[...] = jnp.zeros_like(acc_b2)

    lane = lax.broadcasted_iota(jnp.int32, (128, 128), 1)

    def place(half, win, wout, bias):
        for e in range(E):
            at = pl.multiple_of(e * H + half * 128, 128)
            w = win[:, e * 128 : (e + 1) * 128]
            wf[pl.ds(at, 128), :] = w.T
            o = wout[:, e * H : (e + 1) * H]
            wot[pl.ds(e * H, H), pl.ds(pl.multiple_of(half * 128, 128), 128)] = o.T
            gain = column(bias[8 + e : 9 + e, :])
            pk[pl.ds(at, 128), :] = jnp.where(lane == 0, column(bias[e : e + 1, :]), gain)
            g2t[pl.ds(at, 128), :] = gain * 0.5
            b2t[pl.ds(at, 128), :] = column(bias[16 + e : 17 + e, :]) * 0.5

    place(mp, win_snd, wout_snd, bias_snd)
    for copy in st_copies:
        copy.wait()
    total, square, count = merge_stats([st_near[k] for k in range(2 * plan[0][1])])
    for level in range(1, n_levels):
        own = digits[level]
        st_lv[level, own] = jnp.concatenate([total, square, count, jnp.zeros((5, D), F32)], axis=0)
        copies = []
        for step in range(1, plan[level][1]):
            base = 2 * (len(near) + level * 3 + step - 1)
            copies.append(
                send(
                    st_lv.at[level, own], st_lv.at[level, own],
                    sem_st.at[base], sem_st.at[base + 1], peer(level, step),
                )
            )
        if level == 1:
            for copy in w_copies:
                copy.wait()
            place(other, win_rcv, wout_rcv, bias_rcv)
            keep = [
                pltpu.make_async_copy(win_snd, wb_hbm.at[mp], sem_f.at[0]),
                pltpu.make_async_copy(win_rcv, wb_hbm.at[other], sem_f.at[1]),
            ]
            for copy in keep:
                copy.start()
            means = []
            for e in range(E):
                w = wf[e * H : (e + 1) * H, :].astype(F32)
                means.append(jnp.sum(w, axis=0, keepdims=True) * (1.0 / H))
                shift = jnp.sum(pk[e * H : (e + 1) * H, 0:1], axis=0, keepdims=True) * (1.0 / H)
                for k in range(2):
                    at = slice(e * H + k * 128, e * H + (k + 1) * 128)
                    table = pk[at, :]
                    table = jnp.where(lane == 0, table - shift, table)
                    second = column(bout_ref[e : e + 1, k * 128 : (k + 1) * 128])
                    pk[at, :] = jnp.where(lane == 1, second, table)
            pad = [jnp.zeros((2, D), F32)]
            means = jnp.concatenate(means + pad, axis=0)
            means_high = means.astype(BF16).astype(F32)
            wf[E * H : E * H + 32, :] = jnp.concatenate(
                [gate_low, means_high, means - means_high, jnp.zeros((8, D), F32)], axis=0
            ).astype(BF16)
        for copy in copies:
            copy.wait()
        total, square, count = merge_stats([st_lv[level, k] for k in range(plan[level][1])])
    mu = total / count
    inv = lax.rsqrt(square / count + EPS)
    stat_ref[...] = jnp.concatenate([mu, inv, count, jnp.zeros((5, D), F32)], axis=0)

    def forward(i, side):
        abuf, hbuf = abufs[side], hbufs[side]
        r0 = pl.multiple_of(i * TF, TF)
        x_tile = xbuf[pl.ds(r0, TF), :].astype(F32)
        xn = ((x_tile - stat_ref[0:1, :]) * stat_ref[1:2, :]).astype(BF16)
        xbuf[pl.ds(r0, TF), :] = xn
        ext = nt(wf[E * H : E * H + 32, :], xn)
        logit_bufs[side][...] = ext[0:8] + wide(gbt[...], TF)
        means = ext[8:16] + ext[16:24]

        def product(e):
            abuf[e * H : (e + 1) * H, :] = nt(wf[e * H : (e + 1) * H, :], xn)

        def norm(e):
            squares = jnp.zeros((8, TF), F32)
            for at in range(e * H, (e + 1) * H, CH):
                c = (abuf[at : at + CH, :] - means[e : e + 1]) + pk[at : at + CH, 0:1]
                abuf[at : at + CH, :] = c
                squares = squares + fold8(c * c)
            r = lax.rsqrt(jnp.sum(squares, axis=0, keepdims=True) * (1.0 / H) + EPS)
            rbuf[e : e + 1, pl.ds(r0, TF)] = r
            for u in range(0, H, CH):
                at = e * H + u
                zhat = abuf[at : at + CH, :] * r
                zbuf[at : at + CH, pl.ds(r0, TF)] = zhat.astype(BF16)
                half = zhat * wide(g2t[at : at + CH, :], TF) + wide(b2t[at : at + CH, :], TF)
                p = 1.0 + jnp.tanh(half)
                h = half * p
                hbuf[e * HE + u : e * HE + u + CH, :] = h.astype(BF16)
                slope = (p + h * (2.0 - p)) * pk[at : at + CH, 2:3]
                sbuf[at : at + CH, pl.ds(r0, TF)] = slope.astype(BF16)

        def output(e):
            o = nn(wot[e * H : (e + 1) * H, :], hbuf[e * HE : e * HE + H, :])
            abuf[e * H : (e + 1) * H, :] = o + pk[e * H : (e + 1) * H, 1:2]

        product(0)
        product(1)
        yield
        for e in range(E):
            norm(e)
            if e + 2 < E:
                product(e + 2)
            output(e)
            yield

    def heads(i, side):
        abuf, hbuf = abufs[side], hbufs[side]
        r0 = pl.multiple_of(i * TF, TF)
        v0 = pl.multiple_of(mp * R + i * TF, 128)
        logits = logit_bufs[side][...]
        probs = []
        for t in range(2):
            part = logits[4 * t : 4 * t + 4]
            part = jnp.exp(part - jnp.max(part, axis=0, keepdims=True))
            part = part / jnp.sum(part, axis=0, keepdims=True)
            probs.append([part[k : k + 1] for k in range(4)])
        for at in range(0, H, CH):
            for t in range(2):
                mixed = None
                for k in range(4):
                    e = TASK_EXPERTS[t][k]
                    term = probs[t][k] * abuf[e * H + at : e * H + at + CH, :]
                    mixed = term if mixed is None else mixed + term
                mixb[t * H + at : t * H + at + CH, :] = mixed.astype(BF16)
        pres = [nn(w1t[t], mixb[t * H : (t + 1) * H, :]) for t in range(2)]
        yield
        slopes = []
        for t in range(2):
            half = pres[t] + wide(b1t[t * 128 : (t + 1) * 128, :], TF)
            p = 1.0 + jnp.tanh(half)
            u1 = half * p
            u1b[t * 128 : (t + 1) * 128, :] = u1.astype(BF16)
            slopes.append(p + u1 * (2.0 - p))
        pre = nn(w2f[...], u1b[...])
        yield
        half = pre + wide(b2tt[...], TF)
        p = 1.0 + jnp.tanh(half)
        u2 = half * p
        slope2 = p + u2 * (2.0 - p)
        wl = wide(wlt[...], TF)
        weighted = u2 * wl
        d_logits = []
        valid = v_ref[:, pl.ds(v0, TF)].astype(F32)
        for t in range(2):
            logit = jnp.sum(weighted[t * 64 : (t + 1) * 64], axis=0, keepdims=True) + bl_ref[t]
            pred = 0.5 + 0.5 * jnp.tanh(0.5 * logit)
            predbuf[t : t + 1, pl.ds(r0, TF)] = pred
            label = y_ref[t : t + 1, pl.ds(v0, TF)].astype(F32)
            d_logits.append(valid * (pred - label))
        d_logit = jnp.concatenate(
            [jnp.broadcast_to(d_logits[t], (64, TF)) for t in range(2)], axis=0
        )
        acc_last[...] += fold_lanes(u2 * d_logit)
        acc_lb[0:2] += fold_lanes(jnp.concatenate(d_logits, axis=0))
        d2 = (d_logit * 0.5) * (wl * slope2)
        acc_b2[...] += fold_lanes(d2)
        d2_low = d2.astype(BF16)
        d_u1 = nn(w2b[...], d2_low)
        acc_second[...] += nt(d2_low, u1b[...])
        yield
        for t in range(2):
            d1 = d_u1[t * 128 : (t + 1) * 128] * slopes[t]
            acc_b1[t * 128 : (t + 1) * 128] += fold_lanes(d1)
            d1_low = d1.astype(BF16)
            dmix[t * H : (t + 1) * H, :] = nn(w1n[t], d1_low)
            acc_first[t] += nt(mixb[t * H : (t + 1) * H, :], d1_low)
        yield
        dots = [[jnp.zeros((8, TF), F32) for _ in range(4)] for _ in range(2)]
        for at in range(0, H, CH):
            dm = [dmix[t * H + at : t * H + at + CH, :] for t in range(2)]
            grads = [None] * E
            for t in range(2):
                for k in range(4):
                    e = TASK_EXPERTS[t][k]
                    term = probs[t][k] * dm[t]
                    grads[e] = term if grads[e] is None else grads[e] + term
                    o = abuf[e * H + at : e * H + at + CH, :]
                    dots[t][k] = dots[t][k] + fold8(dm[t] * o)
            for e in range(E):
                dobuf[e * H + at : e * H + at + CH, pl.ds(r0, TF)] = grads[e].astype(BF16)
        rows = []
        for t in range(2):
            sums = [jnp.sum(dots[t][k], axis=0, keepdims=True) for k in range(4)]
            centre = sum(probs[t][k] * sums[k] for k in range(4))
            rows += [probs[t][k] * (sums[k] - centre) for k in range(4)]
        d_gate = jnp.concatenate(rows, axis=0)
        acc_dlog[...] += fold_lanes(d_gate)
        high = d_gate.astype(BF16).astype(F32)
        d_gate = jnp.concatenate([high, d_gate - high], axis=0).astype(BF16)
        dlogbuf[:, pl.ds(r0, TF)] = d_gate
        acc_gate[...] += nn(d_gate, xbuf[pl.ds(r0, TF), :])
        yield
        for e in range(E):
            at = pl.ds(e * HE, HE)
            acc_out[at, :] += nt(hbuf[at, :], dobuf[e * H : (e + 1) * H, pl.ds(r0, TF)])
        yield

    def together(*parts):
        parts = list(parts)
        while parts:
            for part in list(parts):
                if next(part, "end") == "end":
                    parts.remove(part)

    for copy in keep:
        copy.wait()
    n_f = R // TF
    together(forward(0, 0))

    def forward_pair(j, carry):
        together(heads(2 * j, 0), forward(2 * j + 1, 1))
        together(heads(2 * j + 1, 1), forward(2 * j + 2, 0))
        return carry

    lax.fori_loop(0, n_f // 2 - 1, forward_pair, 0)
    together(heads(n_f - 2, 0), forward(n_f - 1, 1))
    together(heads(n_f - 1, 1))

    pending = []
    pred_at = pl.ds(pl.multiple_of(mp * R, 128), R)
    pred_local = pltpu.make_async_copy(predbuf, pred_hbm.at[:, pred_at], sem_l.at[0])
    pred_local.start()
    pending.append(pred_local)
    pending.append(send(predbuf, pred_hbm.at[:, pred_at], sem_w.at[6], sem_w.at[7], (b, other)))

    flight = {}
    n_sems = 1 + 2 * sum(radix - 1 for _, radix, _, _ in plan)

    def source(c, rows, place_at):
        w = WIDTHS[c]
        at = sum(p[2] for p in plan[1:place_at])
        if c < E:
            return sbuf.at[pl.ds(c * H + at, rows), pl.ds(min(place_at, 1) * w, w)]
        if place_at:
            return sends_low.at[c - E, pl.ds(at, rows), :]
        return sends.at[c - E, pl.ds(0, rows), :]

    def level_sems(level):
        return 1 + 2 * sum(radix - 1 for _, radix, _, _ in plan[:level])

    def start_pair(c):
        src = source(c, H, 0)
        flight[c] = [send(src, mprecv[c], sem_s.at[c, 0], sem_r.at[c, 0], (b, other))]

    def start_level(c, level, value):
        stride, radix, rows, after = plan[level]
        out = source(c, rows, level)
        out[...] = value.astype(BF16)
        copies = []
        for step in range(1, radix):
            k = level_sems(level) + step - 1
            part = out
            if after != rows:
                to = lax.rem(digits[level] + step, radix)
                part = out.at[pl.ds(pl.multiple_of(to * after, 16), after), :]
            dst = lvrecv[c][level].at[step]
            copies.append(send(part, dst, sem_s.at[c, k], sem_r.at[c, k], peer(level, step)))
        flight[c] = copies
        if after != rows:
            mine = out[pl.ds(pl.multiple_of(digits[level] * after, 16), after), :]
        else:
            mine = out[...]
        lvrecv[c][level][0] = mine

    def finish_level(c, level):
        stride, radix, rows, after = plan[level]
        for copy in flight[c]:
            copy.wait()
        if after != rows:
            parts = [lvrecv[c][level][step].astype(F32) for step in range(radix)]
            return functools.reduce(lambda p, q: p + q, parts)
        total = None
        for k in range(radix):
            step = lax.rem(k - digits[level] + radix, radix)
            part = lvrecv[c][level][step].astype(F32)
            total = part if total is None else total + part
        return total

    def region(c, level):
        at = 0
        for k in range(level + 1):
            if plan[k][2] != plan[k][3]:
                at = at + digits[k] * plan[k][3]
        rows = plan[level][3] if level >= 0 else H
        if isinstance(at, int):
            return gout_hbm.at[c, pl.ds(at, rows), pl.ds(0, WIDTHS[c])]
        return gout_hbm.at[c, pl.ds(pl.multiple_of(at, 16), rows), pl.ds(0, WIDTHS[c])]

    split = [level for level in range(n_levels) if plan[level][2] != plan[level][3]]

    def start_result(c, value):
        rows = plan[-1][3]
        final = source(c, rows, n_levels)
        final[...] = value.astype(BF16)
        local = pltpu.make_async_copy(final, region(c, n_levels - 1), sem_l.at[1 + c])
        local.start()
        flight[c] = [local]
        if split:
            start_gather(c, split[-1], final)

    def start_gather(c, level, src):
        dst = region(c, level)
        for step in range(1, plan[level][1]):
            k = level_sems(level) + plan[level][1] - 1 + step - 1
            flight[c].append(send(src, dst, sem_s.at[c, k], sem_r.at[c, k], peer(level, step)))

    def chunk_steps(c):
        steps = []

        def from_pair():
            for copy in flight[c]:
                copy.wait()
            if c < E:
                value = hkeep[c % 2][...]
            elif c == TOWERS:
                value = source(c, H, 0)[...].astype(F32)
            else:
                value = half_out(c - TOWERS - 1, mp)
            start_level(c, 0, value + mprecv[c][...].astype(F32))

        steps.append(from_pair)
        for level in range(n_levels):

            def next_level(level=level):
                value = finish_level(c, level)
                if level + 1 < n_levels:
                    start_level(c, level + 1, value)
                else:
                    start_result(c, value)

            steps.append(next_level)
        for place_in in range(len(split) - 1, 0, -1):

            def gather(place_in=place_in):
                for copy in flight[c]:
                    copy.wait()
                flight[c] = []
                start_gather(c, split[place_in - 1], region(c, split[place_in] - 1))

            steps.append(gather)

        def finish():
            for copy in flight[c]:
                copy.wait()
            flight[c] = []

        steps.append(finish)
        return steps

    queue = []
    clock = [0]

    def start_steps(steps, spacing):
        queue.append([clock[0] + spacing, spacing, steps])

    def turn():
        clock[0] += 1
        for item in list(queue):
            if clock[0] >= item[0]:
                item[2].pop(0)()
                item[0] = clock[0] + item[1]
                if not item[2]:
                    queue.remove(item)

    def half_out(group, h):
        parts = []
        for e in range(3 * group, 3 * group + 3):
            a = acc_out[pl.ds(pl.multiple_of(e * HE + h * 128, 16), 128), :]
            parts.append(jnp.concatenate([a[:, 0:128], a[:, 128:256]], axis=0))
        return jnp.concatenate(parts, axis=1)

    def half_in(h):
        at = pl.ds(pl.multiple_of(h * 128, 128), 128)
        return jnp.concatenate([acc_in[0][at, :], acc_in[1][at, :]], axis=0)

    def pack_towers():
        src = source(TOWERS, H, 0)
        src[:, 0:128] = acc_first[0].astype(BF16)
        src[:, 128:256] = acc_first[1].astype(BF16)
        gates = acc_gate[0:8] + acc_gate[8:16]
        rest = [acc_second[0:64, 0:128], acc_second[64:128, 128:256]]
        rest += [gates[:, k * 128 : (k + 1) * 128] for k in range(4)]
        rest.append(jnp.zeros((H - 160, 128), F32))
        src[:, 256:384] = jnp.concatenate(rest, axis=0).astype(BF16)

    def launch(c, spacing=3):
        start_pair(c)
        start_steps(chunk_steps(c), spacing)

    pack_towers()
    launch(TOWERS)

    def launch_out(group):
        source(TOWERS + 1 + group, H, 0)[...] = half_out(group, other).astype(BF16)
        launch(TOWERS + 1 + group)

    s2row[...] = jnp.sum(
        (gate_low * (acc_gate[0:8] + acc_gate[8:16])), axis=0, keepdims=True
    )

    def backward_start(e, i):
        rows = slice(e * H, (e + 1) * H)
        for part in range(TB // SB):
            lanes = pl.ds(pl.multiple_of(i * TB + part * SB, SB), SB)
            dmix[part * H : (part + 1) * H, :] = nn(wot[rows, :], dobuf[rows, lanes])

    def backward_part(e, r0, part):
        at0 = e * H
        lanes = pl.ds(r0, SB)
        work = dmix.at[part * H : (part + 1) * H]
        r = rbuf[e : e + 1, lanes]
        m1 = jnp.zeros((8, SB), F32)
        m2 = jnp.zeros((8, SB), F32)
        for u in range(0, H, CH):
            at = at0 + u
            zhat = zbuf[at : at + CH, lanes].astype(F32)
            dzg = work[u : u + CH, :] * sbuf[at : at + CH, lanes].astype(F32)
            q = dzg * zhat
            acc_u[0][u : u + CH, :] += fold_lanes(dzg)
            acc_u[1][u : u + CH, :] += fold_lanes(q)
            work[u : u + CH, :] = dzg
            m1 = m1 + fold8(dzg)
            m2 = m2 + fold8(q)
        m1 = jnp.sum(m1, axis=0, keepdims=True) * (1.0 / H)
        m2 = jnp.sum(m2, axis=0, keepdims=True) * (1.0 / H)
        for u in range(0, H, CH):
            at = at0 + u
            zhat = zbuf[at : at + CH, lanes].astype(F32)
            da = r * (work[u : u + CH, :] - m1 - zhat * m2)
            acc_u[2][u : u + CH, :] += fold_lanes(da)
            zbuf[at : at + CH, lanes] = da.astype(BF16)

    n_b = R // TB

    def weight_part(e, i):
        r0 = pl.multiple_of(i * TB, TB)
        rows = slice(e * H, (e + 1) * H)
        grad = nn(zbuf[rows, pl.ds(r0, TB)], xbuf[pl.ds(r0, TB), :])
        acc_in[0][...] += grad[:, 0:256]
        acc_in[1][...] += grad[:, 256:512]

    def backward_tile(e, i):
        for part in range(TB // SB):
            backward_part(e, pl.multiple_of(i * TB + part * SB, SB), part)

    def clear_units():
        for part in acc_u:
            part[...] = jnp.zeros((H, 128), F32)

    def clear_weights():
        for part in acc_in:
            part[...] = jnp.zeros((H, 256), F32)

    def finish_units(e):
        for k in range(3):
            sums = lane_sums(acc_u[2 - k][...])
            v_mp[mp, k * 12 + 2 * e : k * 12 + 2 * e + 1, :] = sums[:, 0:128]
            v_mp[mp, k * 12 + 2 * e + 1 : k * 12 + 2 * e + 2, :] = sums[:, 128:256]
        bo = acc_out[e * HE + H : e * HE + H + 1, :]
        v_mp[mp, 36 + 2 * e : 37 + 2 * e, :] = bo[:, 0:128]
        v_mp[mp, 37 + 2 * e : 38 + 2 * e, :] = bo[:, 128:256]
        clear_units()

    def finish_expert(e):
        hkeep[e % 2][...] = half_in(mp)
        source(e, H, 0)[...] = half_in(other).astype(BF16)
        launch(e, 2 if e >= E - 2 else 3)
        cross = jnp.zeros((8, D), F32)
        for u in range(0, H, CH):
            w = wf[e * H + u : e * H + u + CH, :].astype(F32)
            grad = jnp.concatenate([acc_in[0][u : u + CH, :], acc_in[1][u : u + CH, :]], axis=1)
            cross = cross + fold8(w * grad)
        s2row[...] += jnp.sum(cross, axis=0, keepdims=True)
        clear_weights()

    clear_weights()
    clear_units()
    for e in range(E):
        rows = slice(e * H, (e + 1) * H)
        wot[rows, :] = (wot[rows, :].T.astype(F32) * 0.5).astype(BF16)
    for e in range(E):

        def backward_step(i, carry, e=e):
            backward_start(e, i)
            weight_part(e, i - 1)
            backward_tile(e, i)
            return carry

        backward_start(e, 0)
        if e:
            weight_part(e - 1, n_b - 1)
        backward_tile(e, 0)
        if e:
            finish_expert(e - 1)
        if e == 2:
            back = []
            for k in range(2 * E):
                half, to = k % 2, 2048 + k * 128
                copy = pltpu.make_async_copy(
                    wb_hbm.at[half, :, (k // 2) * 128 : (k // 2 + 1) * 128],
                    sbuf.at[0:D, to : to + 128],
                    sem_f.at[k],
                )
                copy.start()
                back.append(copy)
        turn()
        if e == 0:
            launch_out(0)
        for k in range(3):
            first, last = 1 + k * (n_b - 1) // 3, 1 + (k + 1) * (n_b - 1) // 3
            lax.fori_loop(first, last, backward_step, 0)
            turn()
            if e == 0 and k == 1:
                launch_out(1)
        finish_units(e)
    weight_part(E - 1, n_b - 1)
    finish_expert(E - 1)
    for copy in back:
        copy.wait()
    wb = sbuf.at[0:D, 2048 : 2048 + E * H]
    for k in range(4):
        g2t[k * 128 : (k + 1) * 128, :] = column(stat_ref[1:2, k * 128 : (k + 1) * 128])

    for k in range(4):
        v_mp[mp, 48 + k : 49 + k, :] = s2row[:, k * 128 : (k + 1) * 128]
    v_mp[mp, 52:60, :] = acc_dlog[...]
    v_mp[mp, 60:61, :] = lane_sums(acc_last[...])
    v_mp[mp, 61:63, :] = acc_lb[0:2]
    b1_sums = lane_sums(acc_b1[...])
    v_mp[mp, 63:64, :] = b1_sums[:, 0:128]
    v_mp[mp, 64:65, :] = b1_sums[:, 128:256]
    v_mp[mp, 65:66, :] = lane_sums(acc_b2[...])
    v_mp[mp, 66:VR, :] = jnp.zeros((VR - 66, 128), F32)
    flight["v"] = [send(v_mp.at[mp], v_mp.at[mp], sem_v.at[0], sem_v.at[1], (b, other))]

    def small_level(level, total):
        own = digits[level]
        v_lv[level, own] = total
        flight["v"] = []
        for step in range(1, plan[level][1]):
            base = 2 + (level * 3 + step - 1) * 2
            flight["v"].append(
                send(
                    v_lv.at[level, own], v_lv.at[level, own],
                    sem_v.at[base], sem_v.at[base + 1], peer(level, step),
                )
            )

    def small_steps():
        steps = []

        def first():
            for copy in flight["v"]:
                copy.wait()
            small_level(0, v_mp[0] + v_mp[1])

        steps.append(first)
        for level in range(n_levels):

            def step(level=level):
                for copy in flight["v"]:
                    copy.wait()
                total = v_lv[level, 0]
                for k in range(1, plan[level][1]):
                    total = total + v_lv[level, k]
                if level + 1 < n_levels:
                    small_level(level + 1, total)
                    return
                vout_ref[...] = total
                row = jnp.concatenate([total[k : k + 1] for k in range(2 * E)], axis=1)
                row_high = row.astype(BF16).astype(F32)
                rows = jnp.concatenate(
                    [row_high, row - row_high, jnp.zeros((14, E * H), F32)], axis=0
                ).astype(BF16)
                s1 = nn(rows, wf[0 : E * H, :])
                gate_sum = jnp.sum(total[52:60], axis=1, keepdims=True)
                gate_part = jnp.sum(gate_low * gate_sum, axis=0, keepdims=True)
                stat_ref[3:4, :] = s1[0:1] + s1[1:2] + gate_part
                stat_ref[4:5, :] = jnp.concatenate([total[48 + k : 49 + k] for k in range(4)], axis=1)

            steps.append(step)
        return steps

    start_steps(small_steps(), 2)
    turn()

    def input_gradient(i):
        lanes = pl.ds(i * TB, TB)
        da = zbuf[:, lanes]
        dl = dlogbuf[:, lanes]
        for k, half in ((0, mp), (1, other)):
            at = pl.ds(pl.multiple_of(half * 256, 256), 256)
            grad = nn(wb[at, :], da) + nn(gback[at, 0:16], dl)
            grad = grad * wide(g2t[at, :], TB)
            dobuf[k * H : (k + 1) * H, lanes] = grad.astype(BF16)

    n_c = R // TB
    for part in range(4):
        for k in range(part * n_c // 4, (part + 1) * n_c // 4):
            input_gradient(k)
            turn()
        w = R // 4
        at = pl.ds(part * w, w)
        to = pl.ds(pl.multiple_of(mp * R + part * w, 128), w)
        local = pltpu.make_async_copy(dobuf.at[0:H, at], d_hbm.at[:, to], sem_l.at[1 + NC + part])
        local.start()
        pending.append(local)
        pending.append(
            send(dobuf.at[H : 2 * H, at], d_hbm.at[:, to], sem_d.at[part], sem_d.at[4 + part], (b, other))
        )
    while queue:
        turn()
    for copy in pending:
        copy.wait()


def final_kernel(
    tile, dt_hbm, x_hbm, v_ref, gain_ref, pred_ref, gout_ref, vout_ref, stat_ref,
    o_pred, feat_hbm, o_in, o_inb, o_gain, o_nb, o_out, o_outb, o_gate, o_gateb,
    o_w1, o_b1, o_w2, o_b2, o_wl, o_bl,
    dtb, xb, fb, sem_d, sem_x, sem_o,
):
    mp = lax.axis_index("mp")
    rows = xb.shape[0]
    half = pl.ds(pl.multiple_of(mp * 256, 256), 256)

    def load(k):
        at = pl.ds(pl.multiple_of(k * tile, tile), tile)
        return (
            pltpu.make_async_copy(dt_hbm.at[:, at], dtb.at[:, at], sem_d.at[k]),
            pltpu.make_async_copy(x_hbm.at[at, half], xb.at[at, :], sem_x.at[k]),
        )

    for k in range(rows // tile):
        for copy in load(k):
            copy.start()

    scale = 1.0 / stat_ref[2:3, 0:128]
    one = scale[:, 0:1]
    o_pred[...] = pred_ref[...]
    for e in range(E):
        for k in range(4):
            g = gout_ref[e, (k // 2) * 128 : (k // 2 + 1) * 128, (k % 2) * 128 : (k % 2 + 1) * 128]
            o_in[e, k * 128 : (k + 1) * 128, :] = (g.astype(F32) * one).T
        for k in range(2):
            g = gout_ref[TOWERS + 1 + e // 3, k * 128 : (k + 1) * 128, (e % 3) * 128 : (e % 3 + 1) * 128]
            o_out[e, :, k * 128 : (k + 1) * 128] = g.astype(F32) * one
        for ref, base in ((o_inb, 0), (o_gain, 12), (o_nb, 24)):
            sums = vout_ref[pl.ds(base + 2 * e + mp, 1), :] * scale
            ref[e : e + 1, :] = sums / gain_ref[e : e + 1, :] if base else sums
        for k in range(2):
            o_outb[e : e + 1, k * 128 : (k + 1) * 128] = (
                vout_ref[36 + 2 * e + k : 37 + 2 * e + k, :] * scale
            )
    o_w1[0] = gout_ref[TOWERS, :, 0:128].astype(F32) * one
    o_w1[1] = gout_ref[TOWERS, :, 128:256].astype(F32) * one
    g = gout_ref[TOWERS, 0:160, 256:384].astype(F32) * one
    o_w2[0] = g[0:64]
    o_w2[1] = g[64:128]
    for k in range(4):
        part = g[128 + 8 * k : 136 + 8 * k]
        o_gate[0, :, k * 128 : (k + 1) * 128] = part[0:4]
        o_gate[1, :, k * 128 : (k + 1) * 128] = part[4:8]
    gate_bias = jnp.sum(vout_ref[52:60, :], axis=1, keepdims=True) * scale
    table = jnp.concatenate([gate_bias, jnp.zeros((120, 128), F32)], axis=0).T
    o_gateb[0:1, :] = table[0:1, 0:4]
    o_gateb[1:2, :] = table[0:1, 4:8]
    last = vout_ref[60:61, :] * scale
    o_wl[0:1, :] = last[:, 0:64]
    o_wl[1:2, :] = last[:, 64:128]
    table = jnp.sum(vout_ref[61:63, :], axis=1, keepdims=True) * scale
    o_bl[...] = jnp.concatenate([table, jnp.zeros((126, 128), F32)], axis=0).T[0:1, 0:2]
    o_b1[...] = vout_ref[63:65, :] * scale
    b2 = vout_ref[65:66, :] * scale
    o_b2[0:1, :] = b2[:, 0:64]
    o_b2[1:2, :] = b2[:, 64:128]

    count = stat_ref[2:3, half]
    inv = stat_ref[1:2, half]
    slope = inv * inv * (stat_ref[4:5, half] / count)
    shift = inv * (stat_ref[3:4, half] / count) - stat_ref[0:1, half] * slope
    eye = jnp.where(
        lax.broadcasted_iota(jnp.int32, (256, 256), 0) == lax.broadcasted_iota(jnp.int32, (256, 256), 1), 1.0, 0.0
    ).astype(BF16)

    def store(k):
        at = pl.ds(pl.multiple_of(k * tile, tile), tile)
        return pltpu.make_async_copy(fb.at[at, :], feat_hbm.at[at, :], sem_o.at[k])

    def step(k, carry):
        for copy in load(k):
            copy.wait()
        for i in range(tile // 256):
            at = pl.ds(pl.multiple_of(k * tile + i * 256, 256), 256)
            grad = nt(eye, dtb[:, at])
            valid = nt(eye, jnp.broadcast_to(v_ref[:, at].astype(F32), (128, 256)).astype(BF16))
            for c in range(2):
                cols = slice(c * 128, (c + 1) * 128)
                term = valid * (shift[:, cols] + xb[at, cols].astype(F32) * slope[:, cols])
                fb[at, cols] = grad[:, cols] - term
        store(k).start()
        return carry

    lax.fori_loop(0, rows // tile, step, 0)
    for k in range(rows // tile):
        store(k).wait()


def on_device(
    features, validity, labels, expert_in, expert_in_bias, norm_gain, norm_bias, expert_out,
    expert_out_bias, gate_weight, gate_bias, tower_first, tower_first_bias, tower_second,
    tower_second_bias, tower_last, tower_last_bias,
):
    rows = features.shape[0]
    R = rows // 2
    n_batch = lax.axis_size("batch")
    plan = plan_of(n_batch)
    n_levels = len(plan)
    n_peers = sum(radix - 1 for _, radix, _, _ in plan)
    n_sems = 1 + 2 * n_peers
    v_row = validity.reshape(1, rows)
    y_rows = labels.T
    vm = pl.BlockSpec(memory_space=pltpu.VMEM)
    sm = pl.BlockSpec(memory_space=pltpu.SMEM)
    hb = pl.BlockSpec(memory_space=pl.ANY)
    dma = pltpu.SemaphoreType.DMA

    def scr(*shape, dtype=F32):
        return pltpu.VMEM(shape, dtype)

    low_rows = sum(p[2] for p in plan[1:]) + plan[-1][3]
    scratch = [
        scr(R, D, dtype=BF16), scr(E * H, R, dtype=BF16), scr(E * H, R, dtype=BF16),
        scr(E * H, R, dtype=BF16), scr(8, R), scr(16, R, dtype=BF16), scr(2, R),
        scr(E * H + 32, D, dtype=BF16), scr(D, 128, dtype=BF16),
        scr(E * H, H, dtype=BF16), scr(E * H, 128), scr(E * H, 128), scr(E * H, 128),
        scr(2, 128, H, dtype=BF16), scr(2, H, 128, dtype=BF16), scr(128, H, dtype=BF16),
        scr(H, 128, dtype=BF16), scr(H, 128), scr(128, 128), scr(128, 128), scr(8, 128),
        [scr(E * H, TF)] * 2, [scr(E * HE, TF, dtype=BF16)] * 2, [scr(8, TF)] * 2,
        scr(2 * H, TF, dtype=BF16), scr(H, TF, dtype=BF16), scr(2 * H, TF),
        scr(E * HE, H), scr(16, D), scr(2, H, 128), scr(128, H),
        scr(8, 128), scr(8, 128), scr(128, 128), scr(128, 128), scr(H, 128), scr(1, D),
        scr(24, 128), scr(24, 128),
        scr(8, 8, D), scr(n_levels, 4, 8, D), scr(2, VR, 128), scr(n_levels, 4, VR, 128),
        scr(3, H, 384, dtype=BF16), scr(3, low_rows, 384, dtype=BF16),
        [scr(H, w, dtype=BF16) for w in WIDTHS],
        [[scr(radix, after, w, dtype=BF16) for _, radix, _, after in plan] for w in WIDTHS],
        dma((8,)), dma((8,)), dma((14 + 6 * n_levels,)), dma((2 + 6 * n_levels,)),
        dma((NC, n_sems)), dma((NC, n_sems)), dma((5 + NC,)), dma((8,)), dma((3 * E,)),
    ]
    flops = 2 * R * (6 * D * E * H // 2 + 3 * E * H * H)
    d_half, preds, gsum, vsum, stats, _ = pl.pallas_call(
        functools.partial(main_kernel, plan, R),
        out_shape=(
            jax.ShapeDtypeStruct((256, rows), BF16),
            jax.ShapeDtypeStruct((2, rows), F32),
            jax.ShapeDtypeStruct((NC, H, 384), BF16),
            jax.ShapeDtypeStruct((VR, 128), F32),
            jax.ShapeDtypeStruct((8, D), F32),
            jax.ShapeDtypeStruct((2, D, E * 128), BF16),
        ),
        in_specs=[hb] + [vm] * 2 + [hb] * 2 + [vm] * 5 + [sm] + [vm] * 5 + [sm],
        out_specs=(hb, hb, hb, vm, vm, hb),
        scratch_shapes=scratch,
        compiler_params=pltpu.CompilerParams(
            collective_id=0, has_side_effects=True, vmem_limit_bytes=64 * 2**20 - 65536
        ),
        cost_estimate=pl.CostEstimate(flops=flops, bytes_accessed=20 * 2**20, transcendentals=0),
        name="layer",
    )(
        features, v_row, y_rows, expert_in, expert_out, expert_in_bias, norm_gain, norm_bias,
        expert_out_bias, jnp.swapaxes(gate_weight, 1, 2), gate_bias, tower_first, tower_first_bias,
        jnp.swapaxes(tower_second, 1, 2), tower_second_bias, tower_last, tower_last_bias,
    )

    tile = 1024
    n_tiles = rows // tile
    out_shapes = [
        (2, rows), (rows, 256), (E, D, 128), (E, 128), (E, 128), (E, 128), (E, 128, H), (E, H),
        (2, 4, D), (2, 4), (2, H, 128), (2, 128), (2, 64, 128), (2, 64), (2, 64), (1, 2),
    ]
    outs = pl.pallas_call(
        functools.partial(final_kernel, tile),
        out_shape=[jax.ShapeDtypeStruct(shape, F32) for shape in out_shapes],
        in_specs=[hb, hb] + [vm] * 6,
        out_specs=[vm, hb] + [vm] * 14,
        scratch_shapes=[
            scr(256, rows, dtype=BF16), scr(rows, 256, dtype=BF16), scr(rows, 256),
            dma((n_tiles,)), dma((n_tiles,)), dma((n_tiles,)),
        ],
        compiler_params=pltpu.CompilerParams(vmem_limit_bytes=64 * 2**20 - 65536),
        cost_estimate=pl.CostEstimate(
            flops=rows * 256 * 8, bytes_accessed=rows * 256 * 8, transcendentals=0
        ),
        name="finish",
    )(d_half, features, v_row, norm_gain, preds, gsum, vsum, stats)
    outs = list(outs)
    outs[0] = outs[0].T
    outs[8] = jnp.swapaxes(outs[8], 1, 2)
    outs[12] = jnp.swapaxes(outs[12], 1, 2)
    outs[15] = outs[15].reshape(2)
    return tuple(outs)


def solution(mesh):
    in_specs = (
        P("batch", None), P("batch"), P("batch", None), P(None, None, "mp"), P(None, "mp"),
        P(None, "mp"), P(None, "mp"), P(None, "mp", None), P(), P(), P(), P(), P(), P(), P(), P(), P(),
    )
    out_specs = (
        P("batch", None), P("batch", "mp"), P(None, None, "mp"), P(None, "mp"), P(None, "mp"),
        P(None, "mp"), P(None, "mp", None), P(), P(), P(), P(), P(), P(), P(), P(), P(),
    )
    return jax.shard_map(
        on_device, mesh=mesh, in_specs=in_specs, out_specs=out_specs, check_vma=False
    )
```

```python
import functools

import jax
import jax.numpy as jnp
from jax import lax
from jax.experimental import pallas as pl
from jax.experimental.pallas import tpu as pltpu
from jax.sharding import PartitionSpec as P

MESH = pl.DeviceIdType.MESH
F32 = jnp.float32
BF16 = jnp.bfloat16
EPS = 1e-05
TASK_EXPERTS = ((0, 1, 4, 5), (2, 3, 4, 5))
E = 6
H = 256
D = 512
TF = 256
TB = 512
SB = 256
CH = 32
VR = 72
HE = H + 16
WIDTHS = (256,) * E + (384,) * 3
NC = len(WIDTHS)
TOWERS = E


def levels_of(count):
    levels, stride = [], 1
    while stride < count:
        radix = 4 if (count // stride) % 4 == 0 else count // stride
        levels.append((stride, radix))
        stride *= radix
    return levels


def plan_of(count):
    plan, rows = [], H
    for stride, radix in levels_of(count):
        split = rows % radix == 0 and (rows // radix) % 16 == 0
        plan.append((stride, radix, rows, rows // radix if split else rows))
        rows = plan[-1][3]
    return plan


def nn(a, b):
    return lax.dot_general(a, b, (((1,), (0,)), ((), ())), preferred_element_type=F32)


def nt(a, b):
    return lax.dot_general(a, b, (((1,), (1,)), ((), ())), preferred_element_type=F32)


def column(row):
    return jnp.broadcast_to(row, (128, 128)).T


def wide(table, width):
    return jnp.concatenate([table] * (width // 128), axis=1)


def fold8(value):
    total = value[0:8]
    for start in range(8, value.shape[0], 8):
        total = total + value[start : start + 8]
    return total


def fold_lanes(value):
    total = value[:, 0:128]
    for start in range(128, value.shape[1], 128):
        total = total + value[:, start : start + 128]
    return total


def lane_sums(partial):
    rows = [
        jnp.sum(partial[at : at + 128].T, axis=0, keepdims=True)
        for at in range(0, partial.shape[0], 128)
    ]
    return jnp.concatenate(rows, axis=1)


def merge_stats(items):
    count = items[0][2:3]
    total = items[0][0:1]
    for item in items[1:]:
        count = count + item[2:3]
        total = total + item[0:1]
    mean = total / jnp.maximum(count, 1.0)
    square = jnp.zeros_like(total)
    for item in items:
        shift = item[0:1] / jnp.maximum(item[2:3], 1.0) - mean
        square = square + item[1:2] + item[2:3] * shift * shift
    return total, square, count


def main_kernel(
    plan, rows_core,
    x_hbm, v_ref, y_ref, win_hbm, wout_hbm, bin_ref, gain_ref, nb_ref, bout_ref, gate_ref, gb_ref,
    w1_ref, b1_ref, w2_ref, b2_ref, wl_ref, bl_ref,
    d_hbm, pred_hbm, gout_hbm, vout_ref, stat_ref, wb_hbm,
    xbuf, zbuf, sbuf, dobuf, rbuf, dlogbuf, predbuf,
    wf, gback, wot, pk, g2t, b2t,
    w1t, w1n, w2f, w2b, b1t, b2tt, wlt, gbt,
    abufs, hbufs, logit_bufs, mixb, u1b, dmix,
    acc_out, acc_gate, acc_first, acc_second,
    acc_dlog, acc_lb, acc_last, acc_b2, acc_b1, s2row,
    bias_snd, bias_rcv,
    st_near, st_lv, v_mp, v_lv, sends, sends_low, mprecv, lvrecv,
    sem_x, sem_w, sem_st, sem_v, sem_s, sem_r, sem_l, sem_d, sem_f,
):
    R = rows_core
    abuf = abufs[0]
    acc_in = (abuf.at[0:H, :], abuf.at[H : 2 * H, :])
    hkeep = (abuf.at[2 * H : 3 * H, :], abuf.at[3 * H : 4 * H, :])
    acc_u = (
        abuf.at[4 * H : 5 * H, 0:128], abuf.at[4 * H : 5 * H, 128:256], abuf.at[5 * H : 6 * H, 0:128]
    )
    n_levels = len(plan)
    b = lax.axis_index("batch")
    mp = lax.axis_index("mp")
    other = 1 - mp
    digits = [lax.rem(lax.div(b, stride), radix) for stride, radix, _, _ in plan]

    def peer(level, step):
        stride, radix = plan[level][:2]
        to = lax.rem(digits[level] + step, radix)
        return (b + (to - digits[level]) * stride, mp)

    def send(src, dst, ssem, rsem, to):
        copy = pltpu.make_async_remote_copy(
            src_ref=src, dst_ref=dst, send_sem=ssem, recv_sem=rsem,
            device_id=to, device_id_type=MESH,
        )
        copy.start()
        return copy

    n_x = 8
    xr = R // n_x
    x_copies = []
    for k in range(n_x):
        copy = pltpu.make_async_copy(
            x_hbm.at[pl.ds(pl.multiple_of(mp * R + k * xr, 16), xr), :],
            xbuf.at[pl.ds(k * xr, xr), :],
            sem_x.at[k],
        )
        copy.start()
        x_copies.append(copy)

    f_copies = []
    for e in range(E):
        for k in range(2):
            f_copies.append(
                pltpu.make_async_copy(
                    win_hbm.at[e, k * H : (k + 1) * H, :],
                    abuf.at[e * H : (e + 1) * H, k * 128 : (k + 1) * 128],
                    sem_f.at[2 * e + k],
                )
            )
        f_copies.append(
            pltpu.make_async_copy(
                wout_hbm.at[e], acc_out.at[e * 128 : (e + 1) * 128, :], sem_f.at[2 * E + e]
            )
        )
    for copy in f_copies:
        copy.start()

    barrier = pltpu.get_barrier_semaphore()
    near = [(step, m) for step in range(plan[0][1]) for m in range(2) if step or m]

    def near_peer(step, m):
        return (peer(0, step)[0], other if m else mp)

    greets = [near_peer(step, m) for step, m in near]
    for level in range(1, n_levels):
        greets += [peer(level, step) for step in range(1, plan[level][1])]
    for to in greets:
        pl.semaphore_signal(barrier, inc=1, device_id=to, device_id_type=MESH)

    v_row = v_ref[:, pl.ds(pl.multiple_of(mp * R, 128), R)].astype(F32)
    count = jnp.sum(v_row, axis=1, keepdims=True)
    total = jnp.zeros((16, D), F32)
    for k in range(n_x):
        x_copies[k].wait()
        v16 = jnp.broadcast_to(v_row[:, k * xr : (k + 1) * xr], (16, xr)).astype(BF16)
        total = total + nn(v16, xbuf[pl.ds(k * xr, xr), :])
    mean = total[0:1] / jnp.maximum(count, 1.0)

    def square_step(k, total):
        for part in range(2):
            r0 = pl.multiple_of(k * 512 + part * 256, 256)
            off = xbuf[pl.ds(r0, 256), :].astype(F32) - mean
            v16 = v_ref[:, pl.ds(pl.multiple_of(mp * R + r0, 128), 256)]
            v16 = jnp.broadcast_to(v16.astype(F32), (16, 256)).astype(BF16)
            total = total + nn(v16, (off * off).astype(BF16))
        return total

    square = lax.fori_loop(0, R // 512, square_step, jnp.zeros((16, D), F32))
    pl.semaphore_wait(barrier, len(greets))
    me = digits[0] * 2 + mp
    st_near[me] = jnp.concatenate(
        [total[0:1], square[0:1], jnp.broadcast_to(count, (1, D)), jnp.zeros((5, D), F32)], axis=0
    )
    st_copies = [
        send(st_near.at[me], st_near.at[me], sem_st.at[2 * k], sem_st.at[2 * k + 1], near_peer(*near[k]))
        for k in range(len(near))
    ]

    win_snd = dobuf.at[0:D, 0 : E * 128]
    win_rcv = dobuf.at[0:D, 1024 : 1024 + E * 128]
    wout_snd = dobuf.at[D : D + 128, 0 : E * H]
    wout_rcv = dobuf.at[D : D + 128, 2048 : 2048 + E * H]
    for copy in f_copies:
        copy.wait()
    for e in range(E):
        for k in range(2):
            win_snd[k * H : (k + 1) * H, e * 128 : (e + 1) * 128] = abuf[
                e * H : (e + 1) * H, k * 128 : (k + 1) * 128
            ].astype(BF16)
        wout_snd[:, e * H : (e + 1) * H] = acc_out[e * 128 : (e + 1) * 128, :].astype(BF16)
    bias_snd[0:E] = bin_ref[...]
    bias_snd[8 : 8 + E] = gain_ref[...]
    bias_snd[16 : 16 + E] = nb_ref[...]
    w_copies = [
        send(win_snd, win_rcv, sem_w.at[0], sem_w.at[1], (b, other)),
        send(wout_snd, wout_rcv, sem_w.at[2], sem_w.at[3], (b, other)),
        send(bias_snd, bias_rcv, sem_w.at[4], sem_w.at[5], (b, other)),
    ]

    for t in range(2):
        w1n[t] = w1_ref[t].astype(BF16)
        w1t[t] = (w1_ref[t].T * 0.5).astype(BF16)
        b1t[t * 128 : (t + 1) * 128] = column(b1_ref[t : t + 1, :]) * 0.5
    zero64 = jnp.zeros((64, 128), F32)
    zero128 = jnp.zeros((128, 64), F32)
    w2f[0:64] = (jnp.concatenate([w2_ref[0], zero64], axis=1) * 0.5).astype(BF16)
    w2f[64:128] = (jnp.concatenate([zero64, w2_ref[1]], axis=1) * 0.5).astype(BF16)
    w2b[0:128] = (jnp.concatenate([w2_ref[0].T, zero128], axis=1) * 0.5).astype(BF16)
    w2b[128:256] = (jnp.concatenate([zero128, w2_ref[1].T], axis=1) * 0.5).astype(BF16)
    b2tt[...] = column(jnp.concatenate([b2_ref[0:1, :], b2_ref[1:2, :]], axis=1)) * 0.5
    wlt[...] = column(jnp.concatenate([wl_ref[0:1, :], wl_ref[1:2, :]], axis=1))
    gbt[...] = jnp.concatenate(
        [jnp.full((1, 128), gb_ref[t, k], F32) for t in range(2) for k in range(4)], axis=0
    )
    gate = jnp.concatenate([gate_ref[0], gate_ref[1]], axis=0)
    gate_low = gate.astype(BF16).astype(F32)
    gback[...] = jnp.concatenate([gate_low, gate_low, jnp.zeros((112, D), F32)], axis=0).T.astype(BF16)
    acc_gate[...] = jnp.zeros_like(acc_gate)
    acc_out[...] = jnp.zeros_like(acc_out)
    for hbuf in hbufs:
        for e in range(E):
            hbuf[e * HE + H : (e + 1) * HE, :] = jnp.ones((16, TF), BF16)
    acc_first[...] = jnp.zeros_like(acc_first)
    acc_second[...] = jnp.zeros_like(acc_second)
    acc_dlog[...] = jnp.zeros_like(acc_dlog)
    acc_lb[...] = jnp.zeros_like(acc_lb)
    acc_last[...] = jnp.zeros_like(acc_last)
    acc_b1[...] = jnp.zeros_like(acc_b1)
    acc_b2[...] = jnp.zeros_like(acc_b2)

    lane = lax.broadcasted_iota(jnp.int32, (128, 128), 1)

    def place(half, win, wout, bias):
        for e in range(E):
            at = pl.multiple_of(e * H + half * 128, 128)
            w = win[:, e * 128 : (e + 1) * 128]
            wf[pl.ds(at, 128), :] = w.T
            o = wout[:, e * H : (e + 1) * H]
            wot[pl.ds(e * H, H), pl.ds(pl.multiple_of(half * 128, 128), 128)] = o.T
            gain = column(bias[8 + e : 9 + e, :])
            pk[pl.ds(at, 128), :] = jnp.where(lane == 0, column(bias[e : e + 1, :]), gain)
            g2t[pl.ds(at, 128), :] = gain * 0.5
            b2t[pl.ds(at, 128), :] = column(bias[16 + e : 17 + e, :]) * 0.5

    place(mp, win_snd, wout_snd, bias_snd)
    for copy in st_copies:
        copy.wait()
    total, square, count = merge_stats([st_near[k] for k in range(2 * plan[0][1])])
    for level in range(1, n_levels):
        own = digits[level]
        st_lv[level, own] = jnp.concatenate([total, square, count, jnp.zeros((5, D), F32)], axis=0)
        copies = []
        for step in range(1, plan[level][1]):
            base = 2 * (len(near) + level * 3 + step - 1)
            copies.append(
                send(
                    st_lv.at[level, own], st_lv.at[level, own],
                    sem_st.at[base], sem_st.at[base + 1], peer(level, step),
                )
            )
        if level == 1:
            for copy in w_copies:
                copy.wait()
            place(other, win_rcv, wout_rcv, bias_rcv)
            keep = [
                pltpu.make_async_copy(win_snd, wb_hbm.at[mp], sem_f.at[0]),
                pltpu.make_async_copy(win_rcv, wb_hbm.at[other], sem_f.at[1]),
            ]
            for copy in keep:
                copy.start()
            means = []
            for e in range(E):
                w = wf[e * H : (e + 1) * H, :].astype(F32)
                means.append(jnp.sum(w, axis=0, keepdims=True) * (1.0 / H))
                shift = jnp.sum(pk[e * H : (e + 1) * H, 0:1], axis=0, keepdims=True) * (1.0 / H)
                for k in range(2):
                    at = slice(e * H + k * 128, e * H + (k + 1) * 128)
                    table = pk[at, :]
                    table = jnp.where(lane == 0, table - shift, table)
                    second = column(bout_ref[e : e + 1, k * 128 : (k + 1) * 128])
                    pk[at, :] = jnp.where(lane == 1, second, table)
            pad = [jnp.zeros((2, D), F32)]
            means = jnp.concatenate(means + pad, axis=0)
            means_high = means.astype(BF16).astype(F32)
            wf[E * H : E * H + 32, :] = jnp.concatenate(
                [gate_low, means_high, means - means_high, jnp.zeros((8, D), F32)], axis=0
            ).astype(BF16)
        for copy in copies:
            copy.wait()
        total, square, count = merge_stats([st_lv[level, k] for k in range(plan[level][1])])
    mu = total / count
    inv = lax.rsqrt(square / count + EPS)
    stat_ref[...] = jnp.concatenate([mu, inv, count, jnp.zeros((5, D), F32)], axis=0)

    def forward(i, side):
        abuf, hbuf = abufs[side], hbufs[side]
        r0 = pl.multiple_of(i * TF, TF)
        x_tile = xbuf[pl.ds(r0, TF), :].astype(F32)
        xn = ((x_tile - stat_ref[0:1, :]) * stat_ref[1:2, :]).astype(BF16)
        xbuf[pl.ds(r0, TF), :] = xn
        ext = nt(wf[E * H : E * H + 32, :], xn)
        logit_bufs[side][...] = ext[0:8] + wide(gbt[...], TF)
        means = ext[8:16] + ext[16:24]

        def product(e):
            abuf[e * H : (e + 1) * H, :] = nt(wf[e * H : (e + 1) * H, :], xn)

        def norm(e):
            squares = jnp.zeros((8, TF), F32)
            for at in range(e * H, (e + 1) * H, CH):
                c = (abuf[at : at + CH, :] - means[e : e + 1]) + pk[at : at + CH, 0:1]
                abuf[at : at + CH, :] = c
                squares = squares + fold8(c * c)
            r = lax.rsqrt(jnp.sum(squares, axis=0, keepdims=True) * (1.0 / H) + EPS)
            rbuf[e : e + 1, pl.ds(r0, TF)] = r
            for u in range(0, H, CH):
                at = e * H + u
                zhat = abuf[at : at + CH, :] * r
                zbuf[at : at + CH, pl.ds(r0, TF)] = zhat.astype(BF16)
                half = zhat * wide(g2t[at : at + CH, :], TF) + wide(b2t[at : at + CH, :], TF)
                p = 1.0 + jnp.tanh(half)
                h = half * p
                hbuf[e * HE + u : e * HE + u + CH, :] = h.astype(BF16)
                slope = (p + h * (2.0 - p)) * pk[at : at + CH, 2:3]
                sbuf[at : at + CH, pl.ds(r0, TF)] = slope.astype(BF16)

        def output(e):
            o = nn(wot[e * H : (e + 1) * H, :], hbuf[e * HE : e * HE + H, :])
            abuf[e * H : (e + 1) * H, :] = o + pk[e * H : (e + 1) * H, 1:2]

        product(0)
        product(1)
        yield
        for e in range(E):
            norm(e)
            if e + 2 < E:
                product(e + 2)
            output(e)
            yield

    def heads(i, side):
        abuf, hbuf = abufs[side], hbufs[side]
        r0 = pl.multiple_of(i * TF, TF)
        v0 = pl.multiple_of(mp * R + i * TF, 128)
        logits = logit_bufs[side][...]
        probs = []
        for t in range(2):
            part = logits[4 * t : 4 * t + 4]
            part = jnp.exp(part - jnp.max(part, axis=0, keepdims=True))
            part = part / jnp.sum(part, axis=0, keepdims=True)
            probs.append([part[k : k + 1] for k in range(4)])
        for at in range(0, H, CH):
            for t in range(2):
                mixed = None
                for k in range(4):
                    e = TASK_EXPERTS[t][k]
                    term = probs[t][k] * abuf[e * H + at : e * H + at + CH, :]
                    mixed = term if mixed is None else mixed + term
                mixb[t * H + at : t * H + at + CH, :] = mixed.astype(BF16)
        pres = [nn(w1t[t], mixb[t * H : (t + 1) * H, :]) for t in range(2)]
        yield
        slopes = []
        for t in range(2):
            half = pres[t] + wide(b1t[t * 128 : (t + 1) * 128, :], TF)
            p = 1.0 + jnp.tanh(half)
            u1 = half * p
            u1b[t * 128 : (t + 1) * 128, :] = u1.astype(BF16)
            slopes.append(p + u1 * (2.0 - p))
        pre = nn(w2f[...], u1b[...])
        yield
        half = pre + wide(b2tt[...], TF)
        p = 1.0 + jnp.tanh(half)
        u2 = half * p
        slope2 = p + u2 * (2.0 - p)
        wl = wide(wlt[...], TF)
        weighted = u2 * wl
        d_logits = []
        valid = v_ref[:, pl.ds(v0, TF)].astype(F32)
        for t in range(2):
            logit = jnp.sum(weighted[t * 64 : (t + 1) * 64], axis=0, keepdims=True) + bl_ref[t]
            pred = 0.5 + 0.5 * jnp.tanh(0.5 * logit)
            predbuf[t : t + 1, pl.ds(r0, TF)] = pred
            label = y_ref[t : t + 1, pl.ds(v0, TF)].astype(F32)
            d_logits.append(valid * (pred - label))
        d_logit = jnp.concatenate(
            [jnp.broadcast_to(d_logits[t], (64, TF)) for t in range(2)], axis=0
        )
        acc_last[...] += fold_lanes(u2 * d_logit)
        acc_lb[0:2] += fold_lanes(jnp.concatenate(d_logits, axis=0))
        d2 = (d_logit * 0.5) * (wl * slope2)
        acc_b2[...] += fold_lanes(d2)
        d2_low = d2.astype(BF16)
        d_u1 = nn(w2b[...], d2_low)
        acc_second[...] += nt(d2_low, u1b[...])
        yield
        for t in range(2):
            d1 = d_u1[t * 128 : (t + 1) * 128] * slopes[t]
            acc_b1[t * 128 : (t + 1) * 128] += fold_lanes(d1)
            d1_low = d1.astype(BF16)
            dmix[t * H : (t + 1) * H, :] = nn(w1n[t], d1_low)
            acc_first[t] += nt(mixb[t * H : (t + 1) * H, :], d1_low)
        yield
        dots = [[jnp.zeros((8, TF), F32) for _ in range(4)] for _ in range(2)]
        for at in range(0, H, CH):
            dm = [dmix[t * H + at : t * H + at + CH, :] for t in range(2)]
            grads = [None] * E
            for t in range(2):
                for k in range(4):
                    e = TASK_EXPERTS[t][k]
                    term = probs[t][k] * dm[t]
                    grads[e] = term if grads[e] is None else grads[e] + term
                    o = abuf[e * H + at : e * H + at + CH, :]
                    dots[t][k] = dots[t][k] + fold8(dm[t] * o)
            for e in range(E):
                dobuf[e * H + at : e * H + at + CH, pl.ds(r0, TF)] = grads[e].astype(BF16)
        rows = []
        for t in range(2):
            sums = [jnp.sum(dots[t][k], axis=0, keepdims=True) for k in range(4)]
            centre = sum(probs[t][k] * sums[k] for k in range(4))
            rows += [probs[t][k] * (sums[k] - centre) for k in range(4)]
        d_gate = jnp.concatenate(rows, axis=0)
        acc_dlog[...] += fold_lanes(d_gate)
        high = d_gate.astype(BF16).astype(F32)
        d_gate = jnp.concatenate([high, d_gate - high], axis=0).astype(BF16)
        dlogbuf[:, pl.ds(r0, TF)] = d_gate
        acc_gate[...] += nn(d_gate, xbuf[pl.ds(r0, TF), :])
        yield
        for e in range(E):
            at = pl.ds(e * HE, HE)
            acc_out[at, :] += nt(hbuf[at, :], dobuf[e * H : (e + 1) * H, pl.ds(r0, TF)])
        yield

    def together(*parts):
        parts = list(parts)
        while parts:
            for part in list(parts):
                if next(part, "end") == "end":
                    parts.remove(part)

    for copy in keep:
        copy.wait()
    n_f = R // TF
    together(forward(0, 0))

    def forward_pair(j, carry):
        together(heads(2 * j, 0), forward(2 * j + 1, 1))
        together(heads(2 * j + 1, 1), forward(2 * j + 2, 0))
        return carry

    lax.fori_loop(0, n_f // 2 - 1, forward_pair, 0)
    together(heads(n_f - 2, 0), forward(n_f - 1, 1))
    together(heads(n_f - 1, 1))

    pending = []
    pred_at = pl.ds(pl.multiple_of(mp * R, 128), R)
    pred_local = pltpu.make_async_copy(predbuf, pred_hbm.at[:, pred_at], sem_l.at[0])
    pred_local.start()
    pending.append(pred_local)
    pending.append(send(predbuf, pred_hbm.at[:, pred_at], sem_w.at[6], sem_w.at[7], (b, other)))

    flight = {}
    n_sems = 1 + 2 * sum(radix - 1 for _, radix, _, _ in plan)

    def source(c, rows, place_at):
        w = WIDTHS[c]
        at = sum(p[2] for p in plan[1:place_at])
        if c < E:
            return sbuf.at[pl.ds(c * H + at, rows), pl.ds(min(place_at, 1) * w, w)]
        if place_at:
            return sends_low.at[c - E, pl.ds(at, rows), :]
        return sends.at[c - E, pl.ds(0, rows), :]

    def level_sems(level):
        return 1 + 2 * sum(radix - 1 for _, radix, _, _ in plan[:level])

    def start_pair(c):
        src = source(c, H, 0)
        flight[c] = [send(src, mprecv[c], sem_s.at[c, 0], sem_r.at[c, 0], (b, other))]

    def start_level(c, level, value):
        stride, radix, rows, after = plan[level]
        out = source(c, rows, level)
        out[...] = value.astype(BF16)
        copies = []
        for step in range(1, radix):
            k = level_sems(level) + step - 1
            part = out
            if after != rows:
                to = lax.rem(digits[level] + step, radix)
                part = out.at[pl.ds(pl.multiple_of(to * after, 16), after), :]
            dst = lvrecv[c][level].at[step]
            copies.append(send(part, dst, sem_s.at[c, k], sem_r.at[c, k], peer(level, step)))
        flight[c] = copies
        if after != rows:
            mine = out[pl.ds(pl.multiple_of(digits[level] * after, 16), after), :]
        else:
            mine = out[...]
        lvrecv[c][level][0] = mine

    def finish_level(c, level):
        stride, radix, rows, after = plan[level]
        for copy in flight[c]:
            copy.wait()
        if after != rows:
            parts = [lvrecv[c][level][step].astype(F32) for step in range(radix)]
            return functools.reduce(lambda p, q: p + q, parts)
        total = None
        for k in range(radix):
            step = lax.rem(k - digits[level] + radix, radix)
            part = lvrecv[c][level][step].astype(F32)
            total = part if total is None else total + part
        return total

    def region(c, level):
        at = 0
        for k in range(level + 1):
            if plan[k][2] != plan[k][3]:
                at = at + digits[k] * plan[k][3]
        rows = plan[level][3] if level >= 0 else H
        if isinstance(at, int):
            return gout_hbm.at[c, pl.ds(at, rows), pl.ds(0, WIDTHS[c])]
        return gout_hbm.at[c, pl.ds(pl.multiple_of(at, 16), rows), pl.ds(0, WIDTHS[c])]

    split = [level for level in range(n_levels) if plan[level][2] != plan[level][3]]

    def start_result(c, value):
        rows = plan[-1][3]
        final = source(c, rows, n_levels)
        final[...] = value.astype(BF16)
        local = pltpu.make_async_copy(final, region(c, n_levels - 1), sem_l.at[1 + c])
        local.start()
        flight[c] = [local]
        if split:
            start_gather(c, split[-1], final)

    def start_gather(c, level, src):
        dst = region(c, level)
        for step in range(1, plan[level][1]):
            k = level_sems(level) + plan[level][1] - 1 + step - 1
            flight[c].append(send(src, dst, sem_s.at[c, k], sem_r.at[c, k], peer(level, step)))

    def chunk_steps(c):
        steps = []

        def from_pair():
            for copy in flight[c]:
                copy.wait()
            if c < E:
                value = hkeep[c % 2][...]
            elif c == TOWERS:
                value = source(c, H, 0)[...].astype(F32)
            else:
                value = half_out(c - TOWERS - 1, mp)
            start_level(c, 0, value + mprecv[c][...].astype(F32))

        steps.append(from_pair)
        for level in range(n_levels):

            def next_level(level=level):
                value = finish_level(c, level)
                if level + 1 < n_levels:
                    start_level(c, level + 1, value)
                else:
                    start_result(c, value)

            steps.append(next_level)
        for place_in in range(len(split) - 1, 0, -1):

            def gather(place_in=place_in):
                for copy in flight[c]:
                    copy.wait()
                flight[c] = []
                start_gather(c, split[place_in - 1], region(c, split[place_in] - 1))

            steps.append(gather)

        def finish():
            for copy in flight[c]:
                copy.wait()
            flight[c] = []

        steps.append(finish)
        return steps

    queue = []
    clock = [0]

    def start_steps(steps, spacing):
        queue.append([clock[0] + spacing, spacing, steps])

    def turn():
        clock[0] += 1
        for item in list(queue):
            if clock[0] >= item[0]:
                item[2].pop(0)()
                item[0] = clock[0] + item[1]
                if not item[2]:
                    queue.remove(item)

    def half_out(group, h):
        parts = []
        for e in range(3 * group, 3 * group + 3):
            a = acc_out[pl.ds(pl.multiple_of(e * HE + h * 128, 16), 128), :]
            parts.append(jnp.concatenate([a[:, 0:128], a[:, 128:256]], axis=0))
        return jnp.concatenate(parts, axis=1)

    def half_in(h):
        at = pl.ds(pl.multiple_of(h * 128, 128), 128)
        return jnp.concatenate([acc_in[0][at, :], acc_in[1][at, :]], axis=0)

    def pack_towers():
        src = source(TOWERS, H, 0)
        src[:, 0:128] = acc_first[0].astype(BF16)
        src[:, 128:256] = acc_first[1].astype(BF16)
        gates = acc_gate[0:8] + acc_gate[8:16]
        rest = [acc_second[0:64, 0:128], acc_second[64:128, 128:256]]
        rest += [gates[:, k * 128 : (k + 1) * 128] for k in range(4)]
        rest.append(jnp.zeros((H - 160, 128), F32))
        src[:, 256:384] = jnp.concatenate(rest, axis=0).astype(BF16)

    def launch(c, spacing=4):
        start_pair(c)
        start_steps(chunk_steps(c), spacing)

    pack_towers()
    launch(TOWERS)

    def launch_out(group):
        source(TOWERS + 1 + group, H, 0)[...] = half_out(group, other).astype(BF16)
        launch(TOWERS + 1 + group)

    s2row[...] = jnp.sum(
        (gate_low * (acc_gate[0:8] + acc_gate[8:16])), axis=0, keepdims=True
    )

    def backward_start(e, i):
        rows = slice(e * H, (e + 1) * H)
        for part in range(TB // SB):
            lanes = pl.ds(pl.multiple_of(i * TB + part * SB, SB), SB)
            dmix[part * H : (part + 1) * H, :] = nn(wot[rows, :], dobuf[rows, lanes])

    def backward_part(e, r0, part):
        at0 = e * H
        lanes = pl.ds(r0, SB)
        work = dmix.at[part * H : (part + 1) * H]
        r = rbuf[e : e + 1, lanes]
        m1 = jnp.zeros((8, SB), F32)
        m2 = jnp.zeros((8, SB), F32)
        for u in range(0, H, CH):
            at = at0 + u
            zhat = zbuf[at : at + CH, lanes].astype(F32)
            dzg = work[u : u + CH, :] * sbuf[at : at + CH, lanes].astype(F32)
            q = dzg * zhat
            acc_u[0][u : u + CH, :] += fold_lanes(dzg)
            acc_u[1][u : u + CH, :] += fold_lanes(q)
            work[u : u + CH, :] = dzg
            m1 = m1 + fold8(dzg)
            m2 = m2 + fold8(q)
        m1 = jnp.sum(m1, axis=0, keepdims=True) * (1.0 / H)
        m2 = jnp.sum(m2, axis=0, keepdims=True) * (1.0 / H)
        for u in range(0, H, CH):
            at = at0 + u
            zhat = zbuf[at : at + CH, lanes].astype(F32)
            da = r * (work[u : u + CH, :] - m1 - zhat * m2)
            acc_u[2][u : u + CH, :] += fold_lanes(da)
            zbuf[at : at + CH, lanes] = da.astype(BF16)

    n_b = R // TB

    def weight_part(e, i):
        r0 = pl.multiple_of(i * TB, TB)
        rows = slice(e * H, (e + 1) * H)
        grad = nn(zbuf[rows, pl.ds(r0, TB)], xbuf[pl.ds(r0, TB), :])
        acc_in[0][...] += grad[:, 0:256]
        acc_in[1][...] += grad[:, 256:512]

    def backward_tile(e, i):
        for part in range(TB // SB):
            backward_part(e, pl.multiple_of(i * TB + part * SB, SB), part)

    def clear_units():
        for part in acc_u:
            part[...] = jnp.zeros((H, 128), F32)

    def clear_weights():
        for part in acc_in:
            part[...] = jnp.zeros((H, 256), F32)

    def finish_units(e):
        for k in range(3):
            sums = lane_sums(acc_u[2 - k][...])
            v_mp[mp, k * 12 + 2 * e : k * 12 + 2 * e + 1, :] = sums[:, 0:128]
            v_mp[mp, k * 12 + 2 * e + 1 : k * 12 + 2 * e + 2, :] = sums[:, 128:256]
        bo = acc_out[e * HE + H : e * HE + H + 1, :]
        v_mp[mp, 36 + 2 * e : 37 + 2 * e, :] = bo[:, 0:128]
        v_mp[mp, 37 + 2 * e : 38 + 2 * e, :] = bo[:, 128:256]
        clear_units()

    def finish_expert(e):
        hkeep[e % 2][...] = half_in(mp)
        source(e, H, 0)[...] = half_in(other).astype(BF16)
        launch(e, 2 if e == E - 1 else 3 if e == E - 2 else 4)
        cross = jnp.zeros((8, D), F32)
        for u in range(0, H, CH):
            w = wf[e * H + u : e * H + u + CH, :].astype(F32)
            grad = jnp.concatenate([acc_in[0][u : u + CH, :], acc_in[1][u : u + CH, :]], axis=1)
            cross = cross + fold8(w * grad)
        s2row[...] += jnp.sum(cross, axis=0, keepdims=True)
        clear_weights()

    clear_weights()
    clear_units()
    for e in range(E):
        rows = slice(e * H, (e + 1) * H)
        wot[rows, :] = (wot[rows, :].T.astype(F32) * 0.5).astype(BF16)
    for e in range(E):

        def backward_step(i, carry, e=e):
            backward_start(e, i)
            weight_part(e, i - 1)
            backward_tile(e, i)
            return carry

        backward_start(e, 0)
        if e:
            weight_part(e - 1, n_b - 1)
        backward_tile(e, 0)
        if e:
            finish_expert(e - 1)
        if e == 2:
            back = []
            for k in range(2 * E):
                half, to = k % 2, 2048 + k * 128
                copy = pltpu.make_async_copy(
                    wb_hbm.at[half, :, (k // 2) * 128 : (k // 2 + 1) * 128],
                    sbuf.at[0:D, to : to + 128],
                    sem_f.at[k],
                )
                copy.start()
                back.append(copy)
        turn()
        if e == 0:
            launch_out(0)
        for k in range(3):
            first, last = 1 + k * (n_b - 1) // 3, 1 + (k + 1) * (n_b - 1) // 3
            lax.fori_loop(first, last, backward_step, 0)
            turn()
            if e == 0 and k == 1:
                launch_out(1)
        finish_units(e)
    weight_part(E - 1, n_b - 1)
    finish_expert(E - 1)
    for copy in back:
        copy.wait()
    wb = sbuf.at[0:D, 2048 : 2048 + E * H]
    for k in range(4):
        g2t[k * 128 : (k + 1) * 128, :] = column(stat_ref[1:2, k * 128 : (k + 1) * 128])

    for k in range(4):
        v_mp[mp, 48 + k : 49 + k, :] = s2row[:, k * 128 : (k + 1) * 128]
    v_mp[mp, 52:60, :] = acc_dlog[...]
    v_mp[mp, 60:61, :] = lane_sums(acc_last[...])
    v_mp[mp, 61:63, :] = acc_lb[0:2]
    b1_sums = lane_sums(acc_b1[...])
    v_mp[mp, 63:64, :] = b1_sums[:, 0:128]
    v_mp[mp, 64:65, :] = b1_sums[:, 128:256]
    v_mp[mp, 65:66, :] = lane_sums(acc_b2[...])
    v_mp[mp, 66:VR, :] = jnp.zeros((VR - 66, 128), F32)
    flight["v"] = [send(v_mp.at[mp], v_mp.at[mp], sem_v.at[0], sem_v.at[1], (b, other))]

    def small_level(level, total):
        own = digits[level]
        v_lv[level, own] = total
        flight["v"] = []
        for step in range(1, plan[level][1]):
            base = 2 + (level * 3 + step - 1) * 2
            flight["v"].append(
                send(
                    v_lv.at[level, own], v_lv.at[level, own],
                    sem_v.at[base], sem_v.at[base + 1], peer(level, step),
                )
            )

    def small_steps():
        steps = []

        def first():
            for copy in flight["v"]:
                copy.wait()
            small_level(0, v_mp[0] + v_mp[1])

        steps.append(first)
        for level in range(n_levels):

            def step(level=level):
                for copy in flight["v"]:
                    copy.wait()
                total = v_lv[level, 0]
                for k in range(1, plan[level][1]):
                    total = total + v_lv[level, k]
                if level + 1 < n_levels:
                    small_level(level + 1, total)
                    return
                vout_ref[...] = total
                row = jnp.concatenate([total[k : k + 1] for k in range(2 * E)], axis=1)
                row_high = row.astype(BF16).astype(F32)
                rows = jnp.concatenate(
                    [row_high, row - row_high, jnp.zeros((14, E * H), F32)], axis=0
                ).astype(BF16)
                s1 = nn(rows, wf[0 : E * H, :])
                gate_sum = jnp.sum(total[52:60], axis=1, keepdims=True)
                gate_part = jnp.sum(gate_low * gate_sum, axis=0, keepdims=True)
                stat_ref[3:4, :] = s1[0:1] + s1[1:2] + gate_part
                stat_ref[4:5, :] = jnp.concatenate([total[48 + k : 49 + k] for k in range(4)], axis=1)

            steps.append(step)
        return steps

    start_steps(small_steps(), 2)
    turn()

    def input_gradient(i):
        lanes = pl.ds(i * TB, TB)
        da = zbuf[:, lanes]
        dl = dlogbuf[:, lanes]
        for k, half in ((0, mp), (1, other)):
            at = pl.ds(pl.multiple_of(half * 256, 256), 256)
            grad = nn(wb[at, :], da) + nn(gback[at, 0:16], dl)
            grad = grad * wide(g2t[at, :], TB)
            dobuf[k * H : (k + 1) * H, lanes] = grad.astype(BF16)

    n_c = R // TB
    for part in range(4):
        for k in range(part * n_c // 4, (part + 1) * n_c // 4):
            input_gradient(k)
            turn()
        w = R // 4
        at = pl.ds(part * w, w)
        to = pl.ds(pl.multiple_of(mp * R + part * w, 128), w)
        local = pltpu.make_async_copy(dobuf.at[0:H, at], d_hbm.at[:, to], sem_l.at[1 + NC + part])
        local.start()
        pending.append(local)
        pending.append(
            send(dobuf.at[H : 2 * H, at], d_hbm.at[:, to], sem_d.at[part], sem_d.at[4 + part], (b, other))
        )
    while queue:
        turn()
    for copy in pending:
        copy.wait()


def final_kernel(
    tile, dt_ref, x_ref, v_ref, gain_ref, pred_ref, gout_ref, vout_ref, stat_ref,
    o_pred, o_feat, o_in, o_inb, o_gain, o_nb, o_out, o_outb, o_gate, o_gateb,
    o_w1, o_b1, o_w2, o_b2, o_wl, o_bl,
):
    mp = lax.axis_index("mp")
    half = pl.ds(pl.multiple_of(mp * 256, 256), 256)

    count = stat_ref[2:3, half]
    inv = stat_ref[1:2, half]
    slope = inv * inv * (stat_ref[4:5, half] / count)
    shift = inv * (stat_ref[3:4, half] / count) - stat_ref[0:1, half] * slope
    eye = jnp.where(
        lax.broadcasted_iota(jnp.int32, (256, 256), 0) == lax.broadcasted_iota(jnp.int32, (256, 256), 1), 1.0, 0.0
    ).astype(BF16)
    for at in range(0, tile, 256):
        rows = slice(at, at + 256)
        grad = nt(eye, dt_ref[:, rows])
        valid = nt(eye, jnp.broadcast_to(v_ref[:, rows].astype(F32), (128, 256)).astype(BF16))
        for c in range(2):
            cols = slice(c * 128, (c + 1) * 128)
            term = valid * (shift[:, cols] + x_ref[rows, cols].astype(F32) * slope[:, cols])
            o_feat[rows, cols] = grad[:, cols] - term

    @pl.when(pl.program_id(0) == 0)
    def _():
        scale = 1.0 / stat_ref[2:3, 0:128]
        one = scale[:, 0:1]
        o_pred[...] = pred_ref[...]
        for e in range(E):
            for k in range(4):
                g = gout_ref[e, (k // 2) * 128 : (k // 2 + 1) * 128, (k % 2) * 128 : (k % 2 + 1) * 128]
                o_in[e, k * 128 : (k + 1) * 128, :] = (g.astype(F32) * one).T
            for k in range(2):
                g = gout_ref[TOWERS + 1 + e // 3, k * 128 : (k + 1) * 128, (e % 3) * 128 : (e % 3 + 1) * 128]
                o_out[e, :, k * 128 : (k + 1) * 128] = g.astype(F32) * one
            for ref, base in ((o_inb, 0), (o_gain, 12), (o_nb, 24)):
                sums = vout_ref[pl.ds(base + 2 * e + mp, 1), :] * scale
                ref[e : e + 1, :] = sums / gain_ref[e : e + 1, :] if base else sums
            for k in range(2):
                o_outb[e : e + 1, k * 128 : (k + 1) * 128] = (
                    vout_ref[36 + 2 * e + k : 37 + 2 * e + k, :] * scale
                )
        o_w1[0] = gout_ref[TOWERS, :, 0:128].astype(F32) * one
        o_w1[1] = gout_ref[TOWERS, :, 128:256].astype(F32) * one
        g = gout_ref[TOWERS, 0:160, 256:384].astype(F32) * one
        o_w2[0] = g[0:64]
        o_w2[1] = g[64:128]
        for k in range(4):
            part = g[128 + 8 * k : 136 + 8 * k]
            o_gate[0, :, k * 128 : (k + 1) * 128] = part[0:4]
            o_gate[1, :, k * 128 : (k + 1) * 128] = part[4:8]
        gate_bias = jnp.sum(vout_ref[52:60, :], axis=1, keepdims=True) * scale
        table = jnp.concatenate([gate_bias, jnp.zeros((120, 128), F32)], axis=0).T
        o_gateb[0:1, :] = table[0:1, 0:4]
        o_gateb[1:2, :] = table[0:1, 4:8]
        last = vout_ref[60:61, :] * scale
        o_wl[0:1, :] = last[:, 0:64]
        o_wl[1:2, :] = last[:, 64:128]
        o_bl[...] = jnp.sum(vout_ref[61:63, :], axis=1, keepdims=True) * scale
        o_b1[...] = vout_ref[63:65, :] * scale
        b2 = vout_ref[65:66, :] * scale
        o_b2[0:1, :] = b2[:, 0:64]
        o_b2[1:2, :] = b2[:, 64:128]


def on_device(
    features, validity, labels, expert_in, expert_in_bias, norm_gain, norm_bias, expert_out,
    expert_out_bias, gate_weight, gate_bias, tower_first, tower_first_bias, tower_second,
    tower_second_bias, tower_last, tower_last_bias,
):
    rows = features.shape[0]
    R = rows // 2
    n_batch = lax.axis_size("batch")
    plan = plan_of(n_batch)
    n_levels = len(plan)
    n_peers = sum(radix - 1 for _, radix, _, _ in plan)
    n_sems = 1 + 2 * n_peers
    v_row = validity.reshape(1, rows)
    y_rows = labels.T
    vm = pl.BlockSpec(memory_space=pltpu.VMEM)
    sm = pl.BlockSpec(memory_space=pltpu.SMEM)
    hb = pl.BlockSpec(memory_space=pl.ANY)
    dma = pltpu.SemaphoreType.DMA

    def scr(*shape, dtype=F32):
        return pltpu.VMEM(shape, dtype)

    low_rows = sum(p[2] for p in plan[1:]) + plan[-1][3]
    scratch = [
        scr(R, D, dtype=BF16), scr(E * H, R, dtype=BF16), scr(E * H, R, dtype=BF16),
        scr(E * H, R, dtype=BF16), scr(8, R), scr(16, R, dtype=BF16), scr(2, R),
        scr(E * H + 32, D, dtype=BF16), scr(D, 128, dtype=BF16),
        scr(E * H, H, dtype=BF16), scr(E * H, 128), scr(E * H, 128), scr(E * H, 128),
        scr(2, 128, H, dtype=BF16), scr(2, H, 128, dtype=BF16), scr(128, H, dtype=BF16),
        scr(H, 128, dtype=BF16), scr(H, 128), scr(128, 128), scr(128, 128), scr(8, 128),
        [scr(E * H, TF)] * 2, [scr(E * HE, TF, dtype=BF16)] * 2, [scr(8, TF)] * 2,
        scr(2 * H, TF, dtype=BF16), scr(H, TF, dtype=BF16), scr(2 * H, TF),
        scr(E * HE, H), scr(16, D), scr(2, H, 128), scr(128, H),
        scr(8, 128), scr(8, 128), scr(128, 128), scr(128, 128), scr(H, 128), scr(1, D),
        scr(24, 128), scr(24, 128),
        scr(8, 8, D), scr(n_levels, 4, 8, D), scr(2, VR, 128), scr(n_levels, 4, VR, 128),
        scr(3, H, 384, dtype=BF16), scr(3, low_rows, 384, dtype=BF16),
        [scr(H, w, dtype=BF16) for w in WIDTHS],
        [[scr(radix, after, w, dtype=BF16) for _, radix, _, after in plan] for w in WIDTHS],
        dma((8,)), dma((8,)), dma((14 + 6 * n_levels,)), dma((2 + 6 * n_levels,)),
        dma((NC, n_sems)), dma((NC, n_sems)), dma((5 + NC,)), dma((8,)), dma((3 * E,)),
    ]
    flops = 2 * R * (6 * D * E * H // 2 + 3 * E * H * H)
    d_half, preds, gsum, vsum, stats, _ = pl.pallas_call(
        functools.partial(main_kernel, plan, R),
        out_shape=(
            jax.ShapeDtypeStruct((256, rows), BF16),
            jax.ShapeDtypeStruct((2, rows), F32),
            jax.ShapeDtypeStruct((NC, H, 384), BF16),
            jax.ShapeDtypeStruct((VR, 128), F32),
            jax.ShapeDtypeStruct((8, D), F32),
            jax.ShapeDtypeStruct((2, D, E * 128), BF16),
        ),
        in_specs=[hb] + [vm] * 2 + [hb] * 2 + [vm] * 5 + [sm] + [vm] * 5 + [sm],
        out_specs=(hb, hb, hb, vm, vm, hb),
        scratch_shapes=scratch,
        compiler_params=pltpu.CompilerParams(
            collective_id=0, has_side_effects=True, vmem_limit_bytes=64 * 2**20 - 65536
        ),
        cost_estimate=pl.CostEstimate(flops=flops, bytes_accessed=20 * 2**20, transcendentals=0),
        name="layer",
    )(
        features, v_row, y_rows, expert_in, expert_out, expert_in_bias, norm_gain, norm_bias,
        expert_out_bias, jnp.swapaxes(gate_weight, 1, 2), gate_bias, tower_first, tower_first_bias,
        jnp.swapaxes(tower_second, 1, 2), tower_second_bias, tower_last, tower_last_bias,
    )

    tile = 4096
    whole = lambda *shape: pl.BlockSpec(shape, lambda i: (0,) * len(shape))
    half_index = lambda i: (i, lax.axis_index("mp"))
    out_shapes = [
        (2, rows), (rows, 256), (E, D, 128), (E, 128), (E, 128), (E, 128), (E, 128, H), (E, H),
        (2, 4, D), (2, 4), (2, H, 128), (2, 128), (2, 64, 128), (2, 64), (2, 64), (2, 128),
    ]
    out_specs = [whole(*shape) for shape in out_shapes]
    out_specs[1] = pl.BlockSpec((tile, 256), lambda i: (i, 0))
    outs = pl.pallas_call(
        functools.partial(final_kernel, tile),
        grid=(rows // tile,),
        out_shape=[jax.ShapeDtypeStruct(shape, F32) for shape in out_shapes],
        in_specs=[
            pl.BlockSpec((256, tile), lambda i: (0, i)),
            pl.BlockSpec((tile, 256), half_index),
            pl.BlockSpec((1, tile), lambda i: (0, i)),
            whole(E, 128), whole(2, rows), whole(NC, H, 384), whole(VR, 128), whole(8, D),
        ],
        out_specs=out_specs,
        compiler_params=pltpu.CompilerParams(vmem_limit_bytes=64 * 2**20 - 65536),
        cost_estimate=pl.CostEstimate(
            flops=rows * 256 * 8, bytes_accessed=rows * 256 * 8, transcendentals=0
        ),
        name="finish",
    )(d_half, features, v_row, norm_gain, preds, gsum, vsum, stats)
    outs = list(outs)
    outs[0] = outs[0].T
    outs[8] = jnp.swapaxes(outs[8], 1, 2)
    outs[12] = jnp.swapaxes(outs[12], 1, 2)
    outs[15] = outs[15][:, 0]
    return tuple(outs)


def solution(mesh):
    in_specs = (
        P("batch", None), P("batch"), P("batch", None), P(None, None, "mp"), P(None, "mp"),
        P(None, "mp"), P(None, "mp"), P(None, "mp", None), P(), P(), P(), P(), P(), P(), P(), P(), P(),
    )
    out_specs = (
        P("batch", None), P("batch", "mp"), P(None, None, "mp"), P(None, "mp"), P(None, "mp"),
        P(None, "mp"), P(None, "mp", None), P(), P(), P(), P(), P(), P(), P(), P(), P(),
    )
    return jax.shard_map(
        on_device, mesh=mesh, in_specs=in_specs, out_specs=out_specs, check_vma=False
    )
```

```python
import functools

import jax
import jax.numpy as jnp
from jax import lax
from jax.experimental import pallas as pl
from jax.experimental.pallas import tpu as pltpu
from jax.sharding import PartitionSpec as P

MESH = pl.DeviceIdType.MESH
F32 = jnp.float32
BF16 = jnp.bfloat16
EPS = 1e-05
TASK_EXPERTS = ((0, 1, 4, 5), (2, 3, 4, 5))
E = 6
H = 256
D = 512
TF = 256
TB = 512
SB = 256
CH = 32
VR = 72
HE = H + 16
WIDTHS = (256,) * E + (384,) * 3
NC = len(WIDTHS)
TOWERS = E


def levels_of(count):
    levels, stride = [], 1
    while stride < count:
        radix = 4 if (count // stride) % 4 == 0 else count // stride
        levels.append((stride, radix))
        stride *= radix
    return levels


def plan_of(count):
    plan, rows = [], H
    for stride, radix in levels_of(count):
        split = rows % radix == 0 and (rows // radix) % 16 == 0
        plan.append((stride, radix, rows, rows // radix if split else rows))
        rows = plan[-1][3]
    return plan


def nn(a, b):
    return lax.dot_general(a, b, (((1,), (0,)), ((), ())), preferred_element_type=F32)


def nt(a, b):
    return lax.dot_general(a, b, (((1,), (1,)), ((), ())), preferred_element_type=F32)


def column(row):
    return jnp.broadcast_to(row, (128, 128)).T


def wide(table, width):
    return jnp.concatenate([table] * (width // 128), axis=1)


def fold8(value):
    total = value[0:8]
    for start in range(8, value.shape[0], 8):
        total = total + value[start : start + 8]
    return total


def fold_lanes(value):
    total = value[:, 0:128]
    for start in range(128, value.shape[1], 128):
        total = total + value[:, start : start + 128]
    return total


def lane_sums(partial):
    rows = [
        jnp.sum(partial[at : at + 128].T, axis=0, keepdims=True)
        for at in range(0, partial.shape[0], 128)
    ]
    return jnp.concatenate(rows, axis=1)


def merge_stats(items):
    count = items[0][2:3]
    total = items[0][0:1]
    for item in items[1:]:
        count = count + item[2:3]
        total = total + item[0:1]
    mean = total / jnp.maximum(count, 1.0)
    square = jnp.zeros_like(total)
    for item in items:
        shift = item[0:1] / jnp.maximum(item[2:3], 1.0) - mean
        square = square + item[1:2] + item[2:3] * shift * shift
    return total, square, count


def main_kernel(
    plan, rows_core,
    x_hbm, v_ref, y_ref, win_hbm, wout_hbm, bin_ref, gain_ref, nb_ref, bout_ref, gate_ref, gb_ref,
    w1_ref, b1_ref, w2_ref, b2_ref, wl_ref, bl_ref,
    d_hbm, pred_hbm, gout_hbm, vout_ref, stat_ref, wb_hbm,
    xbuf, zbuf, sbuf, dobuf, rbuf, dlogbuf, predbuf,
    wf, gback, wot, pk, g2t, b2t,
    w1t, w1n, w2f, w2b, b1t, b2tt, wlt, gbt,
    abufs, hbufs, logit_bufs, mixb, u1b, dmix,
    acc_out, acc_gate, acc_first, acc_second,
    acc_dlog, acc_lb, acc_last, acc_b2, acc_b1, s2row,
    bias_snd, bias_rcv,
    st_near, st_lv, v_mp, v_lv, sends, sends_low, mprecv, lvrecv,
    sem_x, sem_w, sem_st, sem_v, sem_s, sem_r, sem_l, sem_d, sem_f,
):
    R = rows_core
    abuf = abufs[0]
    acc_in = (abuf.at[0:H, :], abuf.at[H : 2 * H, :])
    hkeep = (abuf.at[2 * H : 3 * H, :], abuf.at[3 * H : 4 * H, :])
    acc_u = (
        abuf.at[4 * H : 5 * H, 0:128], abuf.at[4 * H : 5 * H, 128:256], abuf.at[5 * H : 6 * H, 0:128]
    )
    n_levels = len(plan)
    b = lax.axis_index("batch")
    mp = lax.axis_index("mp")
    other = 1 - mp
    digits = [lax.rem(lax.div(b, stride), radix) for stride, radix, _, _ in plan]

    def peer(level, step):
        stride, radix = plan[level][:2]
        to = lax.rem(digits[level] + step, radix)
        return (b + (to - digits[level]) * stride, mp)

    def send(src, dst, ssem, rsem, to):
        copy = pltpu.make_async_remote_copy(
            src_ref=src, dst_ref=dst, send_sem=ssem, recv_sem=rsem,
            device_id=to, device_id_type=MESH,
        )
        copy.start()
        return copy

    n_x = 8
    xr = R // n_x
    x_copies = []
    for k in range(n_x):
        copy = pltpu.make_async_copy(
            x_hbm.at[pl.ds(pl.multiple_of(mp * R + k * xr, 16), xr), :],
            xbuf.at[pl.ds(k * xr, xr), :],
            sem_x.at[k],
        )
        copy.start()
        x_copies.append(copy)

    f_copies = []
    for e in range(E):
        for k in range(2):
            f_copies.append(
                pltpu.make_async_copy(
                    win_hbm.at[e, k * H : (k + 1) * H, :],
                    abuf.at[e * H : (e + 1) * H, k * 128 : (k + 1) * 128],
                    sem_f.at[2 * e + k],
                )
            )
        f_copies.append(
            pltpu.make_async_copy(
                wout_hbm.at[e], acc_out.at[e * 128 : (e + 1) * 128, :], sem_f.at[2 * E + e]
            )
        )
    for copy in f_copies:
        copy.start()

    barrier = pltpu.get_barrier_semaphore()
    near = [(step, m) for step in range(plan[0][1]) for m in range(2) if step or m]

    def near_peer(step, m):
        return (peer(0, step)[0], other if m else mp)

    greets = [near_peer(step, m) for step, m in near]
    for level in range(1, n_levels):
        greets += [peer(level, step) for step in range(1, plan[level][1])]
    for to in greets:
        pl.semaphore_signal(barrier, inc=1, device_id=to, device_id_type=MESH)

    v_row = v_ref[:, pl.ds(pl.multiple_of(mp * R, 128), R)].astype(F32)
    count = jnp.sum(v_row, axis=1, keepdims=True)
    total = jnp.zeros((16, D), F32)
    for k in range(n_x):
        x_copies[k].wait()
        v16 = jnp.broadcast_to(v_row[:, k * xr : (k + 1) * xr], (16, xr)).astype(BF16)
        total = total + nn(v16, xbuf[pl.ds(k * xr, xr), :])
    mean = total[0:1] / jnp.maximum(count, 1.0)

    def square_step(k, total):
        for part in range(2):
            r0 = pl.multiple_of(k * 512 + part * 256, 256)
            off = xbuf[pl.ds(r0, 256), :].astype(F32) - mean
            v16 = v_ref[:, pl.ds(pl.multiple_of(mp * R + r0, 128), 256)]
            v16 = jnp.broadcast_to(v16.astype(F32), (16, 256)).astype(BF16)
            total = total + nn(v16, (off * off).astype(BF16))
        return total

    square = lax.fori_loop(0, R // 512, square_step, jnp.zeros((16, D), F32))
    pl.semaphore_wait(barrier, len(greets))
    me = digits[0] * 2 + mp
    st_near[me] = jnp.concatenate(
        [total[0:1], square[0:1], jnp.broadcast_to(count, (1, D)), jnp.zeros((5, D), F32)], axis=0
    )
    st_copies = [
        send(st_near.at[me], st_near.at[me], sem_st.at[2 * k], sem_st.at[2 * k + 1], near_peer(*near[k]))
        for k in range(len(near))
    ]

    win_snd = dobuf.at[0:D, 0 : E * 128]
    win_rcv = dobuf.at[0:D, 1024 : 1024 + E * 128]
    wout_snd = dobuf.at[D : D + 128, 0 : E * H]
    wout_rcv = dobuf.at[D : D + 128, 2048 : 2048 + E * H]
    for copy in f_copies:
        copy.wait()
    for e in range(E):
        for k in range(2):
            win_snd[k * H : (k + 1) * H, e * 128 : (e + 1) * 128] = abuf[
                e * H : (e + 1) * H, k * 128 : (k + 1) * 128
            ].astype(BF16)
        wout_snd[:, e * H : (e + 1) * H] = acc_out[e * 128 : (e + 1) * 128, :].astype(BF16)
    bias_snd[0:E] = bin_ref[...]
    bias_snd[8 : 8 + E] = gain_ref[...]
    bias_snd[16 : 16 + E] = nb_ref[...]
    w_copies = [
        send(win_snd, win_rcv, sem_w.at[0], sem_w.at[1], (b, other)),
        send(wout_snd, wout_rcv, sem_w.at[2], sem_w.at[3], (b, other)),
        send(bias_snd, bias_rcv, sem_w.at[4], sem_w.at[5], (b, other)),
    ]

    for t in range(2):
        w1n[t] = w1_ref[t].astype(BF16)
        w1t[t] = (w1_ref[t].T * 0.5).astype(BF16)
        b1t[t * 128 : (t + 1) * 128] = column(b1_ref[t : t + 1, :]) * 0.5
    zero64 = jnp.zeros((64, 128), F32)
    zero128 = jnp.zeros((128, 64), F32)
    w2f[0:64] = (jnp.concatenate([w2_ref[0], zero64], axis=1) * 0.5).astype(BF16)
    w2f[64:128] = (jnp.concatenate([zero64, w2_ref[1]], axis=1) * 0.5).astype(BF16)
    w2b[0:128] = (jnp.concatenate([w2_ref[0].T, zero128], axis=1) * 0.5).astype(BF16)
    w2b[128:256] = (jnp.concatenate([zero128, w2_ref[1].T], axis=1) * 0.5).astype(BF16)
    b2tt[...] = column(jnp.concatenate([b2_ref[0:1, :], b2_ref[1:2, :]], axis=1)) * 0.5
    wlt[...] = column(jnp.concatenate([wl_ref[0:1, :], wl_ref[1:2, :]], axis=1))
    gbt[...] = jnp.concatenate(
        [jnp.full((1, 128), gb_ref[t, k], F32) for t in range(2) for k in range(4)], axis=0
    )
    gate = jnp.concatenate([gate_ref[0], gate_ref[1]], axis=0)
    gate_low = gate.astype(BF16).astype(F32)
    gback[...] = jnp.concatenate([gate_low, gate_low, jnp.zeros((112, D), F32)], axis=0).T.astype(BF16)
    acc_gate[...] = jnp.zeros_like(acc_gate)
    acc_out[...] = jnp.zeros_like(acc_out)
    for hbuf in hbufs:
        for e in range(E):
            hbuf[e * HE + H : (e + 1) * HE, :] = jnp.ones((16, TF), BF16)
    acc_first[...] = jnp.zeros_like(acc_first)
    acc_second[...] = jnp.zeros_like(acc_second)
    acc_dlog[...] = jnp.zeros_like(acc_dlog)
    acc_lb[...] = jnp.zeros_like(acc_lb)
    acc_last[...] = jnp.zeros_like(acc_last)
    acc_b1[...] = jnp.zeros_like(acc_b1)
    acc_b2[...] = jnp.zeros_like(acc_b2)

    lane = lax.broadcasted_iota(jnp.int32, (128, 128), 1)

    def place(half, win, wout, bias):
        for e in range(E):
            at = pl.multiple_of(e * H + half * 128, 128)
            w = win[:, e * 128 : (e + 1) * 128]
            wf[pl.ds(at, 128), :] = w.T
            o = wout[:, e * H : (e + 1) * H]
            wot[pl.ds(e * H, H), pl.ds(pl.multiple_of(half * 128, 128), 128)] = o.T
            gain = column(bias[8 + e : 9 + e, :])
            pk[pl.ds(at, 128), :] = jnp.where(lane == 0, column(bias[e : e + 1, :]), gain)
            g2t[pl.ds(at, 128), :] = gain * 0.5
            b2t[pl.ds(at, 128), :] = column(bias[16 + e : 17 + e, :]) * 0.5

    place(mp, win_snd, wout_snd, bias_snd)
    for copy in st_copies:
        copy.wait()
    total, square, count = merge_stats([st_near[k] for k in range(2 * plan[0][1])])
    for level in range(1, n_levels):
        own = digits[level]
        st_lv[level, own] = jnp.concatenate([total, square, count, jnp.zeros((5, D), F32)], axis=0)
        copies = []
        for step in range(1, plan[level][1]):
            base = 2 * (len(near) + level * 3 + step - 1)
            copies.append(
                send(
                    st_lv.at[level, own], st_lv.at[level, own],
                    sem_st.at[base], sem_st.at[base + 1], peer(level, step),
                )
            )
        if level == 1:
            for copy in w_copies:
                copy.wait()
            place(other, win_rcv, wout_rcv, bias_rcv)
            keep = [
                pltpu.make_async_copy(win_snd, wb_hbm.at[mp], sem_f.at[0]),
                pltpu.make_async_copy(win_rcv, wb_hbm.at[other], sem_f.at[1]),
            ]
            for copy in keep:
                copy.start()
            means = []
            for e in range(E):
                w = wf[e * H : (e + 1) * H, :].astype(F32)
                means.append(jnp.sum(w, axis=0, keepdims=True) * (1.0 / H))
                shift = jnp.sum(pk[e * H : (e + 1) * H, 0:1], axis=0, keepdims=True) * (1.0 / H)
                for k in range(2):
                    at = slice(e * H + k * 128, e * H + (k + 1) * 128)
                    table = pk[at, :]
                    table = jnp.where(lane == 0, table - shift, table)
                    second = column(bout_ref[e : e + 1, k * 128 : (k + 1) * 128])
                    pk[at, :] = jnp.where(lane == 1, second, table)
            pad = [jnp.zeros((2, D), F32)]
            means = jnp.concatenate(means + pad, axis=0)
            means_high = means.astype(BF16).astype(F32)
            wf[E * H : E * H + 32, :] = jnp.concatenate(
                [gate_low, means_high, means - means_high, jnp.zeros((8, D), F32)], axis=0
            ).astype(BF16)
        for copy in copies:
            copy.wait()
        total, square, count = merge_stats([st_lv[level, k] for k in range(plan[level][1])])
    mu = total / count
    inv = lax.rsqrt(square / count + EPS)
    stat_ref[...] = jnp.concatenate([mu, inv, count, jnp.zeros((5, D), F32)], axis=0)

    def forward(i, side):
        abuf, hbuf = abufs[side], hbufs[side]
        r0 = pl.multiple_of(i * TF, TF)
        x_tile = xbuf[pl.ds(r0, TF), :].astype(F32)
        xn = ((x_tile - stat_ref[0:1, :]) * stat_ref[1:2, :]).astype(BF16)
        xbuf[pl.ds(r0, TF), :] = xn
        ext = nt(wf[E * H : E * H + 32, :], xn)
        logit_bufs[side][...] = ext[0:8] + wide(gbt[...], TF)
        means = ext[8:16] + ext[16:24]

        def product(e):
            abuf[e * H : (e + 1) * H, :] = nt(wf[e * H : (e + 1) * H, :], xn)

        def norm(e):
            squares = jnp.zeros((8, TF), F32)
            for at in range(e * H, (e + 1) * H, CH):
                c = (abuf[at : at + CH, :] - means[e : e + 1]) + pk[at : at + CH, 0:1]
                abuf[at : at + CH, :] = c
                squares = squares + fold8(c * c)
            r = lax.rsqrt(jnp.sum(squares, axis=0, keepdims=True) * (1.0 / H) + EPS)
            rbuf[e : e + 1, pl.ds(r0, TF)] = r
            for u in range(0, H, CH):
                at = e * H + u
                zhat = abuf[at : at + CH, :] * r
                zbuf[at : at + CH, pl.ds(r0, TF)] = zhat.astype(BF16)
                half = zhat * wide(g2t[at : at + CH, :], TF) + wide(b2t[at : at + CH, :], TF)
                p = 1.0 + jnp.tanh(half)
                h = half * p
                hbuf[e * HE + u : e * HE + u + CH, :] = h.astype(BF16)
                slope = (p + h * (2.0 - p)) * pk[at : at + CH, 2:3]
                sbuf[at : at + CH, pl.ds(r0, TF)] = slope.astype(BF16)

        def output(e):
            o = nn(wot[e * H : (e + 1) * H, :], hbuf[e * HE : e * HE + H, :])
            abuf[e * H : (e + 1) * H, :] = o + pk[e * H : (e + 1) * H, 1:2]

        product(0)
        product(1)
        yield
        for e in range(E):
            norm(e)
            if e + 2 < E:
                product(e + 2)
            output(e)
            yield

    def heads(i, side):
        abuf, hbuf = abufs[side], hbufs[side]
        r0 = pl.multiple_of(i * TF, TF)
        v0 = pl.multiple_of(mp * R + i * TF, 128)
        logits = logit_bufs[side][...]
        probs = []
        for t in range(2):
            part = logits[4 * t : 4 * t + 4]
            part = jnp.exp(part - jnp.max(part, axis=0, keepdims=True))
            part = part / jnp.sum(part, axis=0, keepdims=True)
            probs.append([part[k : k + 1] for k in range(4)])
        for at in range(0, H, CH):
            for t in range(2):
                mixed = None
                for k in range(4):
                    e = TASK_EXPERTS[t][k]
                    term = probs[t][k] * abuf[e * H + at : e * H + at + CH, :]
                    mixed = term if mixed is None else mixed + term
                mixb[t * H + at : t * H + at + CH, :] = mixed.astype(BF16)
        pres = [nn(w1t[t], mixb[t * H : (t + 1) * H, :]) for t in range(2)]
        yield
        slopes = []
        for t in range(2):
            half = pres[t] + wide(b1t[t * 128 : (t + 1) * 128, :], TF)
            p = 1.0 + jnp.tanh(half)
            u1 = half * p
            u1b[t * 128 : (t + 1) * 128, :] = u1.astype(BF16)
            slopes.append(p + u1 * (2.0 - p))
        pre = nn(w2f[...], u1b[...])
        yield
        half = pre + wide(b2tt[...], TF)
        p = 1.0 + jnp.tanh(half)
        u2 = half * p
        slope2 = p + u2 * (2.0 - p)
        wl = wide(wlt[...], TF)
        weighted = u2 * wl
        d_logits = []
        valid = v_ref[:, pl.ds(v0, TF)].astype(F32)
        for t in range(2):
            logit = jnp.sum(weighted[t * 64 : (t + 1) * 64], axis=0, keepdims=True) + bl_ref[t]
            pred = 0.5 + 0.5 * jnp.tanh(0.5 * logit)
            predbuf[t : t + 1, pl.ds(r0, TF)] = pred
            label = y_ref[t : t + 1, pl.ds(v0, TF)].astype(F32)
            d_logits.append(valid * (pred - label))
        d_logit = jnp.concatenate(
            [jnp.broadcast_to(d_logits[t], (64, TF)) for t in range(2)], axis=0
        )
        acc_last[...] += fold_lanes(u2 * d_logit)
        acc_lb[0:2] += fold_lanes(jnp.concatenate(d_logits, axis=0))
        d2 = (d_logit * 0.5) * (wl * slope2)
        acc_b2[...] += fold_lanes(d2)
        d2_low = d2.astype(BF16)
        d_u1 = nn(w2b[...], d2_low)
        acc_second[...] += nt(d2_low, u1b[...])
        yield
        for t in range(2):
            d1 = d_u1[t * 128 : (t + 1) * 128] * slopes[t]
            acc_b1[t * 128 : (t + 1) * 128] += fold_lanes(d1)
            d1_low = d1.astype(BF16)
            dmix[t * H : (t + 1) * H, :] = nn(w1n[t], d1_low)
            acc_first[t] += nt(mixb[t * H : (t + 1) * H, :], d1_low)
        yield
        dots = [[jnp.zeros((8, TF), F32) for _ in range(4)] for _ in range(2)]
        for at in range(0, H, CH):
            dm = [dmix[t * H + at : t * H + at + CH, :] for t in range(2)]
            grads = [None] * E
            for t in range(2):
                for k in range(4):
                    e = TASK_EXPERTS[t][k]
                    term = probs[t][k] * dm[t]
                    grads[e] = term if grads[e] is None else grads[e] + term
                    o = abuf[e * H + at : e * H + at + CH, :]
                    dots[t][k] = dots[t][k] + fold8(dm[t] * o)
            for e in range(E):
                dobuf[e * H + at : e * H + at + CH, pl.ds(r0, TF)] = grads[e].astype(BF16)
        rows = []
        for t in range(2):
            sums = [jnp.sum(dots[t][k], axis=0, keepdims=True) for k in range(4)]
            centre = sum(probs[t][k] * sums[k] for k in range(4))
            rows += [probs[t][k] * (sums[k] - centre) for k in range(4)]
        d_gate = jnp.concatenate(rows, axis=0)
        acc_dlog[...] += fold_lanes(d_gate)
        high = d_gate.astype(BF16).astype(F32)
        d_gate = jnp.concatenate([high, d_gate - high], axis=0).astype(BF16)
        dlogbuf[:, pl.ds(r0, TF)] = d_gate
        acc_gate[...] += nn(d_gate, xbuf[pl.ds(r0, TF), :])
        yield
        for e in range(E):
            at = pl.ds(e * HE, HE)
            acc_out[at, :] += nt(hbuf[at, :], dobuf[e * H : (e + 1) * H, pl.ds(r0, TF)])
        yield

    def together(*parts):
        parts = list(parts)
        while parts:
            for part in list(parts):
                if next(part, "end") == "end":
                    parts.remove(part)

    for copy in keep:
        copy.wait()
    n_f = R // TF
    together(forward(0, 0))

    def forward_pair(j, carry):
        together(heads(2 * j, 0), forward(2 * j + 1, 1))
        together(heads(2 * j + 1, 1), forward(2 * j + 2, 0))
        return carry

    lax.fori_loop(0, n_f // 2 - 1, forward_pair, 0)
    together(heads(n_f - 2, 0), forward(n_f - 1, 1))
    together(heads(n_f - 1, 1))

    pending = []
    pred_at = pl.ds(pl.multiple_of(mp * R, 128), R)
    pred_local = pltpu.make_async_copy(predbuf, pred_hbm.at[:, pred_at], sem_l.at[0])
    pred_local.start()
    pending.append(pred_local)
    pending.append(send(predbuf, pred_hbm.at[:, pred_at], sem_w.at[6], sem_w.at[7], (b, other)))

    flight = {}
    n_sems = 1 + 2 * sum(radix - 1 for _, radix, _, _ in plan)

    def source(c, rows, place_at):
        w = WIDTHS[c]
        at = sum(p[2] for p in plan[1:place_at])
        if c < E:
            return sbuf.at[pl.ds(c * H + at, rows), pl.ds(min(place_at, 1) * w, w)]
        if place_at:
            return sends_low.at[c - E, pl.ds(at, rows), :]
        return sends.at[c - E, pl.ds(0, rows), :]

    def level_sems(level):
        return 1 + 2 * sum(radix - 1 for _, radix, _, _ in plan[:level])

    def start_pair(c):
        src = source(c, H, 0)
        flight[c] = [send(src, mprecv[c], sem_s.at[c, 0], sem_r.at[c, 0], (b, other))]

    def start_level(c, level, value):
        stride, radix, rows, after = plan[level]
        out = source(c, rows, level)
        out[...] = value.astype(BF16)
        copies = []
        for step in range(1, radix):
            k = level_sems(level) + step - 1
            part = out
            if after != rows:
                to = lax.rem(digits[level] + step, radix)
                part = out.at[pl.ds(pl.multiple_of(to * after, 16), after), :]
            dst = lvrecv[c][level].at[step]
            copies.append(send(part, dst, sem_s.at[c, k], sem_r.at[c, k], peer(level, step)))
        flight[c] = copies
        if after != rows:
            mine = out[pl.ds(pl.multiple_of(digits[level] * after, 16), after), :]
        else:
            mine = out[...]
        lvrecv[c][level][0] = mine

    def finish_level(c, level):
        stride, radix, rows, after = plan[level]
        for copy in flight[c]:
            copy.wait()
        if after != rows:
            parts = [lvrecv[c][level][step].astype(F32) for step in range(radix)]
            return functools.reduce(lambda p, q: p + q, parts)
        total = None
        for k in range(radix):
            step = lax.rem(k - digits[level] + radix, radix)
            part = lvrecv[c][level][step].astype(F32)
            total = part if total is None else total + part
        return total

    def region(c, level):
        at = 0
        for k in range(level + 1):
            if plan[k][2] != plan[k][3]:
                at = at + digits[k] * plan[k][3]
        rows = plan[level][3] if level >= 0 else H
        if isinstance(at, int):
            return gout_hbm.at[c, pl.ds(at, rows), pl.ds(0, WIDTHS[c])]
        return gout_hbm.at[c, pl.ds(pl.multiple_of(at, 16), rows), pl.ds(0, WIDTHS[c])]

    split = [level for level in range(n_levels) if plan[level][2] != plan[level][3]]

    def start_result(c, value):
        rows = plan[-1][3]
        final = source(c, rows, n_levels)
        final[...] = value.astype(BF16)
        local = pltpu.make_async_copy(final, region(c, n_levels - 1), sem_l.at[1 + c])
        local.start()
        flight[c] = [local]
        if split:
            start_gather(c, split[-1], final)

    def start_gather(c, level, src):
        dst = region(c, level)
        for step in range(1, plan[level][1]):
            k = level_sems(level) + plan[level][1] - 1 + step - 1
            flight[c].append(send(src, dst, sem_s.at[c, k], sem_r.at[c, k], peer(level, step)))

    def chunk_steps(c):
        steps = []

        def from_pair():
            for copy in flight[c]:
                copy.wait()
            if c < E:
                value = hkeep[c % 2][...]
            elif c == TOWERS:
                value = source(c, H, 0)[...].astype(F32)
            else:
                value = half_out(c - TOWERS - 1, mp)
            start_level(c, 0, value + mprecv[c][...].astype(F32))

        steps.append(from_pair)
        for level in range(n_levels):

            def next_level(level=level):
                value = finish_level(c, level)
                if level + 1 < n_levels:
                    start_level(c, level + 1, value)
                else:
                    start_result(c, value)

            steps.append(next_level)
        for place_in in range(len(split) - 1, 0, -1):

            def gather(place_in=place_in):
                for copy in flight[c]:
                    copy.wait()
                flight[c] = []
                start_gather(c, split[place_in - 1], region(c, split[place_in] - 1))

            steps.append(gather)

        def finish():
            for copy in flight[c]:
                copy.wait()
            flight[c] = []

        steps.append(finish)
        return steps

    queue = []
    clock = [0]

    def start_steps(steps, spacing):
        queue.append([clock[0] + spacing, spacing, steps])

    def turn():
        clock[0] += 1
        for item in list(queue):
            if clock[0] >= item[0]:
                item[2].pop(0)()
                item[0] = clock[0] + item[1]
                if not item[2]:
                    queue.remove(item)

    def half_out(group, h):
        parts = []
        for e in range(3 * group, 3 * group + 3):
            a = acc_out[pl.ds(pl.multiple_of(e * HE + h * 128, 16), 128), :]
            parts.append(jnp.concatenate([a[:, 0:128], a[:, 128:256]], axis=0))
        return jnp.concatenate(parts, axis=1)

    def half_in(h):
        at = pl.ds(pl.multiple_of(h * 128, 128), 128)
        return jnp.concatenate([acc_in[0][at, :], acc_in[1][at, :]], axis=0)

    def pack_towers():
        src = source(TOWERS, H, 0)
        src[:, 0:128] = acc_first[0].astype(BF16)
        src[:, 128:256] = acc_first[1].astype(BF16)
        gates = acc_gate[0:8] + acc_gate[8:16]
        rest = [acc_second[0:64, 0:128], acc_second[64:128, 128:256]]
        rest += [gates[:, k * 128 : (k + 1) * 128] for k in range(4)]
        rest.append(jnp.zeros((H - 160, 128), F32))
        src[:, 256:384] = jnp.concatenate(rest, axis=0).astype(BF16)

    def launch(c, spacing=3):
        start_pair(c)
        start_steps(chunk_steps(c), spacing)

    pack_towers()
    launch(TOWERS)

    def launch_out(group):
        source(TOWERS + 1 + group, H, 0)[...] = half_out(group, other).astype(BF16)
        launch(TOWERS + 1 + group)

    s2row[...] = jnp.sum(
        (gate_low * (acc_gate[0:8] + acc_gate[8:16])), axis=0, keepdims=True
    )

    def backward_start(e, i):
        rows = slice(e * H, (e + 1) * H)
        for part in range(TB // SB):
            lanes = pl.ds(pl.multiple_of(i * TB + part * SB, SB), SB)
            dmix[part * H : (part + 1) * H, :] = nn(wot[rows, :], dobuf[rows, lanes])

    def backward_part(e, r0, part):
        at0 = e * H
        lanes = pl.ds(r0, SB)
        work = dmix.at[part * H : (part + 1) * H]
        r = rbuf[e : e + 1, lanes]
        m1 = jnp.zeros((8, SB), F32)
        m2 = jnp.zeros((8, SB), F32)
        for u in range(0, H, CH):
            at = at0 + u
            zhat = zbuf[at : at + CH, lanes].astype(F32)
            dzg = work[u : u + CH, :] * sbuf[at : at + CH, lanes].astype(F32)
            q = dzg * zhat
            acc_u[0][u : u + CH, :] += fold_lanes(dzg)
            acc_u[1][u : u + CH, :] += fold_lanes(q)
            work[u : u + CH, :] = dzg
            m1 = m1 + fold8(dzg)
            m2 = m2 + fold8(q)
        m1 = jnp.sum(m1, axis=0, keepdims=True) * (1.0 / H)
        m2 = jnp.sum(m2, axis=0, keepdims=True) * (1.0 / H)
        for u in range(0, H, CH):
            at = at0 + u
            zhat = zbuf[at : at + CH, lanes].astype(F32)
            da = r * (work[u : u + CH, :] - m1 - zhat * m2)
            acc_u[2][u : u + CH, :] += fold_lanes(da)
            zbuf[at : at + CH, lanes] = da.astype(BF16)

    n_b = R // TB

    def weight_part(e, i):
        r0 = pl.multiple_of(i * TB, TB)
        rows = slice(e * H, (e + 1) * H)
        grad = nn(zbuf[rows, pl.ds(r0, TB)], xbuf[pl.ds(r0, TB), :])
        acc_in[0][...] += grad[:, 0:256]
        acc_in[1][...] += grad[:, 256:512]

    def backward_tile(e, i):
        for part in range(TB // SB):
            backward_part(e, pl.multiple_of(i * TB + part * SB, SB), part)

    def clear_units():
        for part in acc_u:
            part[...] = jnp.zeros((H, 128), F32)

    def clear_weights():
        for part in acc_in:
            part[...] = jnp.zeros((H, 256), F32)

    def finish_units(e):
        for k in range(3):
            sums = lane_sums(acc_u[2 - k][...])
            v_mp[mp, k * 12 + 2 * e : k * 12 + 2 * e + 1, :] = sums[:, 0:128]
            v_mp[mp, k * 12 + 2 * e + 1 : k * 12 + 2 * e + 2, :] = sums[:, 128:256]
        bo = acc_out[e * HE + H : e * HE + H + 1, :]
        v_mp[mp, 36 + 2 * e : 37 + 2 * e, :] = bo[:, 0:128]
        v_mp[mp, 37 + 2 * e : 38 + 2 * e, :] = bo[:, 128:256]
        clear_units()

    def finish_expert(e):
        hkeep[e % 2][...] = half_in(mp)
        source(e, H, 0)[...] = half_in(other).astype(BF16)
        launch(e, 2 if e >= E - 2 else 3)
        cross = jnp.zeros((8, D), F32)
        for u in range(0, H, CH):
            w = wf[e * H + u : e * H + u + CH, :].astype(F32)
            grad = jnp.concatenate([acc_in[0][u : u + CH, :], acc_in[1][u : u + CH, :]], axis=1)
            cross = cross + fold8(w * grad)
        s2row[...] += jnp.sum(cross, axis=0, keepdims=True)
        clear_weights()

    clear_weights()
    clear_units()
    for e in range(E):
        rows = slice(e * H, (e + 1) * H)
        wot[rows, :] = (wot[rows, :].T.astype(F32) * 0.5).astype(BF16)
    for e in range(E):

        def backward_step(i, carry, e=e):
            backward_start(e, i)
            weight_part(e, i - 1)
            backward_tile(e, i)
            return carry

        backward_start(e, 0)
        if e:
            weight_part(e - 1, n_b - 1)
        backward_tile(e, 0)
        if e:
            finish_expert(e - 1)
        if e == 2:
            back = []
            for k in range(2 * E):
                half, to = k % 2, 2048 + k * 128
                copy = pltpu.make_async_copy(
                    wb_hbm.at[half, :, (k // 2) * 128 : (k // 2 + 1) * 128],
                    sbuf.at[0:D, to : to + 128],
                    sem_f.at[k],
                )
                copy.start()
                back.append(copy)
        turn()
        if e == 0:
            launch_out(0)
        for k in range(2):
            first, last = 1 + k * (n_b - 1) // 2, 1 + (k + 1) * (n_b - 1) // 2
            lax.fori_loop(first, last, backward_step, 0)
            turn()
            if e == 0 and k == 1:
                launch_out(1)
        finish_units(e)
    weight_part(E - 1, n_b - 1)
    finish_expert(E - 1)
    for copy in back:
        copy.wait()
    wb = sbuf.at[0:D, 2048 : 2048 + E * H]
    for k in range(4):
        g2t[k * 128 : (k + 1) * 128, :] = column(stat_ref[1:2, k * 128 : (k + 1) * 128])

    for k in range(4):
        v_mp[mp, 48 + k : 49 + k, :] = s2row[:, k * 128 : (k + 1) * 128]
    v_mp[mp, 52:60, :] = acc_dlog[...]
    v_mp[mp, 60:61, :] = lane_sums(acc_last[...])
    v_mp[mp, 61:63, :] = acc_lb[0:2]
    b1_sums = lane_sums(acc_b1[...])
    v_mp[mp, 63:64, :] = b1_sums[:, 0:128]
    v_mp[mp, 64:65, :] = b1_sums[:, 128:256]
    v_mp[mp, 65:66, :] = lane_sums(acc_b2[...])
    v_mp[mp, 66:VR, :] = jnp.zeros((VR - 66, 128), F32)
    flight["v"] = [send(v_mp.at[mp], v_mp.at[mp], sem_v.at[0], sem_v.at[1], (b, other))]

    def small_level(level, total):
        own = digits[level]
        v_lv[level, own] = total
        flight["v"] = []
        for step in range(1, plan[level][1]):
            base = 2 + (level * 3 + step - 1) * 2
            flight["v"].append(
                send(
                    v_lv.at[level, own], v_lv.at[level, own],
                    sem_v.at[base], sem_v.at[base + 1], peer(level, step),
                )
            )

    def small_steps():
        steps = []

        def first():
            for copy in flight["v"]:
                copy.wait()
            small_level(0, v_mp[0] + v_mp[1])

        steps.append(first)
        for level in range(n_levels):

            def step(level=level):
                for copy in flight["v"]:
                    copy.wait()
                total = v_lv[level, 0]
                for k in range(1, plan[level][1]):
                    total = total + v_lv[level, k]
                if level + 1 < n_levels:
                    small_level(level + 1, total)
                    return
                vout_ref[...] = total
                row = jnp.concatenate([total[k : k + 1] for k in range(2 * E)], axis=1)
                row_high = row.astype(BF16).astype(F32)
                rows = jnp.concatenate(
                    [row_high, row - row_high, jnp.zeros((14, E * H), F32)], axis=0
                ).astype(BF16)
                s1 = nn(rows, wf[0 : E * H, :])
                gate_sum = jnp.sum(total[52:60], axis=1, keepdims=True)
                gate_part = jnp.sum(gate_low * gate_sum, axis=0, keepdims=True)
                stat_ref[3:4, :] = s1[0:1] + s1[1:2] + gate_part
                stat_ref[4:5, :] = jnp.concatenate([total[48 + k : 49 + k] for k in range(4)], axis=1)

            steps.append(step)
        return steps

    start_steps(small_steps(), 2)
    turn()

    def input_gradient(i):
        lanes = pl.ds(i * TB, TB)
        da = zbuf[:, lanes]
        dl = dlogbuf[:, lanes]
        for k, half in ((0, mp), (1, other)):
            at = pl.ds(pl.multiple_of(half * 256, 256), 256)
            grad = nn(wb[at, :], da) + nn(gback[at, 0:16], dl)
            grad = grad * wide(g2t[at, :], TB)
            dobuf[k * H : (k + 1) * H, lanes] = grad.astype(BF16)

    n_c = R // TB
    for part in range(4):
        for k in range(part * n_c // 4, (part + 1) * n_c // 4):
            input_gradient(k)
            turn()
        w = R // 4
        at = pl.ds(part * w, w)
        to = pl.ds(pl.multiple_of(mp * R + part * w, 128), w)
        local = pltpu.make_async_copy(dobuf.at[0:H, at], d_hbm.at[:, to], sem_l.at[1 + NC + part])
        local.start()
        pending.append(local)
        pending.append(
            send(dobuf.at[H : 2 * H, at], d_hbm.at[:, to], sem_d.at[part], sem_d.at[4 + part], (b, other))
        )
    while queue:
        turn()
    for copy in pending:
        copy.wait()


def final_kernel(
    tile, dt_ref, x_ref, v_ref, gain_ref, pred_ref, gout_ref, vout_ref, stat_ref,
    o_pred, o_feat, o_in, o_inb, o_gain, o_nb, o_out, o_outb, o_gate, o_gateb,
    o_w1, o_b1, o_w2, o_b2, o_wl, o_bl,
):
    mp = lax.axis_index("mp")
    half = pl.ds(pl.multiple_of(mp * 256, 256), 256)

    count = stat_ref[2:3, half]
    inv = stat_ref[1:2, half]
    slope = inv * inv * (stat_ref[4:5, half] / count)
    shift = inv * (stat_ref[3:4, half] / count) - stat_ref[0:1, half] * slope
    eye = jnp.where(
        lax.broadcasted_iota(jnp.int32, (256, 256), 0) == lax.broadcasted_iota(jnp.int32, (256, 256), 1), 1.0, 0.0
    ).astype(BF16)

    def block(i, carry):
        for part in range(2):
            rows = pl.ds(pl.multiple_of(i * 512 + part * 256, 256), 256)
            grad = nt(eye, dt_ref[:, rows])
            valid = nt(eye, jnp.broadcast_to(v_ref[:, rows].astype(F32), (128, 256)).astype(BF16))
            for c in range(2):
                cols = slice(c * 128, (c + 1) * 128)
                term = valid * (shift[:, cols] + x_ref[rows, cols].astype(F32) * slope[:, cols])
                o_feat[rows, cols] = grad[:, cols] - term
        return carry

    lax.fori_loop(0, tile // 512, block, 0)

    @pl.when(pl.program_id(0) == 0)
    def _():
        scale = 1.0 / stat_ref[2:3, 0:128]
        one = scale[:, 0:1]
        o_pred[...] = pred_ref[...]
        for e in range(E):
            for k in range(4):
                g = gout_ref[e, (k // 2) * 128 : (k // 2 + 1) * 128, (k % 2) * 128 : (k % 2 + 1) * 128]
                o_in[e, k * 128 : (k + 1) * 128, :] = (g.astype(F32) * one).T
            for k in range(2):
                g = gout_ref[TOWERS + 1 + e // 3, k * 128 : (k + 1) * 128, (e % 3) * 128 : (e % 3 + 1) * 128]
                o_out[e, :, k * 128 : (k + 1) * 128] = g.astype(F32) * one
            for ref, base in ((o_inb, 0), (o_gain, 12), (o_nb, 24)):
                sums = vout_ref[pl.ds(base + 2 * e + mp, 1), :] * scale
                ref[e : e + 1, :] = sums / gain_ref[e : e + 1, :] if base else sums
            for k in range(2):
                o_outb[e : e + 1, k * 128 : (k + 1) * 128] = (
                    vout_ref[36 + 2 * e + k : 37 + 2 * e + k, :] * scale
                )
        o_w1[0] = gout_ref[TOWERS, :, 0:128].astype(F32) * one
        o_w1[1] = gout_ref[TOWERS, :, 128:256].astype(F32) * one
        g = gout_ref[TOWERS, 0:160, 256:384].astype(F32) * one
        o_w2[0] = g[0:64]
        o_w2[1] = g[64:128]
        for k in range(4):
            part = g[128 + 8 * k : 136 + 8 * k]
            o_gate[0, :, k * 128 : (k + 1) * 128] = part[0:4]
            o_gate[1, :, k * 128 : (k + 1) * 128] = part[4:8]
        gate_bias = jnp.sum(vout_ref[52:60, :], axis=1, keepdims=True) * scale
        table = jnp.concatenate([gate_bias, jnp.zeros((120, 128), F32)], axis=0).T
        o_gateb[0:1, :] = table[0:1, 0:4]
        o_gateb[1:2, :] = table[0:1, 4:8]
        last = vout_ref[60:61, :] * scale
        o_wl[0:1, :] = last[:, 0:64]
        o_wl[1:2, :] = last[:, 64:128]
        table = jnp.sum(vout_ref[61:63, :], axis=1, keepdims=True) * scale
        o_bl[...] = jnp.concatenate([table, jnp.zeros((126, 128), F32)], axis=0).T[0:1, 0:2]
        o_b1[...] = vout_ref[63:65, :] * scale
        b2 = vout_ref[65:66, :] * scale
        o_b2[0:1, :] = b2[:, 0:64]
        o_b2[1:2, :] = b2[:, 64:128]


def on_device(
    features, validity, labels, expert_in, expert_in_bias, norm_gain, norm_bias, expert_out,
    expert_out_bias, gate_weight, gate_bias, tower_first, tower_first_bias, tower_second,
    tower_second_bias, tower_last, tower_last_bias,
):
    rows = features.shape[0]
    R = rows // 2
    n_batch = lax.axis_size("batch")
    plan = plan_of(n_batch)
    n_levels = len(plan)
    n_peers = sum(radix - 1 for _, radix, _, _ in plan)
    n_sems = 1 + 2 * n_peers
    v_row = validity.reshape(1, rows)
    y_rows = labels.T
    vm = pl.BlockSpec(memory_space=pltpu.VMEM)
    sm = pl.BlockSpec(memory_space=pltpu.SMEM)
    hb = pl.BlockSpec(memory_space=pl.ANY)
    dma = pltpu.SemaphoreType.DMA

    def scr(*shape, dtype=F32):
        return pltpu.VMEM(shape, dtype)

    low_rows = sum(p[2] for p in plan[1:]) + plan[-1][3]
    scratch = [
        scr(R, D, dtype=BF16), scr(E * H, R, dtype=BF16), scr(E * H, R, dtype=BF16),
        scr(E * H, R, dtype=BF16), scr(8, R), scr(16, R, dtype=BF16), scr(2, R),
        scr(E * H + 32, D, dtype=BF16), scr(D, 128, dtype=BF16),
        scr(E * H, H, dtype=BF16), scr(E * H, 128), scr(E * H, 128), scr(E * H, 128),
        scr(2, 128, H, dtype=BF16), scr(2, H, 128, dtype=BF16), scr(128, H, dtype=BF16),
        scr(H, 128, dtype=BF16), scr(H, 128), scr(128, 128), scr(128, 128), scr(8, 128),
        [scr(E * H, TF)] * 2, [scr(E * HE, TF, dtype=BF16)] * 2, [scr(8, TF)] * 2,
        scr(2 * H, TF, dtype=BF16), scr(H, TF, dtype=BF16), scr(2 * H, TF),
        scr(E * HE, H), scr(16, D), scr(2, H, 128), scr(128, H),
        scr(8, 128), scr(8, 128), scr(128, 128), scr(128, 128), scr(H, 128), scr(1, D),
        scr(24, 128), scr(24, 128),
        scr(8, 8, D), scr(n_levels, 4, 8, D), scr(2, VR, 128), scr(n_levels, 4, VR, 128),
        scr(3, H, 384, dtype=BF16), scr(3, low_rows, 384, dtype=BF16),
        [scr(H, w, dtype=BF16) for w in WIDTHS],
        [[scr(radix, after, w, dtype=BF16) for _, radix, _, after in plan] for w in WIDTHS],
        dma((8,)), dma((8,)), dma((14 + 6 * n_levels,)), dma((2 + 6 * n_levels,)),
        dma((NC, n_sems)), dma((NC, n_sems)), dma((5 + NC,)), dma((8,)), dma((3 * E,)),
    ]
    flops = 2 * R * (6 * D * E * H // 2 + 3 * E * H * H)
    d_half, preds, gsum, vsum, stats, _ = pl.pallas_call(
        functools.partial(main_kernel, plan, R),
        out_shape=(
            jax.ShapeDtypeStruct((256, rows), BF16),
            jax.ShapeDtypeStruct((2, rows), F32),
            jax.ShapeDtypeStruct((NC, H, 384), BF16),
            jax.ShapeDtypeStruct((VR, 128), F32),
            jax.ShapeDtypeStruct((8, D), F32),
            jax.ShapeDtypeStruct((2, D, E * 128), BF16),
        ),
        in_specs=[hb] + [vm] * 2 + [hb] * 2 + [vm] * 5 + [sm] + [vm] * 5 + [sm],
        out_specs=(hb, hb, hb, vm, vm, hb),
        scratch_shapes=scratch,
        compiler_params=pltpu.CompilerParams(
            collective_id=0, has_side_effects=True, vmem_limit_bytes=64 * 2**20 - 65536
        ),
        cost_estimate=pl.CostEstimate(flops=flops, bytes_accessed=20 * 2**20, transcendentals=0),
        name="layer",
    )(
        features, v_row, y_rows, expert_in, expert_out, expert_in_bias, norm_gain, norm_bias,
        expert_out_bias, jnp.swapaxes(gate_weight, 1, 2), gate_bias, tower_first, tower_first_bias,
        jnp.swapaxes(tower_second, 1, 2), tower_second_bias, tower_last, tower_last_bias,
    )

    tile = 4096
    whole = lambda *shape: pl.BlockSpec(shape, lambda i: (0,) * len(shape))
    half_index = lambda i: (i, lax.axis_index("mp"))
    out_shapes = [
        (2, rows), (rows, 256), (E, D, 128), (E, 128), (E, 128), (E, 128), (E, 128, H), (E, H),
        (2, 4, D), (2, 4), (2, H, 128), (2, 128), (2, 64, 128), (2, 64), (2, 64), (1, 2),
    ]
    out_specs = [whole(*shape) for shape in out_shapes]
    out_specs[1] = pl.BlockSpec((tile, 256), lambda i: (i, 0))
    outs = pl.pallas_call(
        functools.partial(final_kernel, tile),
        grid=(rows // tile,),
        out_shape=[jax.ShapeDtypeStruct(shape, F32) for shape in out_shapes],
        in_specs=[
            pl.BlockSpec((256, tile), lambda i: (0, i)),
            pl.BlockSpec((tile, 256), half_index),
            pl.BlockSpec((1, tile), lambda i: (0, i)),
            whole(E, 128), whole(2, rows), whole(NC, H, 384), whole(VR, 128), whole(8, D),
        ],
        out_specs=out_specs,
        compiler_params=pltpu.CompilerParams(vmem_limit_bytes=64 * 2**20 - 65536),
        cost_estimate=pl.CostEstimate(
            flops=rows * 256 * 8, bytes_accessed=rows * 256 * 8, transcendentals=0
        ),
        name="finish",
    )(d_half, features, v_row, norm_gain, preds, gsum, vsum, stats)
    outs = list(outs)
    outs[0] = outs[0].T
    outs[8] = jnp.swapaxes(outs[8], 1, 2)
    outs[12] = jnp.swapaxes(outs[12], 1, 2)
    outs[15] = outs[15].reshape(2)
    return tuple(outs)


def solution(mesh):
    in_specs = (
        P("batch", None), P("batch"), P("batch", None), P(None, None, "mp"), P(None, "mp"),
        P(None, "mp"), P(None, "mp"), P(None, "mp", None), P(), P(), P(), P(), P(), P(), P(), P(), P(),
    )
    out_specs = (
        P("batch", None), P("batch", "mp"), P(None, None, "mp"), P(None, "mp"), P(None, "mp"),
        P(None, "mp"), P(None, "mp", None), P(), P(), P(), P(), P(), P(), P(), P(), P(),
    )
    return jax.shard_map(
        on_device, mesh=mesh, in_specs=in_specs, out_specs=out_specs, check_vma=False
    )
```
